512 devices in a mesh: tm: 64 (over z_lo, y, core), lon: 8 (over x, z_hi).
Axes of the slice: x: 4, y: 4, z: 16 (z_hi: 2, z_lo: 8; z = z_hi * 8 + z_lo), core: 2. Of those that a mesh axis runs over, the one named last changes fastest.
Arguments:
- first_guess: float32 [64, 2880, 128], P('tm', 'lon'), may hold values from -13 to 13
- observed: float32 [64, 2880, 128], P('tm', 'lon'), may hold values from -6 to 6
- track_mask: int32 [64, 2880, 128], P('tm', 'lon'), may hold values 0 or 1
- land_mask: int32 [2880, 128], P('lon'), may hold values 0 or 1
- bending_weight: float32 [2880, 128], P('lon'), may hold values from 0.005 to 0.05
Outputs:
- analysis: float32 [64, 2880, 128], P('tm', 'lon')
- final_gradient: float32 [64, 2880, 128], P('tm', 'lon')
The draws below stay inside these ranges and needn't reach their ends.
All inputs are finite; a program needn't handle non-finite values. No bound on the sum of `track_mask` or of `land_mask` on one device may be relied on, other than what follows from the above.
Results may differ from the reference program's by a relative error of at most 0.0003.
Values sent between devices are 32-bit elements; how exact they have to be, the bound alone decides.
A program may use at most 64 MiB of HBM per device.

```python
import math
import jax
import jax.numpy as jnp
from jax import lax

LAT = 128
CAP = 64
MW = 64
ITERS = 2
DAYS = 64
NLON = 2880


def draw_first_guess(key, part):
    key = jax.random.fold_in(key, 7)
    key_noise, key_day = jax.random.split(key)
    day_index = jnp.arange(DAYS, dtype=jnp.float32)
    growth = 1.0 + 2.0 * day_index / (DAYS - 1)
    jitter = jnp.exp(jax.random.uniform(key_day, (DAYS,), jnp.float32, jnp.log(0.7), jnp.log(1.4)))
    noise = jax.random.truncated_normal(key_noise, -3.0, 3.0, (DAYS, NLON, LAT), jnp.float32)
    return (noise * (growth * jitter)[:, None, None]).astype(jnp.float32)


def set_ends(entries, stream_key, low, top_value):
    place = [jax.random.randint(jax.random.fold_in(stream_key, axis), (), 0, length) for axis, length in enumerate(entries.shape)]
    main_axis = entries.shape.index(max(entries.shape))
    next_to = place[:main_axis] + [(place[main_axis] + 1) % entries.shape[main_axis]] + place[main_axis + 1:]
    return entries.at[tuple(place)].set(low).at[tuple(next_to)].set(top_value)


def shard_levels(key, shape, shards, low, high):
    def one(position, parts):
        heights = jax.random.uniform(jax.random.fold_in(jax.random.fold_in(key, 6), position), (parts,), jnp.float32, low / len(shards), high / len(shards))
        return jnp.repeat(jnp.exp(heights), shape[position] // parts).reshape((-1,) + (1,) * (len(shape) - position - 1))

    gain = one(*shards[0])
    for cut in shards[1:]:
        gain = gain * one(*cut)
    return gain


def centred(rng, dims, spread, bound, cuts=(), kind=jnp.bfloat16):
    result = jax.random.normal(rng, dims, jnp.float32) * spread
    if len(cuts) > 0:
        result = shard_levels(rng, dims, cuts, -0.22, 0.18) * result
    return jnp.clip(result, min=-bound, max=bound).astype(kind)


def setup_inputs(seed: int = 0) -> dict:
    keys = jax.random.split(jax.random.key(seed), 6)
    first_guess = draw_first_guess(jax.random.fold_in(keys[5], 71), 0)
    observed = centred(keys[1], (DAYS, NLON, LAT), 1.0, 6.0, ((0, 64), (1, 8)), jnp.float32)
    track_mask = set_ends((jax.random.randint(keys[2], (DAYS, NLON, LAT), 0, 4) < 1).astype(jnp.int32), jax.random.fold_in(keys[2], 1), 0, 1)
    land_mask = set_ends((jax.random.randint(keys[3], (NLON, LAT), 0, 3) < 1).astype(jnp.int32), jax.random.fold_in(keys[3], 1), 0, 1)
    bending_weight = jnp.clip(jnp.exp(math.log(0.05) - 2.3025851 * jax.random.uniform(keys[4], (NLON, LAT), jnp.float32) ** shard_levels(keys[4], (NLON, LAT), ((0, 8),), -0.2, 0.2)), 0.005, 0.05)
    return {"first_guess": first_guess, "observed": observed, "track_mask": track_mask, "land_mask": land_mask, "bending_weight": bending_weight}


time_coupling = 1.0


def bending_table(row_count):
    positions = jnp.arange(row_count, dtype=jnp.float32)
    latitude = (90.0 - (row_count - positions - 0.5) * 0.125) * (math.pi / 180.0)
    return 1.0 / (jnp.cos(latitude) + 0.5) ** 2


def laplace(surface, bending_row):
    timed = jnp.pad(surface, ((1, 1), (0, 0), (0, 0)))
    across = jnp.pad(surface, ((0, 0), (0, 0), (1, 1)))
    centre = 2.0 * surface
    zonal = jnp.roll(surface, 1, 1) + jnp.roll(surface, -1, 1) - centre
    return time_coupling * (timed[2:] + timed[:-2] - centre) + bending_row * zonal + (across[:, :, 2:] + across[:, :, :-2] - centre)


def mode_table(leading, span_rows, circle):
    positions = leading + jnp.arange(span_rows, dtype=jnp.int32)
    harmonic = jnp.arange(MW, dtype=jnp.int32)
    angles = ((positions[:, None] * harmonic[None, :]) % circle).astype(jnp.float32) * (2.0 * math.pi / circle)
    return jnp.concatenate([jnp.cos(angles), jnp.sin(angles)], axis=1)


def mode_weights(circle):
    harmonic = jnp.arange(MW, dtype=jnp.int32)
    single = jnp.where(harmonic == 0, 1.0 / circle, 2.0 / circle).astype(jnp.float32)
    return jnp.concatenate([single, single])


def cap_shrink():
    cap_rows = jnp.arange(CAP, dtype=jnp.float32)
    return 0.9 * (cap_rows + 1.0) / CAP


def polar_filter(gradient_now):
    cap_panel = gradient_now[:, :, LAT - CAP:]
    mode_rows = mode_table(0, NLON, NLON)
    amplitudes = jnp.einsum('dic,ik->dck', cap_panel, mode_rows, precision=lax.Precision.HIGHEST)
    smoothed = jnp.einsum('dck,ik->dic', amplitudes * mode_weights(NLON), mode_rows, precision=lax.Precision.HIGHEST)
    filtered = cap_panel - cap_shrink() * (cap_panel - smoothed)
    return jnp.concatenate([gradient_now[:, :, :LAT - CAP], filtered], axis=2)


def reference(first_guess, observed, track_mask, land_mask, bending_weight):
    bending_row = bending_table(LAT)
    weight = track_mask.astype(jnp.float32) * (1.0 - land_mask.astype(jnp.float32))[None]
    smooth = bending_weight[None]

    def hessian(surface):
        return weight * surface + laplace(smooth * laplace(surface, bending_row), bending_row)

    def gradient_at(surface):
        return weight * (surface - observed) + laplace(smooth * laplace(surface, bending_row), bending_row)

    analysis = first_guess
    gradient_now = gradient_at(analysis)
    for iteration in range(ITERS):
        search = polar_filter(gradient_now)
        curved = hessian(search)
        stepsize = jnp.sum(gradient_now * search) / jnp.sum(search * curved)
        analysis = analysis - stepsize * search
        gradient_now = gradient_at(analysis)
    return analysis, gradient_now
```

```python
import functools

import jax
import jax.numpy as jnp
import numpy as np
from jax import lax
from jax.experimental import pallas as pl
from jax.experimental.pallas import tpu as pltpu
from jax.sharding import PartitionSpec as P

CAP = 64
MW = 64
MESH = pl.DeviceIdType.MESH
OFF = 16
EXT = 8
F32 = jnp.float32


def tables(segments, length, rows):
    circle = segments * length
    harmonic = np.arange(MW)
    w = np.where(harmonic == 0, 1.0 / circle, 2.0 / circle)
    padded = -(-length // 128) * 128
    forward = np.zeros((segments, 2 * MW, padded), np.float32)
    inverse = np.zeros((segments, length + 16, 2 * MW), np.float32)
    for s in range(segments):
        a = 2 * np.pi * ((np.arange(length) + s * length)[:, None] * harmonic % circle) / circle
        forward[s, :MW, :length] = np.cos(a).T
        forward[s, MW:, :length] = np.sin(a).T
        a = 2 * np.pi * ((np.arange(length + 16) - 8 + s * length)[:, None] * harmonic % circle) / circle
        inverse[s] = np.concatenate([w * np.cos(a), w * np.sin(a)], axis=1)
    phi = (90.0 - (rows - np.arange(rows) - 0.5) * 0.125) * (np.pi / 180.0)
    bend = 1.0 / (np.cos(phi) + 0.5) ** 2
    shrink = np.zeros(rows)
    shrink[rows - CAP:] = 0.9 * (np.arange(CAP) + 1.0) / CAP
    row = np.zeros((8, rows), np.float32)
    row[0] = bend
    row[1] = -2.0 * (bend + 1.0)
    row[2] = shrink
    row[3] = 1.0 - shrink
    return forward, inverse, row


def kernel(
    NT, N, first_ref, obs_ref, track_ref, land_ref, bw_ref, fwd_ref, inv_ref, row_ref,
    out_a, out_g,
    E, G, U, B, W, obs, track, land, fwd, inv, V, TV, T2V, Y, V0, padded, amp, rs_buf, quarter,
    z_buf, AT, dots, res_a, res_g,
    lsem, hs, hr, bs, br, xs, xr, zs, zr, ats, atr, ds_, dr,
):
    tm = lax.axis_index("tm")
    lon = lax.axis_index("lon")
    x, zh = lon // 2, lon % 2
    zl, k = tm // 8, tm % 8
    rows = 128

    def inside(t):
        return (t >= 0) & (t < NT)

    def when_t(dt, fn):
        if dt == 0:
            fn()
        else:
            pl.when(inside(tm + dt))(fn)

    def lon_at(d):
        return lax.rem(lon + d + 8, 8)

    own = pl.ds(OFF, N)
    loads = [
        pltpu.make_async_copy(first_ref.at[0], E.at[2, own], lsem.at[0]),
        pltpu.make_async_copy(bw_ref, B.at[own], lsem.at[1]),
        pltpu.make_async_copy(obs_ref.at[0], obs, lsem.at[2]),
        pltpu.make_async_copy(track_ref.at[0], track, lsem.at[3]),
        pltpu.make_async_copy(land_ref, land, lsem.at[4]),
        pltpu.make_async_copy(fwd_ref.at[lon], fwd, lsem.at[5]),
        pltpu.make_async_copy(inv_ref.at[lon], inv, lsem.at[6]),
    ]
    for c in loads:
        c.start()

    barrier = pltpu.get_barrier_semaphore()

    def greet(t, l):
        pl.semaphore_signal(barrier, inc=1, device_id={"tm": t, "lon": l}, device_id_type=MESH)

    count = jnp.int32(0)
    for dt in (-2, -1, 0, 1, 2):
        steps = [d for d in range(4) if (dt, d) != (0, 0)]
        dls = [2 * d for d in steps] + ([-1, 1] if abs(dt) < 2 else [])

        def signals(dt=dt, dls=dls):
            for dl in dls:
                greet(tm + dt, lon_at(dl))

        when_t(dt, signals)
        count = count + jnp.where(inside(tm + dt), len(dls), 0)
    for d in range(1, 8):
        greet(zl * 8 + lax.rem(k + d, 8), lon)
    z = zh * 8 + zl
    for d in range(1, 16):
        zz = lax.rem(z + d, 16)
        greet(lax.rem(zz, 8) * 8 + k, x * 2 + zz // 8)
    count = count + 7 + 15

    for dt in (-2, -1, 1, 2):

        @pl.when(jnp.logical_not(inside(tm + dt)))
        def _(dt=dt):
            for X in (E, G, U):
                X[2 + dt] = jnp.zeros(X.shape[1:], F32)
            for p in range(2):
                AT[p, 2 + dt] = jnp.zeros(AT.shape[2:], F32)

    padded[pl.ds(N, padded.shape[0] - N)] = jnp.zeros((padded.shape[0] - N, rows), F32)

    pl.semaphore_wait(barrier, count)

    def remote(src, dst, send, recv, t, l):
        return pltpu.make_async_remote_copy(
            src_ref=src, dst_ref=dst, send_sem=send, recv_sem=recv,
            device_id={"tm": t, "lon": l}, device_id_type=MESH,
        )

    head, tail = pl.ds(OFF, 8), pl.ds(OFF + N - 8, 8)
    left, right = pl.ds(OFF - 8, 8), pl.ds(OFF + N, 8)
    halo_kinds = [(dt, 0) for dt in (1, -1, 2, -2)] + [(dt, dl) for dt in (0, 1, -1) for dl in (1, -1)]

    def halo_copy(p, X, i, sending):
        dt, dl = halo_kinds[i]
        src, dst = (own, own) if dl == 0 else ((tail, left) if dl == 1 else (head, right))
        return remote(X.at[2, src], X.at[2 - dt, dst], hs.at[p, i], hr.at[p, i], tm + dt, lon_at(dl))

    order = [4, 5, 6, 7, 8, 9, 0, 1, 2, 3]

    def halo_send(p, X):
        for i in order:
            when_t(halo_kinds[i][0], lambda i=i: halo_copy(p, X, i, True).start())

    def halo_wait(p, X):
        for i in order:
            when_t(-halo_kinds[i][0], lambda i=i: halo_copy(p, X, i, False).wait_recv())

    def halo_done(p, X):
        for i in order:
            when_t(halo_kinds[i][0], lambda i=i: halo_copy(p, X, i, True).wait_send())

    edge_b = [
        remote(B.at[tail], B.at[left], bs.at[0], br.at[0], tm, lon_at(1)),
        remote(B.at[head], B.at[right], bs.at[1], br.at[1], tm, lon_at(-1)),
    ]

    loads[0].wait()
    halo_send(0, E)
    loads[1].wait()
    for c in edge_b:
        c.start()

    lane = lax.broadcasted_iota(jnp.int32, (8, rows), 1)
    first_lane, last_lane = lane[:1] == 0, lane[:1] == rows - 1
    bend = row_ref[0:1]
    centre = row_ref[1:2]
    shrink = row_ref[2:3]
    keep = row_ref[3:4]

    def flat(ref, start, n):
        v = ref[pl.ds(start, n)]
        up, down = ref[pl.ds(start + 1, n)], ref[pl.ds(start - 1, n)]
        lo = jnp.where(first_lane, 0.0, pltpu.roll(v, 1, axis=1))
        hi = jnp.where(last_lane, 0.0, pltpu.roll(v, rows - 1, axis=1))
        return bend * (up + down) + (lo + hi) + centre * v

    ext_chunks = [(EXT, 96), (EXT + 96, 96), (EXT + 192, 96), (EXT + 288, N + 16 - 288)]
    own_chunks = [(OFF + c, 72) for c in range(0, N, 72)]
    centre_t2 = jnp.where((tm == 0) | (tm == NT - 1), 5.0, 6.0).astype(F32)

    def second(a, b, c):
        return a + b - 2.0 * c

    def second2(a, b, c, d, e):
        return a + e - 4.0 * (b + d) + centre_t2 * c

    def operator(field, emit):
        for s, n in ext_chunks:
            Y[pl.ds(s, n)] = B[pl.ds(s, n)] * (TV[pl.ds(s, n)] + flat(field, s, n))
        for s, n in own_chunks:
            emit(s, n, B[pl.ds(s, n)] * (T2V[pl.ds(s, n)] + flat(TV, s, n)) + flat(Y, s, n))

    for c in loads[2:5]:
        c.wait()
    W[...] = track[...].astype(F32) * (1.0 - land[...].astype(F32))

    halo_wait(0, E)
    for c in edge_b:
        c.wait_recv()
    for s, n in ext_chunks:
        r = pl.ds(s, n)
        TV[r] = second(E[1, r], E[3, r], E[2, r])
    for s, n in own_chunks:
        r = pl.ds(s, n)
        T2V[r] = second2(E[0, r], E[1, r], E[2, r], E[3, r], E[4, r])

    def emit_g(s, n, u):
        l = pl.ds(s - OFF, n)
        g = W[l] * (E[2, pl.ds(s, n)] - obs[l]) + u
        G[2, pl.ds(s, n)] = g
        padded[l] = g

    operator(E.at[2], emit_g)
    for c in loads[5:]:
        c.wait()

    half = lax.broadcasted_iota(jnp.int32, (MW, rows), 1) < MW

    def rs_copy(p, d):
        q = lax.rem(x + d, 4)
        return remote(
            amp.at[p, pl.ds(16 * q, 16)], rs_buf.at[p, d], xs.at[p, d], xr.at[p, d], tm, q * 2 + zh
        )

    def z_copy(p):
        return remote(quarter.at[p, 0], z_buf.at[p], zs.at[p], zr.at[p], tm, lon + 1 - 2 * zh)

    at_kinds = [(dt, d) for dt in (0, 1, -1, 2, -2) for d in range(4) if (dt, d) != (0, 0)]

    def at_copy(p, i):
        dt, d = at_kinds[i]
        xx = lax.rem(x + d, 4)
        return remote(
            quarter.at[p, 1], AT.at[p, 2 - dt, pl.ds(16 * x, 16)], ats.at[p, i], atr.at[p, i], tm + dt, xx * 2 + zh
        )

    def at_recv(p, i):
        dt, d = at_kinds[i]
        xx = lax.rem(x - d + 4, 4)
        return remote(
            quarter.at[p, 1], AT.at[p, 2 - dt, pl.ds(16 * xx, 16)], ats.at[p, i], atr.at[p, i], tm, lon
        )

    def transform_start(p):
        part = lax.dot(fwd[...], padded[...], precision=lax.Precision.HIGHEST, preferred_element_type=F32)
        amp[p] = jnp.where(half, pltpu.roll(part[:MW], MW, axis=1), part[MW:])
        for d in (1, 2, 3):
            rs_copy(p, d).start()

    def transform_cross(p):
        total = amp[p, pl.ds(16 * x, 16)]
        for d in (1, 2, 3):
            rs_copy(p, d).wait_recv()
            total = total + rs_buf[p, d]
        quarter[p, 0] = total
        z_copy(p).start()

    def transform_spread(p):
        z_copy(p).wait_recv()
        total = quarter[p, 0] + z_buf[p]
        quarter[p, 1] = total
        for i, (dt, _) in enumerate(at_kinds):
            when_t(dt, lambda i=i: at_copy(p, i).start())
        AT[p, 2, pl.ds(16 * x, 16)] = total

    def transform_finish(p):
        for i, (dt, _) in enumerate(at_kinds):
            when_t(-dt, lambda i=i: at_recv(p, i).wait_recv())

    def transform_done(p):
        for d in (1, 2, 3):
            rs_copy(p, d).wait_send()
        z_copy(p).wait_send()
        for i, (dt, _) in enumerate(at_kinds):
            when_t(dt, lambda i=i: at_copy(p, i).wait_send())

    def stack(a):
        c = jnp.where(half, 0.0, pltpu.roll(a, MW, axis=1))
        s = jnp.where(half, 0.0, a)
        return jnp.concatenate([c, s], axis=0)

    def filtered(p, X, field):
        a = [AT[p, i] for i in range(5)]
        three = jnp.concatenate(
            [stack(a[2]), stack(second(a[1], a[3], a[2])), stack(second2(*a))], axis=1
        )
        for s, n in ext_chunks:
            r = pl.ds(s, n)
            smooth = lax.dot(
                inv[pl.ds(s - EXT, n)], three, precision=lax.Precision.HIGHEST, preferred_element_type=F32
            )
            field[r] = keep * X[2, r] + shrink * smooth[:, :rows]
            TV[r] = keep * second(X[1, r], X[3, r], X[2, r]) + shrink * smooth[:, rows:2 * rows]
            T2V[r] = (
                keep * second2(X[0, r], X[1, r], X[2, r], X[3, r], X[4, r])
                + shrink * smooth[:, 2 * rows:]
            )

    starts, sizes = (0, 8, 12), (8, 4, 16)

    def stage_place(stage):
        return (k, x, z)[stage]

    def stage_device(stage, place):
        if stage == 0:
            return zl * 8 + place, lon
        if stage == 1:
            return tm, place * 2 + zh
        return lax.rem(place, 8) * 8 + k, x * 2 + place // 8

    def dot_copy(p, stage, d):
        size, start = sizes[stage], starts[stage]
        mine = stage_place(stage)
        t, l = stage_device(stage, lax.rem(mine + d, size))
        slot = dots.at[p, start + mine]
        return remote(slot, slot, ds_.at[p, start + d], dr.at[p, start + d], t, l)

    def dot_recv(p, stage, d):
        size, start = sizes[stage], starts[stage]
        mine = stage_place(stage)
        slot = dots.at[p, start + lax.rem(mine - d + size, size)]
        return remote(slot, slot, ds_.at[p, start + d], dr.at[p, start + d], tm, lon)

    def dot_send(p, stage, tile):
        dots[p, starts[stage] + stage_place(stage)] = tile
        for d in range(1, sizes[stage]):
            dot_copy(p, stage, d).start()

    def dot_take(p, stage):
        for d in range(1, sizes[stage]):
            dot_recv(p, stage, d).wait_recv()
        total = dots[p, starts[stage]]
        for i in range(1, sizes[stage]):
            total = total + dots[p, starts[stage] + i]
        return total

    def dot_done(p):
        for stage in range(3):
            for d in range(1, sizes[stage]):
                dot_copy(p, stage, d).wait_send()

    row8 = lax.broadcasted_iota(jnp.int32, (8, rows), 0)

    def pack(slope, curve):
        return jnp.where(row8 == 0, slope, jnp.where(row8 == 1, curve, 0.0))

    def ratio(tile):
        return jnp.sum(tile[0:1], axis=1, keepdims=True) / jnp.sum(tile[1:2], axis=1, keepdims=True)

    transform_start(0)
    halo_send(1, G)
    transform_cross(0)
    transform_spread(0)
    transform_finish(0)
    halo_wait(1, G)
    filtered(0, G, V0)
    acc = [jnp.zeros((1, rows), F32), jnp.zeros((1, rows), F32)]

    def emit_u(s, n, u):
        l, r = pl.ds(s - OFF, n), pl.ds(s, n)
        v = V0[r]
        u = W[l] * v + u
        U[2, r] = u
        padded[l] = u
        acc[0] = acc[0] + jnp.sum(G[2, r] * v, axis=0, keepdims=True)
        acc[1] = acc[1] + jnp.sum(v * u, axis=0, keepdims=True)

    operator(V0, emit_u)

    transform_start(1)
    dot_send(0, 0, pack(*acc))
    halo_send(2, U)
    transform_cross(1)
    dot_send(0, 1, dot_take(0, 0))
    dot_send(0, 2, dot_take(0, 1))
    transform_spread(1)
    step0 = ratio(dot_take(0, 2))
    transform_finish(1)
    halo_wait(2, U)
    filtered(1, U, V)
    acc[0] = acc[1] = jnp.zeros((1, rows), F32)

    def emit_last(s, n, u1):
        l, r = pl.ds(s - OFF, n), pl.ds(s, n)
        v1, v0, u0 = V[r], V0[r], U[2, r]
        u1 = W[l] * v1 + u1
        search = v0 - step0 * v1
        curved = u0 - step0 * u1
        gradient = G[2, r] - step0 * u0
        acc[0] = acc[0] + jnp.sum(gradient * search, axis=0, keepdims=True)
        acc[1] = acc[1] + jnp.sum(search * curved, axis=0, keepdims=True)
        V[r] = search
        obs[l] = curved
        res_g[l] = gradient
        res_a[l] = E[2, r] - step0 * v0

    operator(V, emit_last)
    dot_send(1, 0, pack(*acc))
    dot_send(1, 1, dot_take(1, 0))
    dot_send(1, 2, dot_take(1, 1))
    step1 = ratio(dot_take(1, 2))
    res_a[...] = res_a[...] - step1 * V[own]
    res_g[...] = res_g[...] - step1 * obs[...]
    ca = pltpu.make_async_copy(res_a, out_a.at[0], lsem.at[0])
    cg = pltpu.make_async_copy(res_g, out_g.at[0], lsem.at[1])
    ca.start()
    cg.start()
    for p, X in enumerate((E, G, U)):
        halo_done(p, X)
    for c in edge_b:
        c.wait_send()
    for p in range(2):
        transform_done(p)
        dot_done(p)
    ca.wait()
    cg.wait()


def on_device(NT, NL, first, obs, track, land, bw):
    _, N, rows = first.shape
    forward, inverse, row = tables(NL, N, rows)
    plane = pltpu.VMEM((N + 32, rows), F32)
    planes = pltpu.VMEM((5, N + 32, rows), F32)
    flat = pltpu.VMEM((N, rows), F32)
    whole = pltpu.VMEM((N, rows), jnp.int32)
    dma = pltpu.SemaphoreType.DMA
    hbm = pl.BlockSpec(memory_space=pl.ANY)
    return pl.pallas_call(
        functools.partial(kernel, NT, N),
        out_shape=[jax.ShapeDtypeStruct(first.shape, F32)] * 2,
        in_specs=[hbm] * 7 + [pl.BlockSpec(memory_space=pltpu.VMEM)],
        out_specs=[hbm] * 2,
        scratch_shapes=[
            planes, planes, planes,
            plane, flat, flat, whole, whole,
            pltpu.VMEM(forward.shape[1:], F32), pltpu.VMEM(inverse.shape[1:], F32),
            plane, plane, plane, plane, plane,
            pltpu.VMEM((forward.shape[2], rows), F32),
            pltpu.VMEM((2, MW, rows), F32),
            pltpu.VMEM((2, 4, 16, rows), F32),
            pltpu.VMEM((2, 2, 16, rows), F32),
            pltpu.VMEM((2, 16, rows), F32),
            pltpu.VMEM((2, 5, MW, rows), F32),
            pltpu.VMEM((2, 28, 8, rows), F32),
            flat, flat,
            dma((7,)), dma((3, 10)), dma((3, 10)), dma((2,)), dma((2,)),
            dma((2, 4)), dma((2, 4)), dma((2,)), dma((2,)), dma((2, 19)), dma((2, 19)),
            dma((2, 28)), dma((2, 28)),
        ],
        compiler_params=pltpu.CompilerParams(
            collective_id=0, has_side_effects=True, vmem_limit_bytes=40 * 1024 * 1024
        ),
    )(first, obs, track, land, bw, forward, inverse, row)


def solution(mesh):
    in_specs = (
        P("tm", "lon", None),
        P("tm", "lon", None),
        P("tm", "lon", None),
        P("lon", None),
        P("lon", None),
    )
    out_specs = (P("tm", "lon", None), P("tm", "lon", None))
    return jax.shard_map(
        functools.partial(on_device, mesh.shape["tm"], mesh.shape["lon"]),
        mesh=mesh, in_specs=in_specs, out_specs=out_specs, check_vma=False,
    )
```

```python
import functools

import jax
import jax.numpy as jnp
import numpy as np
from jax import lax
from jax.experimental import pallas as pl
from jax.experimental.pallas import tpu as pltpu
from jax.sharding import PartitionSpec as P

CAP = 64
MW = 64
MESH = pl.DeviceIdType.MESH
OFF = 16
EXT = 8
F32 = jnp.float32


def tables(segments, length, rows):
    circle = segments * length
    harmonic = np.arange(MW)
    w = np.where(harmonic == 0, 1.0 / circle, 2.0 / circle)
    padded = -(-length // 128) * 128
    forward = np.zeros((segments, 2 * MW, padded), np.float32)
    inverse = np.zeros((segments, length + 16, 2 * MW), np.float32)
    for s in range(segments):
        a = 2 * np.pi * ((np.arange(length) + s * length)[:, None] * harmonic % circle) / circle
        forward[s, :MW, :length] = np.cos(a).T
        forward[s, MW:, :length] = np.sin(a).T
        a = 2 * np.pi * ((np.arange(length + 16) - 8 + s * length)[:, None] * harmonic % circle) / circle
        inverse[s] = np.concatenate([w * np.cos(a), w * np.sin(a)], axis=1)
    phi = (90.0 - (rows - np.arange(rows) - 0.5) * 0.125) * (np.pi / 180.0)
    bend = 1.0 / (np.cos(phi) + 0.5) ** 2
    shrink = np.zeros(rows)
    shrink[rows - CAP:] = 0.9 * (np.arange(CAP) + 1.0) / CAP
    row = np.zeros((8, rows), np.float32)
    row[0] = bend
    row[1] = -2.0 * (bend + 1.0)
    row[2] = shrink
    row[3] = 1.0 - shrink
    return forward, inverse, row


def kernel(
    NT, N, first_ref, obs_ref, track_ref, land_ref, bw_ref, fwd_ref, inv_ref, row_ref,
    out_a, out_g,
    E, G, U, B, W, obs, track, land, fwd, inv, V, TV, T2V, Y, V0, padded, amp, rs_buf, quarter,
    z_buf, AT, dots_a, dots_b, ts, tr, ls, lr, res_a, res_g,
    hello, lsem, hs, hr, es, er, rs_, rr, xs, xr, zs, zr, ats, atr, ds_, dr,
):
    tm = lax.axis_index("tm")
    lon = lax.axis_index("lon")
    x, zh = lon // 2, lon % 2
    zl, k = tm // 8, tm % 8
    rows = 128

    def inside(t):
        return (t >= 0) & (t < NT)

    def when_t(dt, fn):
        if dt == 0:
            fn()
        else:
            pl.when(inside(tm + dt))(fn)

    def lon_at(d):
        return lax.rem(lon + d + 8, 8)

    own = pl.ds(OFF, N)
    loads = [
        pltpu.make_async_copy(first_ref.at[0], E.at[2, own], lsem.at[0]),
        pltpu.make_async_copy(bw_ref, B.at[own], lsem.at[1]),
        pltpu.make_async_copy(obs_ref.at[0], obs, lsem.at[2]),
        pltpu.make_async_copy(track_ref.at[0], track, lsem.at[3]),
        pltpu.make_async_copy(land_ref, land, lsem.at[4]),
        pltpu.make_async_copy(fwd_ref.at[lon], fwd, lsem.at[5]),
        pltpu.make_async_copy(inv_ref.at[lon], inv, lsem.at[6]),
    ]
    loads[0].start()

    barrier = pltpu.get_barrier_semaphore()

    def greet(t, l, sem=barrier):
        pl.semaphore_signal(sem, inc=1, device_id={"tm": t, "lon": l}, device_id_type=MESH)

    z = zh * 8 + zl

    def on_z(place, xx):
        place = lax.rem(place + 16, 16)
        return lax.rem(place, 8) * 8 + k, lax.rem(xx + 4, 4) * 2 + place // 8

    fours = [(dz, dx) for dz in (4, -4) for dx in (0, 1, -1)]
    for dz, dx in fours:
        greet(*on_z(z + dz, x + dx))
    for dz in (3, -3, 2, -2, 1, -1):
        greet(*on_z(z + dz, x))
    for d in range(1, 8):
        greet(zl * 8 + lax.rem(k + d, 8), lon)
    for d in range(1, 4):
        greet(tm, lon_at(2 * d))
    count = jnp.int32(len(fours) + 6 + 7 + 3)
    for dt in (-2, -1, 1, 2):
        when_t(dt, lambda dt=dt: greet(tm + dt, lon))
        count = count + jnp.where(inside(tm + dt), 1, 0)
    for c in loads[1:]:
        c.start()

    for dt in (-2, -1, 1, 2):

        @pl.when(jnp.logical_not(inside(tm + dt)))
        def _(dt=dt):
            for X in (E, G, U):
                X[2 + dt] = jnp.zeros(X.shape[1:], F32)
            for p in range(2):
                AT[p, 2 + dt] = jnp.zeros(AT.shape[2:], F32)
            if abs(dt) == 1:
                for p in range(3):
                    tr[p, (dt + 1) // 2] = jnp.zeros(tr.shape[2:], F32)

    padded[pl.ds(N, padded.shape[0] - N)] = jnp.zeros((padded.shape[0] - N, rows), F32)

    with jax.named_scope("entry barrier"):
        pl.semaphore_wait(barrier, count)
    for dz, dx in fours:
        greet(*on_z(z + dz, x + dx), sem=hello)

    def remote(src, dst, send, recv, t, l):
        return pltpu.make_async_remote_copy(
            src_ref=src, dst_ref=dst, send_sem=send, recv_sem=recv,
            device_id={"tm": t, "lon": l}, device_id_type=MESH,
        )

    shifts = (1, -1, 2, -2)

    def halo_copy(p, X, i):
        dt = shifts[i]
        return remote(X.at[2, own], X.at[2 - dt, own], hs.at[p, i], hr.at[p, i], tm + dt, lon)

    def halo_send(p, X):
        for i, dt in enumerate(shifts):
            when_t(dt, lambda i=i: halo_copy(p, X, i).start())

    def halo_wait(p, X):
        for i, dt in enumerate(shifts):
            when_t(-dt, lambda i=i: halo_copy(p, X, i).wait_recv())

    def halo_done(p, X):
        for i, dt in enumerate(shifts):
            when_t(dt, lambda i=i: halo_copy(p, X, i).wait_send())

    first_row, last_row = OFF, OFF + N - 1

    def edge_copy(p, i):
        return remote(ts.at[p], tr.at[p, i], es.at[p, i], er.at[p, i], tm + (1, -1)[i], lon)

    def edge_send(p, X):
        ts[p, 0:1] = X[2, first_row:first_row + 1]
        ts[p, 1:2] = X[2, last_row:last_row + 1]
        for i, dt in enumerate((1, -1)):
            when_t(dt, lambda i=i: edge_copy(p, i).start())

    def rim_copy(p, i):
        return remote(ls.at[p, i], lr.at[p, i], rs_.at[p, i], rr.at[p, i], tm, lon_at((1, -1)[i]))

    def rim_send(p, X):
        for i, dt in enumerate((1, -1)):
            when_t(-dt, lambda i=i: edge_copy(p, i).wait_recv())
        bent = tr[p, 0] + tr[p, 1] - 2.0 * ts[p]
        ls[p, 0, 0:1] = X[2, last_row:last_row + 1]
        ls[p, 0, 1:2] = X[2, last_row - 1:last_row]
        ls[p, 0, 2:3] = bent[1:2]
        ls[p, 0, 3:4] = B[last_row:last_row + 1]
        ls[p, 1, 0:1] = X[2, first_row:first_row + 1]
        ls[p, 1, 1:2] = X[2, first_row + 1:first_row + 2]
        ls[p, 1, 2:3] = bent[0:1]
        ls[p, 1, 3:4] = B[first_row:first_row + 1]
        for i in range(2):
            rim_copy(p, i).start()

    def rim_take(p, X):
        for i in range(2):
            rim_copy(p, i).wait_recv()
        for i, (near, far) in enumerate(((first_row - 1, first_row - 2), (last_row + 1, last_row + 2))):
            X[2, near:near + 1] = lr[p, i, 0:1]
            X[2, far:far + 1] = lr[p, i, 1:2]
            X[1, near:near + 1] = lr[p, i, 2:3] + 2.0 * lr[p, i, 0:1]
            X[3, near:near + 1] = jnp.zeros((1, rows), F32)
            if p == 0:
                B[near:near + 1] = lr[p, i, 3:4]

    def edge_done(p):
        for i, dt in enumerate((1, -1)):
            when_t(dt, lambda i=i: edge_copy(p, i).wait_send())
            rim_copy(p, i).wait_send()

    with jax.named_scope("guess edges"):
        loads[0].wait()
        edge_send(0, E)
        halo_send(0, E)
    loads[1].wait()
    with jax.named_scope("far hello"):
        pl.semaphore_wait(hello, len(fours))
    with jax.named_scope("guess rim"):
        rim_send(0, E)

    lane = lax.broadcasted_iota(jnp.int32, (8, rows), 1)
    first_lane, last_lane = lane[:1] == 0, lane[:1] == rows - 1
    bend = row_ref[0:1]
    centre = row_ref[1:2]
    shrink = row_ref[2:3]
    keep = row_ref[3:4]

    def flat(ref, start, n):
        v = ref[pl.ds(start, n)]
        up, down = ref[pl.ds(start + 1, n)], ref[pl.ds(start - 1, n)]
        lo = jnp.where(first_lane, 0.0, pltpu.roll(v, 1, axis=1))
        hi = jnp.where(last_lane, 0.0, pltpu.roll(v, rows - 1, axis=1))
        return bend * (up + down) + (lo + hi) + centre * v

    ext_chunks = [(EXT, 96), (EXT + 96, 96), (EXT + 192, 96), (EXT + 288, N + 16 - 288)]
    own_chunks = [(OFF + c, 72) for c in range(0, N, 72)]
    centre_t2 = jnp.where((tm == 0) | (tm == NT - 1), 5.0, 6.0).astype(F32)

    def second(a, b, c):
        return a + b - 2.0 * c

    def second2(a, b, c, d, e):
        return a + e - 4.0 * (b + d) + centre_t2 * c

    def operator(field, emit):
        for s, n in ext_chunks:
            Y[pl.ds(s, n)] = B[pl.ds(s, n)] * (TV[pl.ds(s, n)] + flat(field, s, n))
        for s, n in own_chunks:
            emit(s, n, B[pl.ds(s, n)] * (T2V[pl.ds(s, n)] + flat(TV, s, n)) + flat(Y, s, n))

    with jax.named_scope("weights"):
        for c in loads[2:5]:
            c.wait()
        W[...] = track[...].astype(F32) * (1.0 - land[...].astype(F32))

    with jax.named_scope("guess halo wait"):
        halo_wait(0, E)
    with jax.named_scope("guess rim wait"):
        rim_take(0, E)
    for s, n in ext_chunks:
        r = pl.ds(s, n)
        TV[r] = second(E[1, r], E[3, r], E[2, r])
    for s, n in own_chunks:
        r = pl.ds(s, n)
        T2V[r] = second2(E[0, r], E[1, r], E[2, r], E[3, r], E[4, r])

    def emit_g(s, n, u):
        l = pl.ds(s - OFF, n)
        g = W[l] * (E[2, pl.ds(s, n)] - obs[l]) + u
        G[2, pl.ds(s, n)] = g
        padded[l] = g

    with jax.named_scope("first operator"):
        operator(E.at[2], emit_g)
    for c in loads[5:]:
        c.wait()

    half = lax.broadcasted_iota(jnp.int32, (MW, rows), 1) < MW

    def rs_copy(p, d):
        q = lax.rem(x + d, 4)
        return remote(
            amp.at[p, pl.ds(16 * q, 16)], rs_buf.at[p, d], xs.at[p, d], xr.at[p, d], tm, q * 2 + zh
        )

    def z_copy(p):
        return remote(quarter.at[p, 0], z_buf.at[p], zs.at[p], zr.at[p], tm, lon + 1 - 2 * zh)

    at_kinds = [(dt, d) for dt in (0, 1, -1, 2, -2) for d in range(4) if (dt, d) != (0, 0)]

    def at_copy(p, i):
        dt, d = at_kinds[i]
        xx = lax.rem(x + d, 4)
        return remote(
            quarter.at[p, 1], AT.at[p, 2 - dt, pl.ds(16 * x, 16)], ats.at[p, i], atr.at[p, i], tm + dt, xx * 2 + zh
        )

    def at_recv(p, i):
        dt, d = at_kinds[i]
        xx = lax.rem(x - d + 4, 4)
        return remote(
            quarter.at[p, 1], AT.at[p, 2 - dt, pl.ds(16 * xx, 16)], ats.at[p, i], atr.at[p, i], tm, lon
        )

    def transform_start(p):
        part = lax.dot(fwd[...], padded[...], precision=lax.Precision.HIGHEST, preferred_element_type=F32)
        amp[p] = jnp.where(half, pltpu.roll(part[:MW], MW, axis=1), part[MW:])
        for d in (1, 2, 3):
            rs_copy(p, d).start()

    def transform_cross(p):
        total = amp[p, pl.ds(16 * x, 16)]
        for d in (1, 2, 3):
            rs_copy(p, d).wait_recv()
            total = total + rs_buf[p, d]
        quarter[p, 0] = total
        z_copy(p).start()

    def transform_spread(p):
        z_copy(p).wait_recv()
        total = quarter[p, 0] + z_buf[p]
        quarter[p, 1] = total
        for i, (dt, _) in enumerate(at_kinds):
            when_t(dt, lambda i=i: at_copy(p, i).start())
        AT[p, 2, pl.ds(16 * x, 16)] = total

    def transform_finish(p):
        for i, (dt, _) in enumerate(at_kinds):
            when_t(-dt, lambda i=i: at_recv(p, i).wait_recv())

    def transform_done(p):
        for d in (1, 2, 3):
            rs_copy(p, d).wait_send()
        z_copy(p).wait_send()
        for i, (dt, _) in enumerate(at_kinds):
            when_t(dt, lambda i=i: at_copy(p, i).wait_send())

    def stack(a):
        c = jnp.where(half, 0.0, pltpu.roll(a, MW, axis=1))
        s = jnp.where(half, 0.0, a)
        return jnp.concatenate([c, s], axis=0)

    def filtered(p, X, field):
        a = [AT[p, i] for i in range(5)]
        three = jnp.concatenate(
            [stack(a[2]), stack(second(a[1], a[3], a[2])), stack(second2(*a))], axis=1
        )
        for s, n in ext_chunks:
            r = pl.ds(s, n)
            smooth = lax.dot(
                inv[pl.ds(s - EXT, n)], three, precision=lax.Precision.HIGHEST, preferred_element_type=F32
            )
            field[r] = keep * X[2, r] + shrink * smooth[:, :rows]
            TV[r] = keep * second(X[1, r], X[3, r], X[2, r]) + shrink * smooth[:, rows:2 * rows]
            T2V[r] = (
                keep * second2(X[0, r], X[1, r], X[2, r], X[3, r], X[4, r])
                + shrink * smooth[:, 2 * rows:]
            )

    sizes = (32, 16)

    def stage_place(stage):
        return (x * 8 + k, z)[stage]

    def stage_device(stage, place):
        if stage == 0:
            return zl * 8 + lax.rem(place, 8), (place // 8) * 2 + zh
        return on_z(place, x)

    def dot_slots(stage):
        return (dots_a, dots_b)[stage]

    def dot_copy(p, stage, d):
        size, mine, slots = sizes[stage], stage_place(stage), dot_slots(stage)
        t, l = stage_device(stage, lax.rem(mine + d, size))
        slot = slots.at[p, mine]
        return remote(slot, slot, ds_.at[p, stage, d], dr.at[p, stage, d], t, l)

    def dot_recv(p, stage, d):
        size, mine, slots = sizes[stage], stage_place(stage), dot_slots(stage)
        slot = slots.at[p, lax.rem(mine - d + size, size)]
        return remote(slot, slot, ds_.at[p, stage, d], dr.at[p, stage, d], tm, lon)

    def dot_send(p, stage, line):
        dot_slots(stage)[p, stage_place(stage)] = line

        @pl.loop(1, sizes[stage])
        def _(d):
            dot_copy(p, stage, d).start()

    def dot_take(p, stage):
        @pl.loop(1, sizes[stage])
        def _(d):
            dot_recv(p, stage, d).wait_recv()

        total = dot_slots(stage)[p, 0]
        for i in range(1, sizes[stage]):
            total = total + dot_slots(stage)[p, i]
        return total

    def dot_done(p):
        for stage in range(2):

            @pl.loop(1, sizes[stage])
            def _(d):
                dot_copy(p, stage, d).wait_send()

    low = lane[:1] < MW

    def pack(slope, curve):
        return jnp.where(low, slope + pltpu.roll(slope, MW, axis=1), curve + pltpu.roll(curve, MW, axis=1))

    def ratio(line):
        slope = jnp.sum(jnp.where(low, line, 0.0), axis=1, keepdims=True)
        return slope / jnp.sum(jnp.where(low, 0.0, line), axis=1, keepdims=True)

    with jax.named_scope("transform zero"):
        transform_start(0)
    with jax.named_scope("edges one send"):
        edge_send(1, G)
    with jax.named_scope("cross zero"):
        transform_cross(0)
    with jax.named_scope("rim one send"):
        rim_send(1, G)
    with jax.named_scope("halo one send"):
        halo_send(1, G)
    with jax.named_scope("spread zero"):
        transform_spread(0)
    with jax.named_scope("rim one wait"):
        rim_take(1, G)
    with jax.named_scope("halo one wait"):
        halo_wait(1, G)
    with jax.named_scope("finish zero"):
        transform_finish(0)
    with jax.named_scope("filter zero"):
        filtered(0, G, V0)
    acc = [jnp.zeros((1, rows), F32), jnp.zeros((1, rows), F32)]

    def emit_u(s, n, u):
        l, r = pl.ds(s - OFF, n), pl.ds(s, n)
        v = V0[r]
        u = W[l] * v + u
        U[2, r] = u
        padded[l] = u
        acc[0] = acc[0] + jnp.sum(G[2, r] * v, axis=0, keepdims=True)
        acc[1] = acc[1] + jnp.sum(v * u, axis=0, keepdims=True)

    with jax.named_scope("operator one"):
        operator(V0, emit_u)

    with jax.named_scope("transform one"):
        transform_start(1)
    with jax.named_scope("edges two send"):
        dot_send(0, 0, pack(*acc))
        edge_send(2, U)
    with jax.named_scope("cross one"):
        transform_cross(1)
    with jax.named_scope("rim two send"):
        rim_send(2, U)
    with jax.named_scope("halo two send"):
        halo_send(2, U)
    with jax.named_scope("sums zero"):
        dot_send(0, 1, dot_take(0, 0))
    with jax.named_scope("spread one"):
        transform_spread(1)
    with jax.named_scope("rim two wait"):
        rim_take(2, U)
    with jax.named_scope("step zero"):
        step0 = ratio(dot_take(0, 1))
    with jax.named_scope("halo two wait"):
        halo_wait(2, U)
    with jax.named_scope("finish one"):
        transform_finish(1)
    with jax.named_scope("filter one"):
        filtered(1, U, V)
    acc[0] = acc[1] = jnp.zeros((1, rows), F32)

    def emit_last(s, n, u1):
        l, r = pl.ds(s - OFF, n), pl.ds(s, n)
        v1, v0, u0 = V[r], V0[r], U[2, r]
        u1 = W[l] * v1 + u1
        search = v0 - step0 * v1
        curved = u0 - step0 * u1
        gradient = G[2, r] - step0 * u0
        acc[0] = acc[0] + jnp.sum(gradient * search, axis=0, keepdims=True)
        acc[1] = acc[1] + jnp.sum(search * curved, axis=0, keepdims=True)
        V[r] = search
        obs[l] = curved
        res_g[l] = gradient
        res_a[l] = E[2, r] - step0 * v0

    with jax.named_scope("operator two"):
        operator(V, emit_last)
    with jax.named_scope("sums one a"):
        dot_send(1, 0, pack(*acc))
    with jax.named_scope("sums one b"):
        dot_send(1, 1, dot_take(1, 0))
    with jax.named_scope("sums one c"):
        step1 = ratio(dot_take(1, 1))
    with jax.named_scope("update"):
        res_a[...] = res_a[...] - step1 * V[own]
        res_g[...] = res_g[...] - step1 * obs[...]
    ca = pltpu.make_async_copy(res_a, out_a.at[0], lsem.at[0])
    cg = pltpu.make_async_copy(res_g, out_g.at[0], lsem.at[1])
    ca.start()
    cg.start()
    with jax.named_scope("drain"):
        for p, X in enumerate((E, G, U)):
            halo_done(p, X)
            edge_done(p)
        for p in range(2):
            transform_done(p)
            dot_done(p)
    ca.wait()
    cg.wait()


def on_device(NT, NL, first, obs, track, land, bw):
    _, N, rows = first.shape
    forward, inverse, row = tables(NL, N, rows)
    plane = pltpu.VMEM((N + 32, rows), F32)
    planes = pltpu.VMEM((5, N + 32, rows), F32)
    flat = pltpu.VMEM((N, rows), F32)
    whole = pltpu.VMEM((N, rows), jnp.int32)
    dma = pltpu.SemaphoreType.DMA
    hbm = pl.BlockSpec(memory_space=pltpu.HBM)
    return pl.pallas_call(
        functools.partial(kernel, NT, N),
        out_shape=[jax.ShapeDtypeStruct(first.shape, F32)] * 2,
        in_specs=[hbm] * 7 + [pl.BlockSpec(memory_space=pltpu.VMEM)],
        out_specs=[hbm] * 2,
        scratch_shapes=[
            planes, planes, planes,
            plane, flat, flat, whole, whole,
            pltpu.VMEM(forward.shape[1:], F32), pltpu.VMEM(inverse.shape[1:], F32),
            plane, plane, plane, plane, plane,
            pltpu.VMEM((forward.shape[2], rows), F32),
            pltpu.VMEM((2, MW, rows), F32),
            pltpu.VMEM((2, 4, 16, rows), F32),
            pltpu.VMEM((2, 2, 16, rows), F32),
            pltpu.VMEM((2, 16, rows), F32),
            pltpu.VMEM((2, 5, MW, rows), F32),
            pltpu.VMEM((2, 32, 1, rows), F32),
            pltpu.VMEM((2, 16, 1, rows), F32),
            pltpu.VMEM((3, 2, rows), F32),
            pltpu.VMEM((3, 2, 2, rows), F32),
            pltpu.VMEM((3, 2, 4, rows), F32),
            pltpu.VMEM((3, 2, 4, rows), F32),
            flat, flat,
            pltpu.SemaphoreType.REGULAR, dma((7,)), dma((3, 4)), dma((3, 4)),
            dma((3, 2)), dma((3, 2)), dma((3, 2)), dma((3, 2)),
            dma((2, 4)), dma((2, 4)), dma((2,)), dma((2,)), dma((2, 19)), dma((2, 19)),
            dma((2, 2, 32)), dma((2, 2, 32)),
        ],
        compiler_params=pltpu.CompilerParams(
            collective_id=0, has_side_effects=True, vmem_limit_bytes=56 * 1024 * 1024
        ),
    )(first, obs, track, land, bw, forward, inverse, row)


def solution(mesh):
    in_specs = (
        P("tm", "lon", None),
        P("tm", "lon", None),
        P("tm", "lon", None),
        P("lon", None),
        P("lon", None),
    )
    out_specs = (P("tm", "lon", None), P("tm", "lon", None))
    return jax.shard_map(
        functools.partial(on_device, mesh.shape["tm"], mesh.shape["lon"]),
        mesh=mesh, in_specs=in_specs, out_specs=out_specs, check_vma=False,
    )
```

```python
import functools

import jax
import jax.numpy as jnp
import numpy as np
from jax import lax
from jax.experimental import pallas as pl
from jax.experimental.pallas import tpu as pltpu
from jax.sharding import PartitionSpec as P

CAP = 64
MW = 64
MESH = pl.DeviceIdType.MESH
OFF = 16
EXT = 8
F32 = jnp.float32


def tables(segments, length, rows):
    circle = segments * length
    harmonic = np.arange(MW)
    w = np.where(harmonic == 0, 1.0 / circle, 2.0 / circle)
    padded = -(-length // 128) * 128
    forward = np.zeros((segments, 2 * MW, padded), np.float32)
    inverse = np.zeros((segments, length + 16, 2 * MW), np.float32)
    for s in range(segments):
        a = 2 * np.pi * ((np.arange(length) + s * length)[:, None] * harmonic % circle) / circle
        forward[s, :MW, :length] = np.cos(a).T
        forward[s, MW:, :length] = np.sin(a).T
        a = 2 * np.pi * ((np.arange(length + 16) - 8 + s * length)[:, None] * harmonic % circle) / circle
        inverse[s] = np.concatenate([w * np.cos(a), w * np.sin(a)], axis=1)
    phi = (90.0 - (rows - np.arange(rows) - 0.5) * 0.125) * (np.pi / 180.0)
    bend = 1.0 / (np.cos(phi) + 0.5) ** 2
    shrink = np.zeros(rows)
    shrink[rows - CAP:] = 0.9 * (np.arange(CAP) + 1.0) / CAP
    row = np.zeros((8, rows), np.float32)
    row[0] = bend
    row[1] = -2.0 * (bend + 1.0)
    row[2] = shrink
    row[3] = 1.0 - shrink
    return forward, inverse, row


def kernel(
    NT, N, first_ref, obs_ref, track_ref, land_ref, bw_ref, fwd_ref, inv_ref, row_hbm,
    out_a, out_s, out_g, out_c, out_step,
    row_ref, E, G, U, B, W, obs, track, land, fwd, inv, V, TV, T2V, Y, V0, padded, amp, rs_buf, quarter,
    z_buf, AT, dots_a, dots_b, ts, tr, ls, lr,
    hello, lsem, hs, hr, es, er, rs_, rr, xs, xr, zs, zr, ats, atr, ds_, dr,
):
    tm = lax.axis_index("tm")
    lon = lax.axis_index("lon")
    x, zh = lon // 2, lon % 2
    zl, k = tm // 8, tm % 8
    rows = 128

    def inside(t):
        return (t >= 0) & (t < NT)

    def when_t(dt, fn):
        if dt == 0:
            fn()
        else:
            pl.when(inside(tm + dt))(fn)

    def lon_at(d):
        return lax.rem(lon + d + 8, 8)

    own = pl.ds(OFF, N)
    loads = [
        pltpu.make_async_copy(first_ref.at[0], E.at[2, own], lsem.at[0]),
        pltpu.make_async_copy(bw_ref, B.at[own], lsem.at[1]),
        pltpu.make_async_copy(obs_ref.at[0], obs, lsem.at[2]),
        pltpu.make_async_copy(track_ref.at[0], track, lsem.at[3]),
        pltpu.make_async_copy(land_ref, land, lsem.at[4]),
        pltpu.make_async_copy(fwd_ref.at[lon], fwd, lsem.at[5]),
        pltpu.make_async_copy(inv_ref.at[lon], inv, lsem.at[6]),
        pltpu.make_async_copy(row_hbm, row_ref, lsem.at[7]),
    ]
    loads[0].start()
    loads[7].start()

    barrier = pltpu.get_barrier_semaphore()

    def greet(t, l, sem=barrier):
        pl.semaphore_signal(sem, inc=1, device_id={"tm": t, "lon": l}, device_id_type=MESH)

    z = zh * 8 + zl

    def on_z(place, xx):
        place = lax.rem(place + 16, 16)
        return lax.rem(place, 8) * 8 + k, lax.rem(xx + 4, 4) * 2 + place // 8

    fours = [(dz, dx) for dz in (4, -4) for dx in (0, 1, -1)]
    for dz, dx in fours:
        greet(*on_z(z + dz, x + dx))
    for dz in (3, -3, 2, -2, 1, -1):
        greet(*on_z(z + dz, x))
    for d in range(1, 8):
        greet(zl * 8 + lax.rem(k + d, 8), lon)
    for d in range(1, 4):
        greet(tm, lon_at(2 * d))
    count = jnp.int32(len(fours) + 6 + 7 + 3)
    for dt in (-2, -1, 1, 2):
        when_t(dt, lambda dt=dt: greet(tm + dt, lon))
        count = count + jnp.where(inside(tm + dt), 1, 0)
    for c in loads[1:7]:
        c.start()

    for dt in (-2, -1, 1, 2):

        @pl.when(jnp.logical_not(inside(tm + dt)))
        def _(dt=dt):
            for X in (E, G, U):
                X[2 + dt] = jnp.zeros(X.shape[1:], F32)
            for p in range(2):
                AT[p, 2 + dt] = jnp.zeros(AT.shape[2:], F32)
            if abs(dt) == 1:
                for p in range(3):
                    tr[p, (dt + 1) // 2] = jnp.zeros(tr.shape[2:], F32)

    padded[pl.ds(N, padded.shape[0] - N)] = jnp.zeros((padded.shape[0] - N, rows), F32)

    with jax.named_scope("entry barrier"):
        pl.semaphore_wait(barrier, count)
    for dz, dx in fours:
        greet(*on_z(z + dz, x + dx), sem=hello)

    def remote(src, dst, send, recv, t, l):
        return pltpu.make_async_remote_copy(
            src_ref=src, dst_ref=dst, send_sem=send, recv_sem=recv,
            device_id={"tm": t, "lon": l}, device_id_type=MESH,
        )

    side = 1 - 2 * lax.rem(tm, 2)
    send_days = (-side, 2 * side, side)
    recv_days = (-side, -2 * side, side, 2 * side)

    def plane_copy(p, X, i):
        dt = send_days[i]
        return remote(X.at[2, own], X.at[2 - dt, own], hs.at[p, i], hr.at[p, i], tm + dt, lon)

    def hand_copy(p, X):
        return remote(X.at[2 - side, own], X.at[2 - 2 * side, own], hs.at[p, 3], hr.at[p, 3], tm + side, lon)

    def plane_recv(p, X, i):
        return remote(X.at[2, own], X.at[2 + recv_days[i], own], hs.at[p, i], hr.at[p, i], tm, lon)

    def halo_send(p, X):
        for i in range(3):
            pl.when(inside(tm + send_days[i]))(lambda i=i: plane_copy(p, X, i).start())

    def halo_hand(p, X):
        @pl.when(inside(tm - side))
        def _():
            plane_recv(p, X, 0).wait_recv()
            hand_copy(p, X).start()

    def halo_wait(p, X):
        for i in (1, 2, 3):
            pl.when(inside(tm + recv_days[i]))(lambda i=i: plane_recv(p, X, i).wait_recv())

    def halo_done(p, X):
        for i in range(3):
            pl.when(inside(tm + send_days[i]))(lambda i=i: plane_copy(p, X, i).wait_send())
        pl.when(inside(tm - side))(lambda: hand_copy(p, X).wait_send())

    first_row, last_row = OFF, OFF + N - 1

    def edge_copy(p, i):
        return remote(ts.at[p], tr.at[p, i], es.at[p, i], er.at[p, i], tm + (1, -1)[i], lon)

    def edge_send(p, X):
        ts[p, 0:1] = X[2, first_row:first_row + 1]
        ts[p, 1:2] = X[2, last_row:last_row + 1]
        for i, dt in enumerate((1, -1)):
            when_t(dt, lambda i=i: edge_copy(p, i).start())

    def rim_copy(p, i):
        return remote(ls.at[p, i], lr.at[p, i], rs_.at[p, i], rr.at[p, i], tm, lon_at((1, -1)[i]))

    def rim_send(p, X):
        for i, dt in enumerate((1, -1)):
            when_t(-dt, lambda i=i: edge_copy(p, i).wait_recv())
        bent = tr[p, 0] + tr[p, 1] - 2.0 * ts[p]
        ls[p, 0, 0:1] = X[2, last_row:last_row + 1]
        ls[p, 0, 1:2] = X[2, last_row - 1:last_row]
        ls[p, 0, 2:3] = bent[1:2]
        ls[p, 0, 3:4] = B[last_row:last_row + 1]
        ls[p, 1, 0:1] = X[2, first_row:first_row + 1]
        ls[p, 1, 1:2] = X[2, first_row + 1:first_row + 2]
        ls[p, 1, 2:3] = bent[0:1]
        ls[p, 1, 3:4] = B[first_row:first_row + 1]
        for i in range(2):
            rim_copy(p, i).start()

    def rim_take(p, X):
        for i in range(2):
            rim_copy(p, i).wait_recv()
        for i, (near, far) in enumerate(((first_row - 1, first_row - 2), (last_row + 1, last_row + 2))):
            X[2, near:near + 1] = lr[p, i, 0:1]
            X[2, far:far + 1] = lr[p, i, 1:2]
            X[1, near:near + 1] = lr[p, i, 2:3] + 2.0 * lr[p, i, 0:1]
            X[3, near:near + 1] = jnp.zeros((1, rows), F32)
            if p == 0:
                B[near:near + 1] = lr[p, i, 3:4]

    def edge_done(p):
        for i, dt in enumerate((1, -1)):
            when_t(dt, lambda i=i: edge_copy(p, i).wait_send())
            rim_copy(p, i).wait_send()

    with jax.named_scope("guess edges"):
        loads[0].wait()
        edge_send(0, E)
        halo_send(0, E)
    loads[1].wait()
    with jax.named_scope("far hello"):
        pl.semaphore_wait(hello, len(fours))
    with jax.named_scope("guess rim"):
        rim_send(0, E)
    with jax.named_scope("guess hand on"):
        halo_hand(0, E)

    lane = lax.broadcasted_iota(jnp.int32, (8, rows), 1)
    first_lane, last_lane = lane[:1] == 0, lane[:1] == rows - 1
    loads[7].wait()
    bend = row_ref[0:1]
    centre = row_ref[1:2]
    shrink = row_ref[2:3]
    keep = row_ref[3:4]

    def flat(ref, start, n):
        v = ref[pl.ds(start, n)]
        up, down = ref[pl.ds(start + 1, n)], ref[pl.ds(start - 1, n)]
        lo = jnp.where(first_lane, 0.0, pltpu.roll(v, 1, axis=1))
        hi = jnp.where(last_lane, 0.0, pltpu.roll(v, rows - 1, axis=1))
        return bend * (up + down) + (lo + hi) + centre * v

    ext_chunks = [(EXT, 96), (EXT + 96, 96), (EXT + 192, 96), (EXT + 288, N + 16 - 288)]
    own_chunks = [(OFF + c, 72) for c in range(0, N, 72)]
    centre_t2 = jnp.where((tm == 0) | (tm == NT - 1), 5.0, 6.0).astype(F32)

    def second(a, b, c):
        return a + b - 2.0 * c

    def second2(a, b, c, d, e):
        return a + e - 4.0 * (b + d) + centre_t2 * c

    def operator(field, emit):
        for s, n in ext_chunks:
            Y[pl.ds(s, n)] = B[pl.ds(s, n)] * (TV[pl.ds(s, n)] + flat(field, s, n))
        for s, n in own_chunks:
            emit(s, n, B[pl.ds(s, n)] * (T2V[pl.ds(s, n)] + flat(TV, s, n)) + flat(Y, s, n))

    with jax.named_scope("weights"):
        for c in loads[2:5]:
            c.wait()
        W[...] = track[...].astype(F32) * (1.0 - land[...].astype(F32))

    with jax.named_scope("guess halo wait"):
        halo_wait(0, E)
    with jax.named_scope("guess rim wait"):
        rim_take(0, E)
    for s, n in ext_chunks:
        r = pl.ds(s, n)
        TV[r] = second(E[1, r], E[3, r], E[2, r])
    for s, n in own_chunks:
        r = pl.ds(s, n)
        T2V[r] = second2(E[0, r], E[1, r], E[2, r], E[3, r], E[4, r])

    def emit_g(s, n, u):
        l = pl.ds(s - OFF, n)
        g = W[l] * (E[2, pl.ds(s, n)] - obs[l]) + u
        G[2, pl.ds(s, n)] = g
        padded[l] = g

    with jax.named_scope("first operator"):
        operator(E.at[2], emit_g)
    for c in loads[5:7]:
        c.wait()

    half = lax.broadcasted_iota(jnp.int32, (MW, rows), 1) < MW

    def rs_copy(p, d):
        q = lax.rem(x + d, 4)
        return remote(amp.at[p, pl.ds(16 * q, 16)], rs_buf.at[p, d], xs.at[p], xr.at[p], tm, q * 2 + zh)

    def rs_all(p):
        return remote(rs_buf.at[p, pl.ds(1, 3)], rs_buf.at[p, pl.ds(1, 3)], xs.at[p], xr.at[p], tm, lon)

    def z_copy(p):
        return remote(quarter.at[p, 0], z_buf.at[p], zs.at[p], zr.at[p], tm, lon + 1 - 2 * zh)

    days = (2, -2, 1, -1, 0)

    def at_copy(p, i, d):
        dt = days[i]
        xx = lax.rem(x + d, 4)
        return remote(
            quarter.at[p, 1], AT.at[p, 2 - dt, pl.ds(16 * x, 16)], ats.at[p, i], atr.at[p, i], tm + dt, xx * 2 + zh
        )

    def at_all(p, i):
        some = AT.at[p, 2 - days[i], pl.ds(0, MW if days[i] else MW - 16)]
        return remote(some, some, ats.at[p, i], atr.at[p, i], tm, lon)

    def transform_start(p):
        part = lax.dot(fwd[...], padded[...], precision=lax.Precision.HIGHEST, preferred_element_type=F32)
        amp[p] = jnp.where(half, pltpu.roll(part[:MW], MW, axis=1), part[MW:])
        for d in (2, 1, 3):
            rs_copy(p, d).start()

    def transform_cross(p):
        total = amp[p, pl.ds(16 * x, 16)]
        rs_all(p).wait_recv()
        for d in (1, 2, 3):
            total = total + rs_buf[p, d]
        quarter[p, 0] = total
        z_copy(p).start()

    def transform_spread(p):
        z_copy(p).wait_recv()
        total = quarter[p, 0] + z_buf[p]
        quarter[p, 1] = total
        for i, dt in enumerate(days):
            for d in (2, 1, 3, 0) if dt else (2, 1, 3):
                when_t(dt, lambda i=i, d=d: at_copy(p, i, d).start())
        AT[p, 2, pl.ds(16 * x, 16)] = total

    def transform_finish(p):
        for i, dt in enumerate(days):
            when_t(-dt, lambda i=i: at_all(p, i).wait_recv())

    def transform_done(p):
        rs_all(p).wait_send()
        z_copy(p).wait_send()
        for i, dt in enumerate(days):
            when_t(dt, lambda i=i: at_all(p, i).wait_send())

    def stack(a):
        c = jnp.where(half, 0.0, pltpu.roll(a, MW, axis=1))
        s = jnp.where(half, 0.0, a)
        return jnp.concatenate([c, s], axis=0)

    def filtered(p, X, field):
        a = [AT[p, i] for i in range(5)]
        three = jnp.concatenate(
            [stack(a[2]), stack(second(a[1], a[3], a[2])), stack(second2(*a))], axis=1
        )
        for s, n in ext_chunks:
            r = pl.ds(s, n)
            smooth = lax.dot(
                inv[pl.ds(s - EXT, n)], three, precision=lax.Precision.HIGHEST, preferred_element_type=F32
            )
            field[r] = keep * X[2, r] + shrink * smooth[:, :rows]
            TV[r] = keep * second(X[1, r], X[3, r], X[2, r]) + shrink * smooth[:, rows:2 * rows]
            T2V[r] = (
                keep * second2(X[0, r], X[1, r], X[2, r], X[3, r], X[4, r])
                + shrink * smooth[:, 2 * rows:]
            )

    sizes = (32, 16)

    def stage_place(stage):
        return (x * 8 + k, z)[stage]

    def stage_device(stage, place):
        if stage == 0:
            return zl * 8 + lax.rem(place, 8), (place // 8) * 2 + zh
        return on_z(place, x)

    def dot_slots(stage):
        return (dots_a, dots_b)[stage]

    def dot_copy(p, stage, d):
        size, mine, slots = sizes[stage], stage_place(stage), dot_slots(stage)
        if stage == 0:
            other = lax.rem(x + d // 8, 4) * 8 + lax.rem(k + d % 8, 8)
        else:
            other = lax.rem(mine + d, size)
        t, l = stage_device(stage, other)
        slot = slots.at[p, mine]
        return remote(slot, slot, ds_.at[p, stage], dr.at[p, stage], t, l)

    def dot_all(p, stage):
        some = dot_slots(stage).at[p, pl.ds(0, sizes[stage] - 1)]
        return remote(some, some, ds_.at[p, stage], dr.at[p, stage], tm, lon)

    steps = (
        [8 * dx + dk for dx in (2, 1, 3, 0) for dk in (4, 3, 5, 2, 6, 1, 7, 0)][:-1],
        [8, 7, 9, 6, 10, 5, 11, 4, 12, 3, 13, 2, 14, 1, 15],
    )

    def dot_send(p, stage, line):
        dot_slots(stage)[p, stage_place(stage)] = line
        for d in steps[stage]:
            dot_copy(p, stage, d).start()

    def dot_take(p, stage):
        dot_all(p, stage).wait_recv()
        total = dot_slots(stage)[p, 0]
        for i in range(1, sizes[stage]):
            total = total + dot_slots(stage)[p, i]
        return total

    def dot_done(p):
        for stage in range(2):
            dot_all(p, stage).wait_send()

    low = lane[:1] < MW

    def pack(slope, curve):
        return jnp.where(low, slope + pltpu.roll(slope, MW, axis=1), curve + pltpu.roll(curve, MW, axis=1))

    def ratio(line):
        slope = jnp.sum(jnp.where(low, line, 0.0), axis=1, keepdims=True)
        return slope / jnp.sum(jnp.where(low, 0.0, line), axis=1, keepdims=True)

    with jax.named_scope("transform zero"):
        transform_start(0)
    with jax.named_scope("edges one send"):
        edge_send(1, G)
    with jax.named_scope("cross zero"):
        transform_cross(0)
    with jax.named_scope("rim one send"):
        rim_send(1, G)
    with jax.named_scope("halo one send"):
        halo_send(1, G)
    with jax.named_scope("spread zero"):
        transform_spread(0)
    with jax.named_scope("hand on one"):
        halo_hand(1, G)
    with jax.named_scope("rim one wait"):
        rim_take(1, G)
    with jax.named_scope("halo one wait"):
        halo_wait(1, G)
    with jax.named_scope("finish zero"):
        transform_finish(0)
    with jax.named_scope("filter zero"):
        filtered(0, G, V0)
    acc = [jnp.zeros((1, rows), F32), jnp.zeros((1, rows), F32)]

    def emit_u(s, n, u):
        l, r = pl.ds(s - OFF, n), pl.ds(s, n)
        v = V0[r]
        u = W[l] * v + u
        U[2, r] = u
        padded[l] = u
        acc[0] = acc[0] + jnp.sum(G[2, r] * v, axis=0, keepdims=True)
        acc[1] = acc[1] + jnp.sum(v * u, axis=0, keepdims=True)

    with jax.named_scope("operator one"):
        operator(V0, emit_u)

    with jax.named_scope("transform one"):
        transform_start(1)
    with jax.named_scope("edges two send"):
        dot_send(0, 0, pack(*acc))
        edge_send(2, U)
    with jax.named_scope("cross one"):
        transform_cross(1)
    with jax.named_scope("rim two send"):
        rim_send(2, U)
    with jax.named_scope("halo two send"):
        halo_send(2, U)
    with jax.named_scope("sums zero"):
        dot_send(0, 1, dot_take(0, 0))
    with jax.named_scope("spread one"):
        transform_spread(1)
    with jax.named_scope("hand on two"):
        halo_hand(2, U)
    with jax.named_scope("rim two wait"):
        rim_take(2, U)
    with jax.named_scope("step zero"):
        step0 = ratio(dot_take(0, 1))
    with jax.named_scope("halo two wait"):
        halo_wait(2, U)
    with jax.named_scope("finish one"):
        transform_finish(1)
    with jax.named_scope("filter one"):
        filtered(1, U, V)
    acc[0] = acc[1] = jnp.zeros((1, rows), F32)

    def emit_last(s, n, u1):
        l, r = pl.ds(s - OFF, n), pl.ds(s, n)
        v1, v0, u0 = V[r], V0[r], U[2, r]
        u1 = W[l] * v1 + u1
        search = v0 - step0 * v1
        curved = u0 - step0 * u1
        out_c[0, l] = curved
        out_s[0, l] = search
        gradient = G[2, r] - step0 * u0
        acc[0] = acc[0] + jnp.sum(gradient * search, axis=0, keepdims=True)
        acc[1] = acc[1] + jnp.sum(search * curved, axis=0, keepdims=True)
        out_g[0, l] = gradient
        out_a[0, l] = E[2, r] - step0 * v0

    with jax.named_scope("operator two"):
        operator(V, emit_last)
    with jax.named_scope("sums one a"):
        dot_send(1, 0, pack(*acc))
    with jax.named_scope("sums one b"):
        dot_send(1, 1, dot_take(1, 0))
    for p, X in enumerate((E, G, U)):
        halo_done(p, X)
        edge_done(p)
    for p in range(2):
        transform_done(p)
    dot_done(0)
    with jax.named_scope("sums one c"):
        out_step[...] = jnp.broadcast_to(ratio(dot_take(1, 1)), out_step.shape)
    with jax.named_scope("drain"):
        dot_done(1)


def on_device(NT, NL, first, obs, track, land, bw):
    _, N, rows = first.shape
    forward, inverse, row = tables(NL, N, rows)
    plane = pltpu.VMEM((N + 32, rows), F32)
    planes = pltpu.VMEM((5, N + 32, rows), F32)
    flat = pltpu.VMEM((N, rows), F32)
    whole = pltpu.VMEM((N, rows), jnp.int32)
    dma = pltpu.SemaphoreType.DMA
    hbm = pl.BlockSpec(memory_space=pltpu.HBM)
    surface, search, gradient, curved, step = pl.pallas_call(
        functools.partial(kernel, NT, N),
        out_shape=[pltpu.VMEM(first.shape, F32)] * 4 + [pltpu.VMEM((1, rows), F32)],
        in_specs=[hbm] * 8,
        out_specs=[pl.BlockSpec(memory_space=pltpu.VMEM)] * 5,
        scratch_shapes=[
            pltpu.VMEM(row.shape, F32), planes, planes, planes,
            plane, flat, flat, whole, whole,
            pltpu.VMEM(forward.shape[1:], F32), pltpu.VMEM(inverse.shape[1:], F32),
            plane, plane, plane, plane, plane,
            pltpu.VMEM((forward.shape[2], rows), F32),
            pltpu.VMEM((2, MW, rows), F32),
            pltpu.VMEM((2, 4, 16, rows), F32),
            pltpu.VMEM((2, 2, 16, rows), F32),
            pltpu.VMEM((2, 16, rows), F32),
            pltpu.VMEM((2, 5, MW, rows), F32),
            pltpu.VMEM((2, 32, 1, rows), F32),
            pltpu.VMEM((2, 16, 1, rows), F32),
            pltpu.VMEM((3, 2, rows), F32),
            pltpu.VMEM((3, 2, 2, rows), F32),
            pltpu.VMEM((3, 2, 4, rows), F32),
            pltpu.VMEM((3, 2, 4, rows), F32),
            pltpu.SemaphoreType.REGULAR, dma((8,)), dma((3, 4)), dma((3, 4)),
            dma((3, 2)), dma((3, 2)), dma((3, 2)), dma((3, 2)),
            dma((2,)), dma((2,)), dma((2,)), dma((2,)), dma((2, 5)), dma((2, 5)),
            dma((2, 2)), dma((2, 2)),
        ],
        compiler_params=pltpu.CompilerParams(
            collective_id=0, has_side_effects=True, vmem_limit_bytes=56 * 1024 * 1024
        ),
    )(first, obs, track, land, bw, forward, inverse, row)
    return surface - step[None] * search, gradient - step[None] * curved


def solution(mesh):
    in_specs = (
        P("tm", "lon", None),
        P("tm", "lon", None),
        P("tm", "lon", None),
        P("lon", None),
        P("lon", None),
    )
    out_specs = (P("tm", "lon", None), P("tm", "lon", None))
    return jax.shard_map(
        functools.partial(on_device, mesh.shape["tm"], mesh.shape["lon"]),
        mesh=mesh, in_specs=in_specs, out_specs=out_specs, check_vma=False,
    )
```

```python
import functools

import jax
import jax.numpy as jnp
import numpy as np
from jax import lax
from jax.experimental import pallas as pl
from jax.experimental.pallas import tpu as pltpu
from jax.sharding import PartitionSpec as P

CAP = 64
MW = 64
MESH = pl.DeviceIdType.MESH
OFF = 16
EXT = 8
F32 = jnp.float32


def tables(segments, length, rows):
    circle = segments * length
    harmonic = np.arange(MW)
    w = np.where(harmonic == 0, 1.0 / circle, 2.0 / circle)
    padded = -(-length // 128) * 128
    forward = np.zeros((segments, 2 * MW, padded), np.float32)
    inverse = np.zeros((segments, length + 16, 2 * MW), np.float32)
    for s in range(segments):
        a = 2 * np.pi * ((np.arange(length) + s * length)[:, None] * harmonic % circle) / circle
        forward[s, :MW, :length] = np.cos(a).T
        forward[s, MW:, :length] = np.sin(a).T
        a = 2 * np.pi * ((np.arange(length + 16) - 8 + s * length)[:, None] * harmonic % circle) / circle
        inverse[s] = np.concatenate([w * np.cos(a), w * np.sin(a)], axis=1)
    phi = (90.0 - (rows - np.arange(rows) - 0.5) * 0.125) * (np.pi / 180.0)
    bend = 1.0 / (np.cos(phi) + 0.5) ** 2
    shrink = np.zeros(rows)
    shrink[rows - CAP:] = 0.9 * (np.arange(CAP) + 1.0) / CAP
    row = np.zeros((8, rows), np.float32)
    row[0] = bend
    row[1] = -2.0 * (bend + 1.0)
    row[2] = shrink
    row[3] = 1.0 - shrink
    return forward, inverse, row


def kernel(
    NT, N, first_ref, obs_ref, track_ref, land_ref, bw_ref, fwd_ref, inv_ref, row_hbm,
    out_a, out_s, out_g, out_c, out_step,
    row_ref, E, G, U, B, W, obs, track, land, fwd, inv, V, TV, T2V, Y, V0, LV0, padded, amp, rs_buf, quarter,
    z_buf, AT, dots_a, dots_b, ts, tr, ls, lr,
    hello, lsem, hs, hr, es, er, rs_, rr, xs, xr, zs, zr, ats, atr, ds_, dr,
):
    tm = lax.axis_index("tm")
    lon = lax.axis_index("lon")
    x, zh = lon // 2, lon % 2
    zl, k = tm // 8, tm % 8
    rows = 128

    def inside(t):
        return (t >= 0) & (t < NT)

    def when_t(dt, fn):
        if dt == 0:
            fn()
        else:
            pl.when(inside(tm + dt))(fn)

    def lon_at(d):
        return lax.rem(lon + d + 8, 8)

    own = pl.ds(OFF, N)
    loads = [
        pltpu.make_async_copy(first_ref.at[0], E.at[2, own], lsem.at[0]),
        pltpu.make_async_copy(bw_ref, B.at[own], lsem.at[1]),
        pltpu.make_async_copy(obs_ref.at[0], obs, lsem.at[2]),
        pltpu.make_async_copy(track_ref.at[0], track, lsem.at[3]),
        pltpu.make_async_copy(land_ref, land, lsem.at[4]),
        pltpu.make_async_copy(fwd_ref.at[lon], fwd, lsem.at[5]),
        pltpu.make_async_copy(inv_ref.at[lon], inv, lsem.at[6]),
        pltpu.make_async_copy(row_hbm, row_ref, lsem.at[7]),
    ]
    loads[0].start()
    loads[7].start()

    barrier = pltpu.get_barrier_semaphore()

    def greet(t, l, sem=barrier):
        pl.semaphore_signal(sem, inc=1, device_id={"tm": t, "lon": l}, device_id_type=MESH)

    z = zh * 8 + zl

    def on_z(place, xx):
        place = lax.rem(place + 16, 16)
        return lax.rem(place, 8) * 8 + k, lax.rem(xx + 4, 4) * 2 + place // 8

    fours = [(dz, dx) for dz in (4, -4) for dx in (0, 1, -1)]
    for dz, dx in fours:
        greet(*on_z(z + dz, x + dx))
    for dz in (3, -3, 2, -2, 1, -1):
        greet(*on_z(z + dz, x))
    for d in range(1, 8):
        greet(zl * 8 + lax.rem(k + d, 8), lon)
    for d in range(1, 4):
        greet(tm, lon_at(2 * d))
    count = jnp.int32(len(fours) + 6 + 7 + 3)
    for dt in (-2, -1, 1, 2):
        when_t(dt, lambda dt=dt: greet(tm + dt, lon))
        count = count + jnp.where(inside(tm + dt), 1, 0)
    for c in loads[1:7]:
        c.start()

    for dt in (-2, -1, 1, 2):

        @pl.when(jnp.logical_not(inside(tm + dt)))
        def _(dt=dt):
            for X in (E, G, U):
                X[2 + dt] = jnp.zeros(X.shape[1:], F32)
            for p in range(2):
                AT[p, 2 + dt] = jnp.zeros(AT.shape[2:], F32)
            if abs(dt) == 1:
                for p in range(3):
                    tr[p, (dt + 1) // 2] = jnp.zeros(tr.shape[2:], F32)

    padded[pl.ds(N, padded.shape[0] - N)] = jnp.zeros((padded.shape[0] - N, rows), F32)

    with jax.named_scope("entry barrier"):
        pl.semaphore_wait(barrier, count)
    for dz, dx in fours:
        greet(*on_z(z + dz, x + dx), sem=hello)

    def remote(src, dst, send, recv, t, l):
        return pltpu.make_async_remote_copy(
            src_ref=src, dst_ref=dst, send_sem=send, recv_sem=recv,
            device_id={"tm": t, "lon": l}, device_id_type=MESH,
        )

    side = 1 - 2 * lax.rem(tm, 2)
    send_days = (-side, 2 * side, side)
    recv_days = (-side, -2 * side, side, 2 * side)

    def plane_copy(p, X, i):
        dt = send_days[i]
        return remote(X.at[2, own], X.at[2 - dt, own], hs.at[p, i], hr.at[p, i], tm + dt, lon)

    def hand_copy(p, X):
        return remote(X.at[2 - side, own], X.at[2 - 2 * side, own], hs.at[p, 3], hr.at[p, 3], tm + side, lon)

    def plane_recv(p, X, i):
        return remote(X.at[2, own], X.at[2 + recv_days[i], own], hs.at[p, i], hr.at[p, i], tm, lon)

    def halo_send(p, X):
        for i in range(3):
            pl.when(inside(tm + send_days[i]))(lambda i=i: plane_copy(p, X, i).start())

    def halo_hand(p, X):
        @pl.when(inside(tm - side))
        def _():
            plane_recv(p, X, 0).wait_recv()
            hand_copy(p, X).start()

    def halo_wait(p, X):
        for i in (1, 2, 3):
            pl.when(inside(tm + recv_days[i]))(lambda i=i: plane_recv(p, X, i).wait_recv())

    def halo_done(p, X):
        for i in range(3):
            pl.when(inside(tm + send_days[i]))(lambda i=i: plane_copy(p, X, i).wait_send())
        pl.when(inside(tm - side))(lambda: hand_copy(p, X).wait_send())

    first_row, last_row = OFF, OFF + N - 1

    def edge_copy(p, i):
        return remote(ts.at[p], tr.at[p, i], es.at[p, i], er.at[p, i], tm + (1, -1)[i], lon)

    def edge_send(p, X):
        ts[p, 0:1] = X[2, first_row:first_row + 1]
        ts[p, 1:2] = X[2, last_row:last_row + 1]
        for i, dt in enumerate((1, -1)):
            when_t(dt, lambda i=i: edge_copy(p, i).start())

    def rim_copy(p, i):
        return remote(ls.at[p, i], lr.at[p, i], rs_.at[p, i], rr.at[p, i], tm, lon_at((1, -1)[i]))

    def rim_send(p, X):
        for i, dt in enumerate((1, -1)):
            when_t(-dt, lambda i=i: edge_copy(p, i).wait_recv())
        bent = tr[p, 0] + tr[p, 1] - 2.0 * ts[p]
        ls[p, 0, 0:1] = X[2, last_row:last_row + 1]
        ls[p, 0, 1:2] = X[2, last_row - 1:last_row]
        ls[p, 0, 2:3] = bent[1:2]
        ls[p, 0, 3:4] = B[last_row:last_row + 1]
        ls[p, 1, 0:1] = X[2, first_row:first_row + 1]
        ls[p, 1, 1:2] = X[2, first_row + 1:first_row + 2]
        ls[p, 1, 2:3] = bent[0:1]
        ls[p, 1, 3:4] = B[first_row:first_row + 1]
        for i in range(2):
            rim_copy(p, i).start()

    def rim_take(p, X):
        for i in range(2):
            rim_copy(p, i).wait_recv()
        for i, (near, far) in enumerate(((first_row - 1, first_row - 2), (last_row + 1, last_row + 2))):
            X[2, near:near + 1] = lr[p, i, 0:1]
            X[2, far:far + 1] = lr[p, i, 1:2]
            X[1, near:near + 1] = lr[p, i, 2:3] + 2.0 * lr[p, i, 0:1]
            X[3, near:near + 1] = jnp.zeros((1, rows), F32)
            if p == 0:
                B[near:near + 1] = lr[p, i, 3:4]

    def edge_done(p):
        for i, dt in enumerate((1, -1)):
            when_t(dt, lambda i=i: edge_copy(p, i).wait_send())
            rim_copy(p, i).wait_send()

    with jax.named_scope("guess edges"):
        loads[0].wait()
        edge_send(0, E)
        halo_send(0, E)
    loads[1].wait()
    with jax.named_scope("far hello"):
        pl.semaphore_wait(hello, len(fours))
    with jax.named_scope("guess rim"):
        rim_send(0, E)
    with jax.named_scope("guess hand on"):
        halo_hand(0, E)

    lane = lax.broadcasted_iota(jnp.int32, (8, rows), 1)
    first_lane, last_lane = lane[:1] == 0, lane[:1] == rows - 1
    loads[7].wait()
    bend = row_ref[0:1]
    centre = row_ref[1:2]
    shrink = row_ref[2:3]
    keep = row_ref[3:4]

    def flat(ref, start, n):
        v = ref[pl.ds(start, n)]
        up, down = ref[pl.ds(start + 1, n)], ref[pl.ds(start - 1, n)]
        lo = jnp.where(first_lane, 0.0, pltpu.roll(v, 1, axis=1))
        hi = jnp.where(last_lane, 0.0, pltpu.roll(v, rows - 1, axis=1))
        return bend * (up + down) + (lo + hi) + centre * v

    own_chunks = [(OFF + c, 72) for c in range(0, N, 72)]
    ext_chunks = [(EXT, 8)] + own_chunks + [(OFF + N, 8)]
    centre_t2 = jnp.where((tm == 0) | (tm == NT - 1), 5.0, 6.0).astype(F32)

    def second(a, b, c):
        return a + b - 2.0 * c

    def second2(a, b, c, d, e):
        return a + e - 4.0 * (b + d) + centre_t2 * c

    def flatten(field):
        for s, n in ext_chunks:
            Y[pl.ds(s, n)] = flat(field, s, n)

    def once(emit=None):
        for s, n in ext_chunks:
            full = TV[pl.ds(s, n)] + Y[pl.ds(s, n)]
            Y[pl.ds(s, n)] = B[pl.ds(s, n)] * full
            if emit is not None and OFF <= s < OFF + N:
                emit(s, n, full)

    def twice(emit):
        for s, n in own_chunks:
            emit(s, n, B[pl.ds(s, n)] * (T2V[pl.ds(s, n)] + flat(TV, s, n)) + flat(Y, s, n))

    with jax.named_scope("weights"):
        for c in loads[2:5]:
            c.wait()
        W[...] = track[...].astype(F32) * (1.0 - land[...].astype(F32))

    with jax.named_scope("guess halo wait"):
        halo_wait(0, E)
    with jax.named_scope("guess rim wait"):
        rim_take(0, E)
    for s, n in ext_chunks:
        r = pl.ds(s, n)
        TV[r] = second(E[1, r], E[3, r], E[2, r])
    for s, n in own_chunks:
        r = pl.ds(s, n)
        T2V[r] = second2(E[0, r], E[1, r], E[2, r], E[3, r], E[4, r])

    def emit_g(s, n, u):
        l = pl.ds(s - OFF, n)
        g = W[l] * (E[2, pl.ds(s, n)] - obs[l]) + u
        G[2, pl.ds(s, n)] = g
        padded[l] = g

    with jax.named_scope("first operator"):
        flatten(E.at[2])
        once()
        twice(emit_g)
    for c in loads[5:7]:
        c.wait()

    half = lax.broadcasted_iota(jnp.int32, (MW, rows), 1) < MW

    def rs_copy(p, d):
        q = lax.rem(x + d, 4)
        return remote(amp.at[p, pl.ds(16 * q, 16)], rs_buf.at[p, d], xs.at[p], xr.at[p], tm, q * 2 + zh)

    def rs_all(p):
        return remote(rs_buf.at[p, pl.ds(1, 3)], rs_buf.at[p, pl.ds(1, 3)], xs.at[p], xr.at[p], tm, lon)

    def z_copy(p):
        return remote(quarter.at[p, 0], z_buf.at[p], zs.at[p], zr.at[p], tm, lon + 1 - 2 * zh)

    days = (2, -2, 1, -1, 0)

    def at_copy(p, i, d):
        dt = days[i]
        xx = lax.rem(x + d, 4)
        return remote(
            quarter.at[p, 1], AT.at[p, 2 - dt, pl.ds(16 * x, 16)], ats.at[p, i], atr.at[p, i], tm + dt, xx * 2 + zh
        )

    def at_all(p, i):
        some = AT.at[p, 2 - days[i], pl.ds(0, MW if days[i] else MW - 16)]
        return remote(some, some, ats.at[p, i], atr.at[p, i], tm, lon)

    def transform_start(p):
        part = lax.dot(fwd[...], padded[...], precision=lax.Precision.HIGH, preferred_element_type=F32)
        amp[p] = jnp.where(half, pltpu.roll(part[:MW], MW, axis=1), part[MW:])
        for d in (2, 1, 3):
            rs_copy(p, d).start()

    def transform_cross(p):
        total = amp[p, pl.ds(16 * x, 16)]
        rs_all(p).wait_recv()
        for d in (1, 2, 3):
            total = total + rs_buf[p, d]
        quarter[p, 0] = total
        z_copy(p).start()

    def transform_spread(p):
        z_copy(p).wait_recv()
        total = quarter[p, 0] + z_buf[p]
        quarter[p, 1] = total
        for i, dt in enumerate(days):
            for d in (2, 1, 3, 0) if dt else (2, 1, 3):
                when_t(dt, lambda i=i, d=d: at_copy(p, i, d).start())
        AT[p, 2, pl.ds(16 * x, 16)] = total

    def transform_finish(p, some):
        for i, dt in enumerate(days):
            if dt in some:
                when_t(-dt, lambda i=i: at_all(p, i).wait_recv())

    def transform_done(p):
        rs_all(p).wait_send()
        z_copy(p).wait_send()
        for i, dt in enumerate(days):
            when_t(dt, lambda i=i: at_all(p, i).wait_send())

    def stack(a):
        return jnp.concatenate([pltpu.roll(a, MW, axis=1), a], axis=0) * shrink

    def synthesis(s, n, amplitudes):
        return lax.dot(
            inv[pl.ds(s - EXT, n)], amplitudes, precision=lax.Precision.HIGH, preferred_element_type=F32
        )

    def filter_local(X, field):
        for s, n in ext_chunks:
            r = pl.ds(s, n)
            field[r] = keep * X[2, r]
            TV[r] = keep * second(X[1, r], X[3, r], X[2, r])
            T2V[r] = keep * second2(X[0, r], X[1, r], X[2, r], X[3, r], X[4, r])

    def filter_own(p, field):
        amplitudes = stack(AT[p, 2])
        for s, n in ext_chunks:
            field[pl.ds(s, n)] += synthesis(s, n, amplitudes)
        flatten(field)

    def filter_days(p):
        a = [AT[p, i] for i in range(5)]
        amplitudes = jnp.concatenate([stack(second(a[1], a[3], a[2])), stack(second2(*a))], axis=1)
        for s, n in ext_chunks:
            smooth = synthesis(s, n, amplitudes)
            TV[pl.ds(s, n)] += smooth[:, :rows]
            T2V[pl.ds(s, n)] += smooth[:, rows:]

    sizes = (32, 16)

    def stage_place(stage):
        return (x * 8 + k, z)[stage]

    def stage_device(stage, place):
        if stage == 0:
            return zl * 8 + lax.rem(place, 8), (place // 8) * 2 + zh
        return on_z(place, x)

    def dot_slots(stage):
        return (dots_a, dots_b)[stage]

    def dot_copy(p, stage, d):
        size, mine, slots = sizes[stage], stage_place(stage), dot_slots(stage)
        if stage == 0:
            other = lax.rem(x + d // 8, 4) * 8 + lax.rem(k + d % 8, 8)
        else:
            other = lax.rem(mine + d, size)
        t, l = stage_device(stage, other)
        slot = slots.at[p, mine]
        return remote(slot, slot, ds_.at[p, stage], dr.at[p, stage], t, l)

    def dot_all(p, stage):
        some = dot_slots(stage).at[p, pl.ds(0, sizes[stage] - 1)]
        return remote(some, some, ds_.at[p, stage], dr.at[p, stage], tm, lon)

    steps = (
        [8 * dx + dk for dx in (2, 1, 3, 0) for dk in (4, 3, 5, 2, 6, 1, 7, 0)][:-1],
        [8, 7, 9, 6, 10, 5, 11, 4, 12, 3, 13, 2, 14, 1, 15],
    )

    def dot_send(p, stage, line):
        dot_slots(stage)[p, stage_place(stage)] = line
        for d in steps[stage]:
            dot_copy(p, stage, d).start()

    def dot_take(p, stage):
        dot_all(p, stage).wait_recv()
        total = dot_slots(stage)[p, 0]
        for i in range(1, sizes[stage]):
            total = total + dot_slots(stage)[p, i]
        return total

    def dot_done(p):
        for stage in range(2):
            dot_all(p, stage).wait_send()

    low = lane[:1] < MW

    def pack(slope, curve):
        return jnp.where(low, slope + pltpu.roll(slope, MW, axis=1), curve + pltpu.roll(curve, MW, axis=1))

    def ratio(line):
        slope = jnp.sum(jnp.where(low, line, 0.0), axis=1, keepdims=True)
        return slope / jnp.sum(jnp.where(low, 0.0, line), axis=1, keepdims=True)

    with jax.named_scope("transform zero"):
        transform_start(0)
    with jax.named_scope("edges one send"):
        edge_send(1, G)
    with jax.named_scope("cross zero"):
        transform_cross(0)
    with jax.named_scope("rim one send"):
        rim_send(1, G)
    with jax.named_scope("halo one send"):
        halo_send(1, G)
    with jax.named_scope("spread zero"):
        transform_spread(0)
    with jax.named_scope("hand on one"):
        halo_hand(1, G)
    with jax.named_scope("rim one wait"):
        rim_take(1, G)
    with jax.named_scope("halo one wait"):
        halo_wait(1, G)
    with jax.named_scope("filter zero local"):
        filter_local(G, V0)
    with jax.named_scope("finish zero"):
        transform_finish(0, (0,))
    with jax.named_scope("filter zero own"):
        filter_own(0, V0)
    with jax.named_scope("finish zero days"):
        transform_finish(0, (1, -1, 2, -2))
    with jax.named_scope("filter zero days"):
        filter_days(0)
    acc = [jnp.zeros((1, rows), F32), jnp.zeros((1, rows), F32)]

    def emit_first(s, n, full):
        LV0[pl.ds(s - OFF, n)] = full

    def emit_u(s, n, u):
        l, r = pl.ds(s - OFF, n), pl.ds(s, n)
        v = V0[r]
        u = W[l] * v + u
        U[2, r] = u
        padded[l] = u
        acc[0] = acc[0] + jnp.sum(G[2, r] * v, axis=0, keepdims=True)
        acc[1] = acc[1] + jnp.sum(v * u, axis=0, keepdims=True)

    with jax.named_scope("operator one"):
        once(emit_first)
        twice(emit_u)

    with jax.named_scope("transform one"):
        transform_start(1)
    with jax.named_scope("edges two send"):
        dot_send(0, 0, pack(*acc))
        edge_send(2, U)
    with jax.named_scope("cross one"):
        transform_cross(1)
    with jax.named_scope("rim two send"):
        rim_send(2, U)
    with jax.named_scope("halo two send"):
        halo_send(2, U)
    with jax.named_scope("sums zero"):
        dot_send(0, 1, dot_take(0, 0))
    with jax.named_scope("spread one"):
        transform_spread(1)
    with jax.named_scope("hand on two"):
        halo_hand(2, U)
    with jax.named_scope("rim two wait"):
        rim_take(2, U)
    with jax.named_scope("halo two wait"):
        halo_wait(2, U)
    with jax.named_scope("filter one local"):
        filter_local(U, V)
    with jax.named_scope("finish one"):
        transform_finish(1, (0,))
    with jax.named_scope("filter one own"):
        filter_own(1, V)
    with jax.named_scope("step zero"):
        step0 = ratio(dot_take(0, 1))
    with jax.named_scope("finish one days"):
        transform_finish(1, (1, -1, 2, -2))
    with jax.named_scope("filter one days"):
        filter_days(1)
    acc[0] = acc[1] = jnp.zeros((1, rows), F32)

    def emit_sums(s, n, full):
        l, r = pl.ds(s - OFF, n), pl.ds(s, n)
        search = V0[r] - step0 * V[r]
        gradient = G[2, r] - step0 * U[2, r]
        bent = LV0[l] - step0 * full
        acc[0] = acc[0] + jnp.sum(gradient * search, axis=0, keepdims=True)
        acc[1] = acc[1] + jnp.sum(W[l] * (search * search) + B[r] * (bent * bent), axis=0, keepdims=True)
        out_s[0, l] = search
        out_g[0, l] = gradient

    with jax.named_scope("operator two once"):
        once(emit_sums)
    with jax.named_scope("sums one a"):
        dot_send(1, 0, pack(*acc))

    def emit_last(s, n, u1):
        l, r = pl.ds(s - OFF, n), pl.ds(s, n)
        out_c[0, l] = U[2, r] - step0 * (W[l] * V[r] + u1)
        out_a[0, l] = E[2, r] - step0 * V0[r]

    with jax.named_scope("operator two twice"):
        twice(emit_last)
    with jax.named_scope("sums one b"):
        dot_send(1, 1, dot_take(1, 0))
    for p, X in enumerate((E, G, U)):
        halo_done(p, X)
        edge_done(p)
    for p in range(2):
        transform_done(p)
    dot_done(0)
    with jax.named_scope("sums one c"):
        out_step[...] = jnp.broadcast_to(ratio(dot_take(1, 1)), out_step.shape)
    with jax.named_scope("drain"):
        dot_done(1)


def on_device(NT, NL, first, obs, track, land, bw):
    _, N, rows = first.shape
    forward, inverse, row = tables(NL, N, rows)
    plane = pltpu.VMEM((N + 32, rows), F32)
    planes = pltpu.VMEM((5, N + 32, rows), F32)
    flat = pltpu.VMEM((N, rows), F32)
    whole = pltpu.VMEM((N, rows), jnp.int32)
    dma = pltpu.SemaphoreType.DMA
    hbm = pl.BlockSpec(memory_space=pltpu.HBM)
    surface, search, gradient, curved, step = pl.pallas_call(
        functools.partial(kernel, NT, N),
        out_shape=[pltpu.VMEM(first.shape, F32)] * 4 + [pltpu.VMEM((1, rows), F32)],
        in_specs=[hbm] * 8,
        out_specs=[pl.BlockSpec(memory_space=pltpu.VMEM)] * 5,
        scratch_shapes=[
            pltpu.VMEM(row.shape, F32), planes, planes, planes,
            plane, flat, flat, whole, whole,
            pltpu.VMEM(forward.shape[1:], F32), pltpu.VMEM(inverse.shape[1:], F32),
            plane, plane, plane, plane, plane, flat,
            pltpu.VMEM((forward.shape[2], rows), F32),
            pltpu.VMEM((2, MW, rows), F32),
            pltpu.VMEM((2, 4, 16, rows), F32),
            pltpu.VMEM((2, 2, 16, rows), F32),
            pltpu.VMEM((2, 16, rows), F32),
            pltpu.VMEM((2, 5, MW, rows), F32),
            pltpu.VMEM((2, 32, 1, rows), F32),
            pltpu.VMEM((2, 16, 1, rows), F32),
            pltpu.VMEM((3, 2, rows), F32),
            pltpu.VMEM((3, 2, 2, rows), F32),
            pltpu.VMEM((3, 2, 4, rows), F32),
            pltpu.VMEM((3, 2, 4, rows), F32),
            pltpu.SemaphoreType.REGULAR, dma((8,)), dma((3, 4)), dma((3, 4)),
            dma((3, 2)), dma((3, 2)), dma((3, 2)), dma((3, 2)),
            dma((2,)), dma((2,)), dma((2,)), dma((2,)), dma((2, 5)), dma((2, 5)),
            dma((2, 2)), dma((2, 2)),
        ],
        compiler_params=pltpu.CompilerParams(
            collective_id=0, has_side_effects=True, vmem_limit_bytes=56 * 1024 * 1024
        ),
    )(first, obs, track, land, bw, forward, inverse, row)
    return surface - step[None] * search, gradient - step[None] * curved


def solution(mesh):
    in_specs = (
        P("tm", "lon", None),
        P("tm", "lon", None),
        P("tm", "lon", None),
        P("lon", None),
        P("lon", None),
    )
    out_specs = (P("tm", "lon", None), P("tm", "lon", None))
    return jax.shard_map(
        functools.partial(on_device, mesh.shape["tm"], mesh.shape["lon"]),
        mesh=mesh, in_specs=in_specs, out_specs=out_specs, check_vma=False,
    )
```

```python
import functools

import jax
import jax.numpy as jnp
import numpy as np
from jax import lax
from jax.experimental import pallas as pl
from jax.experimental.pallas import tpu as pltpu
from jax.sharding import PartitionSpec as P

CAP = 64
MW = 64
MESH = pl.DeviceIdType.MESH
OFF = 16
EXT = 8
F32 = jnp.float32


def tables(segments, length, rows):
    circle = segments * length
    harmonic = np.arange(MW)
    w = np.where(harmonic == 0, 1.0 / circle, 2.0 / circle)
    padded = -(-length // 128) * 128
    forward = np.zeros((segments, 2 * MW, padded), np.float32)
    inverse = np.zeros((segments, length + 16, 2 * MW), np.float32)
    for s in range(segments):
        a = 2 * np.pi * ((np.arange(length) + s * length)[:, None] * harmonic % circle) / circle
        forward[s, :MW, :length] = np.cos(a).T
        forward[s, MW:, :length] = np.sin(a).T
        a = 2 * np.pi * ((np.arange(length + 16) - 8 + s * length)[:, None] * harmonic % circle) / circle
        inverse[s] = np.concatenate([w * np.cos(a), w * np.sin(a)], axis=1)
    phi = (90.0 - (rows - np.arange(rows) - 0.5) * 0.125) * (np.pi / 180.0)
    bend = 1.0 / (np.cos(phi) + 0.5) ** 2
    shrink = np.zeros(rows)
    shrink[rows - CAP:] = 0.9 * (np.arange(CAP) + 1.0) / CAP
    row = np.zeros((8, rows), np.float32)
    row[0] = bend
    row[1] = -2.0 * (bend + 1.0)
    row[2] = shrink
    row[3] = 1.0 - shrink
    seams = np.zeros((4, 32, 128), np.float32)
    for i, offset in enumerate((0, 1, -1, -2)):
        place = (np.arange(segments) + 1) * length + offset
        a = 2 * np.pi * (place[None, :] * harmonic[:, None] % circle) / circle
        for q in range(4):
            seams[q, :16, 8 * i:8 * i + 8] = np.cos(a[16 * q:16 * q + 16])
            seams[q, 16:, 8 * i:8 * i + 8] = np.sin(a[16 * q:16 * q + 16])
    return forward, inverse, row, seams


def kernel(
    NT, N, first_ref, obs_ref, track_ref, land_ref, bw_ref, fwd_ref, inv_ref, row_hbm, seams_hbm,
    out_a, out_s, out_g, out_c, out_step,
    row_ref, E, G, U, B, W, obs, track, land, fwd, inv, V, TV, T2V, Y, V0, LV0, padded, seams, seam_rows, seam_amp, ED, amp, rs_buf, quarter,
    z_buf, AT, dots_a, dots_b, ts, tr, ls, lr,
    hello, hello2, sems, lsem, hs, hr, es, er, rs_, rr, xs, xr, zs, zr, ats, atr, ds_, dr,
):
    tm = lax.axis_index("tm")
    lon = lax.axis_index("lon")
    x, zh = lon // 2, lon % 2
    zl, k = tm // 8, tm % 8
    rows = 128

    def inside(t):
        return (t >= 0) & (t < NT)

    def when_t(dt, fn):
        if dt == 0:
            fn()
        else:
            pl.when(inside(tm + dt))(fn)

    def lon_at(d):
        return lax.rem(lon + d + 8, 8)

    own = pl.ds(OFF, N)
    loads = [
        pltpu.make_async_copy(first_ref.at[0], E.at[2, own], lsem.at[0]),
        pltpu.make_async_copy(bw_ref, B.at[own], lsem.at[1]),
        pltpu.make_async_copy(obs_ref.at[0], obs, lsem.at[2]),
        pltpu.make_async_copy(track_ref.at[0], track, lsem.at[3]),
        pltpu.make_async_copy(land_ref, land, lsem.at[4]),
        pltpu.make_async_copy(fwd_ref.at[lon], fwd, lsem.at[5]),
        pltpu.make_async_copy(inv_ref.at[lon], inv, lsem.at[6]),
        pltpu.make_async_copy(row_hbm, row_ref, lsem.at[7]),
        pltpu.make_async_copy(seams_hbm.at[x], seams, lsem.at[8]),
    ]
    loads[0].start()
    loads[7].start()

    barrier = pltpu.get_barrier_semaphore()

    def greet(t, l, sem=barrier):
        pl.semaphore_signal(sem, inc=1, device_id={"tm": t, "lon": l}, device_id_type=MESH)

    z = zh * 8 + zl

    def on_z(place, xx):
        place = lax.rem(place + 16, 16)
        return lax.rem(place, 8) * 8 + k, lax.rem(xx + 4, 4) * 2 + place // 8

    fours = [(dz, dx) for dz in (4, -4) for dx in (0, 1, -1)]
    for dz, dx in fours:
        greet(*on_z(z + dz, x + dx))
    for dz in (3, -3, 2, -2, 1, -1):
        greet(*on_z(z + dz, x))
    for d in range(1, 8):
        greet(zl * 8 + lax.rem(k + d, 8), lon)
    for d in range(1, 4):
        greet(tm, lon_at(2 * d))
    count = jnp.int32(len(fours) + 6 + 7 + 3)
    for dt in (-2, -1, 1, 2):
        when_t(dt, lambda dt=dt: greet(tm + dt, lon))
        count = count + jnp.where(inside(tm + dt), 1, 0)
    for c in loads[1:7] + loads[8:]:
        c.start()

    for dt in (-2, -1, 1, 2):

        @pl.when(jnp.logical_not(inside(tm + dt)))
        def _(dt=dt):
            for X in (E, G, U):
                X[2 + dt] = jnp.zeros(X.shape[1:], F32)
            for p in range(2):
                AT[p, 2 + dt] = jnp.zeros(AT.shape[2:], F32)
            if abs(dt) == 1:
                tr[(dt + 1) // 2] = jnp.zeros(tr.shape[1:], F32)

    seam_rows[...] = jnp.zeros(seam_rows.shape, F32)
    padded[pl.ds(N, padded.shape[0] - N)] = jnp.zeros((padded.shape[0] - N, rows), F32)

    with jax.named_scope("entry barrier"):
        pl.semaphore_wait(barrier, count)
    for dz, dx in fours:
        greet(*on_z(z + dz, x + dx), sem=hello)

    def remote(src, dst, send, recv, t, l):
        return pltpu.make_async_remote_copy(
            src_ref=src, dst_ref=dst, send_sem=send, recv_sem=recv,
            device_id={"tm": t, "lon": l}, device_id_type=MESH,
        )

    side = 1 - 2 * lax.rem(tm, 2)
    send_days = (-side, 2 * side, side)
    recv_days = (-side, -2 * side, side, 2 * side)

    def plane_copy(p, X, i):
        dt = send_days[i]
        return remote(X.at[2, own], X.at[2 - dt, own], hs.at[p, i], hr.at[p, i], tm + dt, lon)

    def hand_copy(p, X):
        return remote(X.at[2 - side, own], X.at[2 - 2 * side, own], hs.at[p, 3], hr.at[p, 3], tm + side, lon)

    def plane_recv(p, X, i):
        return remote(X.at[2, own], X.at[2 + recv_days[i], own], hs.at[p, i], hr.at[p, i], tm, lon)

    def halo_send(p, X):
        for i in range(3):
            pl.when(inside(tm + send_days[i]))(lambda i=i: plane_copy(p, X, i).start())

    def halo_hand(p, X):
        @pl.when(inside(tm - side))
        def _():
            plane_recv(p, X, 0).wait_recv()
            hand_copy(p, X).start()

    def halo_wait(p, X):
        for i in (1, 2, 3):
            pl.when(inside(tm + recv_days[i]))(lambda i=i: plane_recv(p, X, i).wait_recv())

    def halo_done(p, X):
        for i in range(3):
            pl.when(inside(tm + send_days[i]))(lambda i=i: plane_copy(p, X, i).wait_send())
        pl.when(inside(tm - side))(lambda: hand_copy(p, X).wait_send())

    first_row, last_row = OFF, OFF + N - 1

    def edge_copy(i):
        return remote(ts, tr.at[i], es.at[i], er.at[i], tm + (1, -1)[i], lon)

    def edge_send():
        ts[0:1] = E[2, first_row:first_row + 1]
        ts[1:2] = E[2, last_row:last_row + 1]
        for i, dt in enumerate((1, -1)):
            when_t(dt, lambda i=i: edge_copy(i).start())

    def seam_copy(l):
        return remote(ED.at[lon], ED.at[lon], sems.at[0], sems.at[1], tm, l)

    def seam_all():
        return remote(ED.at[pl.ds(0, 7)], ED.at[pl.ds(0, 7)], sems.at[0], sems.at[1], tm, lon)

    def seam_fill():
        for i, dt in enumerate((1, -1)):
            when_t(-dt, lambda i=i: edge_copy(i).wait_recv())
        bent = tr[0] + tr[1] - 2.0 * ts[...]
        for at, row, inner, side_row in ((0, first_row, first_row + 1, 0), (4, last_row, last_row - 1, 1)):
            ED[lon, at:at + 1] = E[2, row:row + 1]
            ED[lon, at + 1:at + 2] = E[2, inner:inner + 1]
            ED[lon, at + 2:at + 3] = bent[side_row:side_row + 1]
            ED[lon, at + 3:at + 4] = B[row:row + 1]

    def far_lon(d):
        return lax.rem(x + d, 4) * 2 + 1 - zh

    rim_days = (0, 1, -1)

    def rim_copy(p, i, j):
        dt = rim_days[i]
        return remote(ls.at[p, j], lr.at[p, i, j], rs_.at[p, i], rr.at[p, i], tm + dt, lon_at((1, -1)[j]))

    def rim_all(p, i):
        return remote(lr.at[p, i], lr.at[p, i], rs_.at[p, i], rr.at[p, i], tm, lon)

    def rim_send(p, X):
        ls[p, 0, 0:1] = X[2, last_row:last_row + 1]
        ls[p, 0, 1:2] = X[2, last_row - 1:last_row]
        ls[p, 1, 0:1] = X[2, first_row:first_row + 1]
        ls[p, 1, 1:2] = X[2, first_row + 1:first_row + 2]
        for i in (1, 2, 0):
            for j in range(2):
                when_t(rim_days[i], lambda i=i, j=j: rim_copy(p, i, j).start())

    beside = ((first_row - 1, first_row - 2), (last_row + 1, last_row + 2))

    def rim_take(p, X):
        for i, dt in enumerate(rim_days):

            def take(i=i, dt=dt):
                rim_all(p, i).wait_recv()
                for j, (near, far) in enumerate(beside):
                    X[2 - dt, near:near + 1] = lr[p, i, j, 0:1]
                    if dt == 0:
                        X[2, far:far + 1] = lr[p, i, j, 1:2]

            when_t(-dt, take)

    def rim_done(p):
        for i, dt in enumerate(rim_days):
            when_t(dt, lambda i=i: rim_all(p, i).wait_send())

    with jax.named_scope("guess edges"):
        loads[0].wait()
        edge_send()
        halo_send(0, E)
    loads[1].wait()
    with jax.named_scope("far hello"):
        pl.semaphore_wait(hello, len(fours))
    with jax.named_scope("guess seams"):
        for d in (1, 3):
            greet(tm, lon_at(2 * d), sem=hello2)
        seam_fill()
        for d in (0, 1, 3):
            seam_copy(far_lon(d)).start()
        for d in (2, 1, 3):
            seam_copy(lon_at(2 * d)).start()
        pl.semaphore_wait(hello2, 2)
        seam_copy(far_lon(2)).start()
    with jax.named_scope("guess hand on"):
        halo_hand(0, E)

    lane = lax.broadcasted_iota(jnp.int32, (8, rows), 1)
    first_lane, last_lane = lane[:1] == 0, lane[:1] == rows - 1
    loads[7].wait()
    bend = row_ref[0:1]
    centre = row_ref[1:2]
    shrink = row_ref[2:3]
    keep = row_ref[3:4]

    def flat(ref, start, n):
        v = ref[pl.ds(start, n)]
        up, down = ref[pl.ds(start + 1, n)], ref[pl.ds(start - 1, n)]
        lo = jnp.where(first_lane, 0.0, pltpu.roll(v, 1, axis=1))
        hi = jnp.where(last_lane, 0.0, pltpu.roll(v, rows - 1, axis=1))
        return bend * (up + down) + (lo + hi) + centre * v

    own_chunks = [(OFF + c, 72) for c in range(0, N, 72)]
    ext_chunks = [(EXT, 8)] + own_chunks + [(OFF + N, 8)]
    centre_t2 = jnp.where((tm == 0) | (tm == NT - 1), 5.0, 6.0).astype(F32)

    def second(a, b, c):
        return a + b - 2.0 * c

    def second2(a, b, c, d, e):
        return a + e - 4.0 * (b + d) + centre_t2 * c

    def flatten(field):
        for s, n in ext_chunks:
            Y[pl.ds(s, n)] = flat(field, s, n)

    def once(emit=None):
        for s, n in ext_chunks:
            full = TV[pl.ds(s, n)] + Y[pl.ds(s, n)]
            Y[pl.ds(s, n)] = B[pl.ds(s, n)] * full
            if emit is not None and OFF <= s < OFF + N:
                emit(s, n, full)

    def twice(emit):
        for s, n in own_chunks:
            emit(s, n, B[pl.ds(s, n)] * (T2V[pl.ds(s, n)] + flat(TV, s, n)) + flat(Y, s, n))

    with jax.named_scope("weights"):
        for c in loads[2:5]:
            c.wait()
        W[...] = track[...].astype(F32) * (1.0 - land[...].astype(F32))

    with jax.named_scope("guess halo wait"):
        halo_wait(0, E)
    for s, n in ext_chunks:
        r = pl.ds(s, n)
        TV[r] = second(E[1, r], E[3, r], E[2, r])
    for near, _ in beside:
        TV[near:near + 1] = jnp.zeros((1, rows), F32)
    for s, n in own_chunks:
        r = pl.ds(s, n)
        T2V[r] = second2(E[0, r], E[1, r], E[2, r], E[3, r], E[4, r])

    def emit_g(s, n, u):
        l = pl.ds(s - OFF, n)
        g = W[l] * (E[2, pl.ds(s, n)] - obs[l]) + u
        G[2, pl.ds(s, n)] = g
        padded[l] = g

    with jax.named_scope("first operator"):
        for near, _ in beside:
            E[2, near:near + 1] = jnp.zeros((1, rows), F32)
        flatten(E.at[2])
        once()
        for near, _ in beside:
            Y[near:near + 1] = jnp.zeros((1, rows), F32)
        twice(emit_g)
    for c in loads[5:7] + loads[8:]:
        c.wait()

    half = lax.broadcasted_iota(jnp.int32, (MW, rows), 1) < MW

    def rs_copy(p, d):
        q = lax.rem(x + d, 4)
        return remote(amp.at[p, pl.ds(16 * q, 16)], rs_buf.at[p, d], xs.at[p], xr.at[p], tm, q * 2 + zh)

    def rs_all(p):
        return remote(rs_buf.at[p, pl.ds(1, 3)], rs_buf.at[p, pl.ds(1, 3)], xs.at[p], xr.at[p], tm, lon)

    def z_copy(p):
        return remote(quarter.at[p, 0], z_buf.at[p], zs.at[p], zr.at[p], tm, lon + 1 - 2 * zh)

    days = (2, -2, 1, -1, 0)

    def at_copy(p, i, d):
        dt = days[i]
        xx = lax.rem(x + d, 4)
        return remote(
            quarter.at[p, 1], AT.at[p, 2 - dt, pl.ds(16 * x, 16)], ats.at[p, i], atr.at[p, i], tm + dt, xx * 2 + zh
        )

    def at_all(p, i):
        some = AT.at[p, 2 - days[i], pl.ds(0, MW if days[i] else MW - 16)]
        return remote(some, some, ats.at[p, i], atr.at[p, i], tm, lon)

    half16 = lax.broadcasted_iota(jnp.int32, (16, rows), 1) < MW

    def seam_take():
        seam_all().wait_recv()
        er1, er2, ter, ber = (pltpu.roll(ED[:, i, :], 7, axis=0) for i in range(4))
        el1, el2, tel, bel = (ED[:, i, :] for i in range(4, 8))

        def across(v):
            lo = jnp.where(first_lane, 0.0, pltpu.roll(v, 1, axis=1))
            hi = jnp.where(last_lane, 0.0, pltpu.roll(v, rows - 1, axis=1))
            return lo + hi - 2.0 * v

        yl = bel * (tel + across(el1) + bend * (el2 + er1 - 2.0 * el1))
        yr = ber * (ter + across(er1) + bend * (er2 + el1 - 2.0 * er1))
        dr_, dl_ = ber * bend * el1, bel * bend * er1
        seam_rows[0:8] = bend * (yl + ber * tel - 2.0 * dr_) + across(dr_)
        seam_rows[8:16] = bend * dr_
        seam_rows[16:24] = bend * (yr + bel * ter - 2.0 * dl_) + across(dl_)
        seam_rows[24:32] = bend * dl_
        before = lon_at(-1)
        for row, place in (
            (first_row, before), (first_row + 1, 8 + before), (last_row, 16 + lon), (last_row - 1, 24 + lon)
        ):
            G[2, row:row + 1] += seam_rows[pl.ds(place, 1)]
        B[first_row - 1:first_row] = ED[before, 7:8]
        B[last_row + 1:last_row + 2] = ED[lon_at(1), 3:4]
        part = lax.dot(seams[...], seam_rows[...], precision=lax.Precision.HIGH, preferred_element_type=F32)
        seam_amp[...] = jnp.where(half16, pltpu.roll(part[:16], MW, axis=1), part[16:])

    def transform_start(p):
        part = lax.dot(fwd[...], padded[...], precision=lax.Precision.HIGH, preferred_element_type=F32)
        amp[p] = jnp.where(half, pltpu.roll(part[:MW], MW, axis=1), part[MW:])
        for d in (2, 1, 3):
            rs_copy(p, d).start()

    def transform_cross(p):
        total = amp[p, pl.ds(16 * x, 16)]
        rs_all(p).wait_recv()
        for d in (1, 2, 3):
            total = total + rs_buf[p, d]
        quarter[p, 0] = total
        z_copy(p).start()

    def transform_spread(p):
        z_copy(p).wait_recv()
        total = quarter[p, 0] + z_buf[p]
        if p == 0:
            total = total + seam_amp[...]
        quarter[p, 1] = total
        for i, dt in enumerate(days):
            for d in (2, 1, 3, 0) if dt else (2, 1, 3):
                when_t(dt, lambda i=i, d=d: at_copy(p, i, d).start())
        AT[p, 2, pl.ds(16 * x, 16)] = total

    def transform_finish(p, some):
        for i, dt in enumerate(days):
            if dt in some:
                when_t(-dt, lambda i=i: at_all(p, i).wait_recv())

    def transform_done(p):
        rs_all(p).wait_send()
        z_copy(p).wait_send()
        for i, dt in enumerate(days):
            when_t(dt, lambda i=i: at_all(p, i).wait_send())

    def stack(a):
        return jnp.concatenate([pltpu.roll(a, MW, axis=1), a], axis=0) * shrink

    def synthesis(s, n, amplitudes):
        return lax.dot(
            inv[pl.ds(s - EXT, n)], amplitudes, precision=lax.Precision.HIGH, preferred_element_type=F32
        )

    def filter_local(X, field):
        for s, n in ext_chunks:
            r = pl.ds(s, n)
            field[r] = keep * X[2, r]
            TV[r] = keep * second(X[1, r], X[3, r], X[2, r])
            T2V[r] = keep * second2(X[0, r], X[1, r], X[2, r], X[3, r], X[4, r])

    def filter_own(p, field):
        amplitudes = stack(AT[p, 2])
        for s, n in ext_chunks:
            field[pl.ds(s, n)] += synthesis(s, n, amplitudes)
        flatten(field)

    def filter_days(p):
        a = [AT[p, i] for i in range(5)]
        amplitudes = jnp.concatenate([stack(second(a[1], a[3], a[2])), stack(second2(*a))], axis=1)
        for s, n in ext_chunks:
            smooth = synthesis(s, n, amplitudes)
            TV[pl.ds(s, n)] += smooth[:, :rows]
            T2V[pl.ds(s, n)] += smooth[:, rows:]

    sizes = (32, 16)

    def stage_place(stage):
        return (x * 8 + k, z)[stage]

    def stage_device(stage, place):
        if stage == 0:
            return zl * 8 + lax.rem(place, 8), (place // 8) * 2 + zh
        return on_z(place, x)

    def dot_slots(stage):
        return (dots_a, dots_b)[stage]

    def dot_copy(p, stage, d):
        size, mine, slots = sizes[stage], stage_place(stage), dot_slots(stage)
        if stage == 0:
            other = lax.rem(x + d // 8, 4) * 8 + lax.rem(k + d % 8, 8)
        else:
            other = lax.rem(mine + d, size)
        t, l = stage_device(stage, other)
        slot = slots.at[p, mine]
        return remote(slot, slot, ds_.at[p, stage], dr.at[p, stage], t, l)

    def dot_all(p, stage):
        some = dot_slots(stage).at[p, pl.ds(0, sizes[stage] - 1)]
        return remote(some, some, ds_.at[p, stage], dr.at[p, stage], tm, lon)

    steps = (
        [8 * dx + dk for dx in (2, 1, 3, 0) for dk in (4, 3, 5, 2, 6, 1, 7, 0)][:-1],
        [8, 7, 9, 6, 10, 5, 11, 4, 12, 3, 13, 2, 14, 1, 15],
    )

    def dot_send(p, stage, line):
        dot_slots(stage)[p, stage_place(stage)] = line
        for d in steps[stage]:
            dot_copy(p, stage, d).start()

    def dot_take(p, stage):
        dot_all(p, stage).wait_recv()
        total = dot_slots(stage)[p, 0]
        for i in range(1, sizes[stage]):
            total = total + dot_slots(stage)[p, i]
        return total

    def dot_done(p):
        for stage in range(2):
            dot_all(p, stage).wait_send()

    low = lane[:1] < MW

    def pack(slope, curve):
        return jnp.where(low, slope + pltpu.roll(slope, MW, axis=1), curve + pltpu.roll(curve, MW, axis=1))

    def ratio(line):
        slope = jnp.sum(jnp.where(low, line, 0.0), axis=1, keepdims=True)
        return slope / jnp.sum(jnp.where(low, 0.0, line), axis=1, keepdims=True)

    with jax.named_scope("transform zero"):
        transform_start(0)
    with jax.named_scope("cross zero"):
        transform_cross(0)
    with jax.named_scope("seams"):
        seam_take()
    with jax.named_scope("rim one send"):
        rim_send(0, G)
    with jax.named_scope("halo one send"):
        halo_send(1, G)
    with jax.named_scope("spread zero"):
        transform_spread(0)
    with jax.named_scope("hand on one"):
        halo_hand(1, G)
    with jax.named_scope("rim one wait"):
        rim_take(0, G)
    with jax.named_scope("halo one wait"):
        halo_wait(1, G)
    with jax.named_scope("filter zero local"):
        filter_local(G, V0)
    with jax.named_scope("finish zero"):
        transform_finish(0, (0,))
    with jax.named_scope("filter zero own"):
        filter_own(0, V0)
    with jax.named_scope("finish zero days"):
        transform_finish(0, (1, -1, 2, -2))
    with jax.named_scope("filter zero days"):
        filter_days(0)
    acc = [jnp.zeros((1, rows), F32), jnp.zeros((1, rows), F32)]

    def emit_first(s, n, full):
        LV0[pl.ds(s - OFF, n)] = full

    def emit_u(s, n, u):
        l, r = pl.ds(s - OFF, n), pl.ds(s, n)
        v = V0[r]
        u = W[l] * v + u
        U[2, r] = u
        padded[l] = u
        acc[0] = acc[0] + jnp.sum(G[2, r] * v, axis=0, keepdims=True)
        acc[1] = acc[1] + jnp.sum(v * u, axis=0, keepdims=True)

    with jax.named_scope("operator one"):
        once(emit_first)
        twice(emit_u)

    with jax.named_scope("transform one"):
        transform_start(1)
    with jax.named_scope("edges two send"):
        dot_send(0, 0, pack(*acc))
    with jax.named_scope("cross one"):
        transform_cross(1)
    with jax.named_scope("rim two send"):
        rim_send(1, U)
    with jax.named_scope("halo two send"):
        halo_send(2, U)
    with jax.named_scope("sums zero"):
        dot_send(0, 1, dot_take(0, 0))
    with jax.named_scope("spread one"):
        transform_spread(1)
    with jax.named_scope("hand on two"):
        halo_hand(2, U)
    with jax.named_scope("rim two wait"):
        rim_take(1, U)
    with jax.named_scope("halo two wait"):
        halo_wait(2, U)
    with jax.named_scope("filter one local"):
        filter_local(U, V)
    with jax.named_scope("finish one"):
        transform_finish(1, (0,))
    with jax.named_scope("filter one own"):
        filter_own(1, V)
    with jax.named_scope("step zero"):
        step0 = ratio(dot_take(0, 1))
    with jax.named_scope("finish one days"):
        transform_finish(1, (1, -1, 2, -2))
    with jax.named_scope("filter one days"):
        filter_days(1)
    acc[0] = acc[1] = jnp.zeros((1, rows), F32)

    def emit_sums(s, n, full):
        l, r = pl.ds(s - OFF, n), pl.ds(s, n)
        search = V0[r] - step0 * V[r]
        gradient = G[2, r] - step0 * U[2, r]
        bent = LV0[l] - step0 * full
        acc[0] = acc[0] + jnp.sum(gradient * search, axis=0, keepdims=True)
        acc[1] = acc[1] + jnp.sum(W[l] * (search * search) + B[r] * (bent * bent), axis=0, keepdims=True)
        out_s[0, l] = search
        out_g[0, l] = gradient

    with jax.named_scope("operator two once"):
        once(emit_sums)
    with jax.named_scope("sums one a"):
        dot_send(1, 0, pack(*acc))

    def emit_last(s, n, u1):
        l, r = pl.ds(s - OFF, n), pl.ds(s, n)
        out_c[0, l] = U[2, r] - step0 * (W[l] * V[r] + u1)
        out_a[0, l] = E[2, r] - step0 * V0[r]

    with jax.named_scope("operator two twice"):
        twice(emit_last)
    with jax.named_scope("sums one b"):
        dot_send(1, 1, dot_take(1, 0))
    for p, X in enumerate((E, G, U)):
        halo_done(p, X)
    for i, dt in enumerate((1, -1)):
        when_t(dt, lambda i=i: edge_copy(i).wait_send())
    seam_all().wait_send()
    for p in range(2):
        transform_done(p)
        rim_done(p)
    dot_done(0)
    with jax.named_scope("sums one c"):
        out_step[...] = jnp.broadcast_to(ratio(dot_take(1, 1)), out_step.shape)
    with jax.named_scope("drain"):
        dot_done(1)


def on_device(NT, NL, first, obs, track, land, bw):
    _, N, rows = first.shape
    forward, inverse, row, seams = tables(NL, N, rows)
    plane = pltpu.VMEM((N + 32, rows), F32)
    planes = pltpu.VMEM((5, N + 32, rows), F32)
    flat = pltpu.VMEM((N, rows), F32)
    whole = pltpu.VMEM((N, rows), jnp.int32)
    dma = pltpu.SemaphoreType.DMA
    hbm = pl.BlockSpec(memory_space=pltpu.HBM)
    surface, search, gradient, curved, step = pl.pallas_call(
        functools.partial(kernel, NT, N),
        out_shape=[pltpu.VMEM(first.shape, F32)] * 4 + [pltpu.VMEM((1, rows), F32)],
        in_specs=[hbm] * 9,
        out_specs=[pl.BlockSpec(memory_space=pltpu.VMEM)] * 5,
        scratch_shapes=[
            pltpu.VMEM(row.shape, F32), planes, planes, planes,
            plane, flat, flat, whole, whole,
            pltpu.VMEM(forward.shape[1:], F32), pltpu.VMEM(inverse.shape[1:], F32),
            plane, plane, plane, plane, plane, flat,
            pltpu.VMEM((forward.shape[2], rows), F32),
            pltpu.VMEM(seams.shape[1:], F32), pltpu.VMEM((128, rows), F32),
            pltpu.VMEM((16, rows), F32), pltpu.VMEM((8, 8, rows), F32),
            pltpu.VMEM((2, MW, rows), F32),
            pltpu.VMEM((2, 4, 16, rows), F32),
            pltpu.VMEM((2, 2, 16, rows), F32),
            pltpu.VMEM((2, 16, rows), F32),
            pltpu.VMEM((2, 5, MW, rows), F32),
            pltpu.VMEM((2, 32, 1, rows), F32),
            pltpu.VMEM((2, 16, 1, rows), F32),
            pltpu.VMEM((2, rows), F32),
            pltpu.VMEM((2, 2, rows), F32),
            pltpu.VMEM((2, 2, 2, rows), F32),
            pltpu.VMEM((2, 3, 2, 2, rows), F32),
            pltpu.SemaphoreType.REGULAR, pltpu.SemaphoreType.REGULAR, dma((2,)), dma((9,)), dma((3, 4)), dma((3, 4)),
            dma((2,)), dma((2,)), dma((2, 3)), dma((2, 3)),
            dma((2,)), dma((2,)), dma((2,)), dma((2,)), dma((2, 5)), dma((2, 5)),
            dma((2, 2)), dma((2, 2)),
        ],
        compiler_params=pltpu.CompilerParams(
            collective_id=0, has_side_effects=True, vmem_limit_bytes=56 * 1024 * 1024
        ),
    )(first, obs, track, land, bw, forward, inverse, row, seams)
    return surface - step[None] * search, gradient - step[None] * curved


def solution(mesh):
    in_specs = (
        P("tm", "lon", None),
        P("tm", "lon", None),
        P("tm", "lon", None),
        P("lon", None),
        P("lon", None),
    )
    out_specs = (P("tm", "lon", None), P("tm", "lon", None))
    return jax.shard_map(
        functools.partial(on_device, mesh.shape["tm"], mesh.shape["lon"]),
        mesh=mesh, in_specs=in_specs, out_specs=out_specs, check_vma=False,
    )
```

```python
import functools

import jax
import jax.numpy as jnp
import numpy as np
from jax import lax
from jax.experimental import pallas as pl
from jax.experimental.pallas import tpu as pltpu
from jax.sharding import PartitionSpec as P

CAP = 64
MW = 64
MESH = pl.DeviceIdType.MESH
OFF = 16
EXT = 8
F32 = jnp.float32


def tables(segments, length, rows):
    circle = segments * length
    harmonic = np.arange(MW)
    w = np.where(harmonic == 0, 1.0 / circle, 2.0 / circle)
    padded = -(-length // 128) * 128
    forward = np.zeros((segments, 2 * MW, padded), np.float32)
    inverse = np.zeros((segments, length + 16, 2 * MW), np.float32)
    for s in range(segments):
        a = 2 * np.pi * ((np.arange(length) + s * length)[:, None] * harmonic % circle) / circle
        forward[s, :MW, :length] = np.cos(a).T
        forward[s, MW:, :length] = np.sin(a).T
        a = 2 * np.pi * ((np.arange(length + 16) - 8 + s * length)[:, None] * harmonic % circle) / circle
        inverse[s] = np.concatenate([w * np.cos(a), w * np.sin(a)], axis=1)
    phi = (90.0 - (rows - np.arange(rows) - 0.5) * 0.125) * (np.pi / 180.0)
    bend = 1.0 / (np.cos(phi) + 0.5) ** 2
    shrink = np.zeros(rows)
    shrink[rows - CAP:] = 0.9 * (np.arange(CAP) + 1.0) / CAP
    row = np.zeros((8, rows), np.float32)
    row[0] = bend
    row[1] = -2.0 * (bend + 1.0)
    row[2] = shrink
    row[3] = 1.0 - shrink
    seams = np.zeros((4, 32, 128), np.float32)
    for i, offset in enumerate((0, 1, -1, -2)):
        place = (np.arange(segments) + 1) * length + offset
        a = 2 * np.pi * (place[None, :] * harmonic[:, None] % circle) / circle
        for q in range(4):
            seams[q, :16, 8 * i:8 * i + 8] = np.cos(a[16 * q:16 * q + 16])
            seams[q, 16:, 8 * i:8 * i + 8] = np.sin(a[16 * q:16 * q + 16])
    return forward, inverse, row, seams


def kernel(
    NT, N, first_ref, obs_ref, track_ref, land_ref, bw_ref, fwd_ref, inv_ref, row_hbm, seams_hbm,
    out_a, out_s, out_g, out_c, out_step,
    row_ref, E, G, U, B, W, obs, track, land, fwd, inv, V, TV, T2V, Y, V0, LV0, padded, seams, seam_rows, seam_amp, ED, amp, rs_buf, quarter,
    z_buf, AT, dots_a, dots_b, ts, tr, ls, lr, bs, br,
    hello, sems, bsem, brem, lsem, hs, hr, es, er, rs_, rr, xs, xr, zs, zr, ats, atr, ds_, dr,
):
    tm = lax.axis_index("tm")
    lon = lax.axis_index("lon")
    x, zh = lon // 2, lon % 2
    zl, k = tm // 8, tm % 8
    rows = 128

    def inside(t):
        return (t >= 0) & (t < NT)

    def when_t(dt, fn):
        if dt == 0:
            fn()
        else:
            pl.when(inside(tm + dt))(fn)

    def lon_at(d):
        return lax.rem(lon + d + 8, 8)

    own = pl.ds(OFF, N)
    loads = [
        pltpu.make_async_copy(first_ref.at[0], E.at[2, own], lsem.at[0]),
        pltpu.make_async_copy(bw_ref, B.at[own], lsem.at[1]),
        pltpu.make_async_copy(obs_ref.at[0], obs, lsem.at[2]),
        pltpu.make_async_copy(track_ref.at[0], track, lsem.at[3]),
        pltpu.make_async_copy(land_ref, land, lsem.at[4]),
        pltpu.make_async_copy(fwd_ref.at[lon], fwd, lsem.at[5]),
        pltpu.make_async_copy(inv_ref.at[lon], inv, lsem.at[6]),
        pltpu.make_async_copy(row_hbm, row_ref, lsem.at[7]),
        pltpu.make_async_copy(seams_hbm.at[x], seams, lsem.at[8]),
    ]
    loads[0].start()
    loads[7].start()

    barrier = pltpu.get_barrier_semaphore()

    def greet(t, l, sem=barrier):
        pl.semaphore_signal(sem, inc=1, device_id={"tm": t, "lon": l}, device_id_type=MESH)

    z = zh * 8 + zl

    def on_z(place, xx):
        place = lax.rem(place + 16, 16)
        return lax.rem(place, 8) * 8 + k, xx * 2 + place // 8

    for dz in (2, -2, 1, -1):
        greet(*on_z(z + dz, x))
    for d in range(1, 8):
        greet(zl * 8 + lax.rem(k + d, 8), lon)
    for d in range(1, 4):
        greet(tm, lon_at(2 * d))
    count = jnp.int32(4 + 7 + 3)
    for dt in (-2, -1, 1, 2):
        when_t(dt, lambda dt=dt: greet(tm + dt, lon))
        count = count + jnp.where(inside(tm + dt), 1, 0)
    for c in loads[1:7] + loads[8:]:
        c.start()

    for dt in (-2, -1, 1, 2):

        @pl.when(jnp.logical_not(inside(tm + dt)))
        def _(dt=dt):
            for X in (E, G, U):
                X[2 + dt] = jnp.zeros(X.shape[1:], F32)
            for p in range(2):
                AT[p, 2 + dt] = jnp.zeros(AT.shape[2:], F32)
            if abs(dt) == 1:
                tr[(dt + 1) // 2] = jnp.zeros(tr.shape[1:], F32)

    seam_rows[...] = jnp.zeros(seam_rows.shape, F32)
    bs[...] = jnp.zeros(bs.shape, F32)
    padded[pl.ds(N, padded.shape[0] - N)] = jnp.zeros((padded.shape[0] - N, rows), F32)

    with jax.named_scope("entry barrier"):
        pl.semaphore_wait(barrier, count)
    for dz in (2, -2):
        greet(*on_z(z + dz, x), sem=hello.at[0])

    def remote(src, dst, send, recv, t, l):
        return pltpu.make_async_remote_copy(
            src_ref=src, dst_ref=dst, send_sem=send, recv_sem=recv,
            device_id={"tm": t, "lon": l}, device_id_type=MESH,
        )

    side = 1 - 2 * lax.rem(tm, 2)
    send_days = (-side, 2 * side, side)
    recv_days = (-side, -2 * side, side, 2 * side)

    def plane_copy(p, X, i):
        dt = send_days[i]
        return remote(X.at[2, own], X.at[2 - dt, own], hs.at[p, i], hr.at[p, i], tm + dt, lon)

    def hand_copy(p, X):
        return remote(X.at[2 - side, own], X.at[2 - 2 * side, own], hs.at[p, 3], hr.at[p, 3], tm + side, lon)

    def plane_recv(p, X, i):
        return remote(X.at[2, own], X.at[2 + recv_days[i], own], hs.at[p, i], hr.at[p, i], tm, lon)

    def halo_send(p, X):
        for i in range(3):
            pl.when(inside(tm + send_days[i]))(lambda i=i: plane_copy(p, X, i).start())

    def halo_hand(p, X):
        @pl.when(inside(tm - side))
        def _():
            plane_recv(p, X, 0).wait_recv()
            hand_copy(p, X).start()

    def halo_wait(p, X):
        for i in (1, 2, 3):
            pl.when(inside(tm + recv_days[i]))(lambda i=i: plane_recv(p, X, i).wait_recv())
        pl.when(inside(tm - side))(lambda: hand_copy(p, X).wait_send())

    def halo_done(p, X):
        for i in range(3):
            pl.when(inside(tm + send_days[i]))(lambda i=i: plane_copy(p, X, i).wait_send())

    first_row, last_row = OFF, OFF + N - 1

    def edge_copy(i):
        return remote(ts, tr.at[i], es.at[i], er.at[i], tm + (1, -1)[i], lon)

    def edge_send():
        ts[0:1] = E[2, first_row:first_row + 1]
        ts[1:2] = E[2, last_row:last_row + 1]
        for i, dt in enumerate((1, -1)):
            when_t(dt, lambda i=i: edge_copy(i).start())

    def seam_copy(l):
        return remote(ED.at[lon], ED.at[lon], sems.at[0], sems.at[1], tm, l)

    def seam_all():
        return remote(ED.at[pl.ds(0, 7)], ED.at[pl.ds(0, 7)], sems.at[0], sems.at[1], tm, lon)

    def seam_fill():
        for i, dt in enumerate((1, -1)):
            when_t(-dt, lambda i=i: edge_copy(i).wait_recv())
        bent = tr[0] + tr[1] - 2.0 * ts[...]
        for at, row, inner, side_row in ((0, first_row, first_row + 1, 0), (4, last_row, last_row - 1, 1)):
            ED[lon, at:at + 1] = E[2, row:row + 1]
            ED[lon, at + 1:at + 2] = E[2, inner:inner + 1]
            ED[lon, at + 2:at + 3] = bent[side_row:side_row + 1]
            ED[lon, at + 3:at + 4] = B[row:row + 1]

    def far_lon(d):
        return lax.rem(x + d, 4) * 2 + 1 - zh

    def rim_copy(p, j):
        return remote(ls.at[p, j], lr.at[p, j], rs_.at[p], rr.at[p], tm, lon_at((1, -1)[j]))

    def rim_all(p):
        return remote(lr.at[p], lr.at[p], rs_.at[p], rr.at[p], tm, lon)

    def rim_send(p, X):
        ls[p, 0, 0:1] = X[2, last_row:last_row + 1]
        ls[p, 0, 1:2] = X[2, last_row - 1:last_row]
        ls[p, 1, 0:1] = X[2, first_row:first_row + 1]
        ls[p, 1, 1:2] = X[2, first_row + 1:first_row + 2]
        for j in range(2):
            rim_copy(p, j).start()

    beside = ((first_row - 1, first_row - 2), (last_row + 1, last_row + 2))
    before = lon_at(-1)

    def rim_take(p, X):
        rim_all(p).wait_recv()
        for j, (near, far) in enumerate(beside):
            for i, row in enumerate((near, far)):
                line = lr[p, j, i:i + 1]
                if p == 0:
                    line = line + seam_rows[pl.ds((16, 0)[j] + 8 * i + (before, lon)[j], 1)]
                X[2, row:row + 1] = line

    border_rows = (first_row, first_row + 1, last_row - 1, last_row, first_row - 1, last_row + 1)
    border_days = (2, -2, 1, -1)

    def border_copy(p, i):
        return remote(bs.at[p], br.at[p, i], bsem.at[p, i], brem.at[p, i], tm + border_days[i], lon)

    def border_send(p, X):
        for i, row in enumerate(border_rows):
            bs[p, i:i + 1] = X[2, row:row + 1]
        for i, dt in enumerate(border_days):
            when_t(dt, lambda i=i: border_copy(p, i).start())

    def border_take(p, X):
        for i, dt in enumerate(border_days):

            def take(i=i, dt=dt):
                border_copy(p, i).wait_recv()
                for j, row in enumerate(border_rows[:6 if abs(dt) == 1 else 4]):
                    X[2 - dt, row:row + 1] = br[p, i, j:j + 1]

            when_t(-dt, take)

    def border_done(p):
        for i, dt in enumerate(border_days):
            when_t(dt, lambda i=i: border_copy(p, i).wait_send())

    with jax.named_scope("guess edges"):
        loads[0].wait()
        edge_send()
        halo_send(0, E)
    with jax.named_scope("far hello"):
        pl.semaphore_wait(hello.at[0], 2)
        for dz in (4, -4):
            greet(*on_z(z + dz, x), sem=hello.at[1])
    loads[1].wait()
    with jax.named_scope("guess seams"):
        seam_fill()
        for d in (2, 1, 3):
            seam_copy(lon_at(2 * d)).start()
        pl.semaphore_wait(hello.at[1], 2)
        for d in (2, 1, 3):
            greet(tm, lon_at(2 * d), sem=hello.at[2])
        seam_copy(far_lon(0)).start()
    with jax.named_scope("guess hand on"):
        halo_hand(0, E)
    with jax.named_scope("guess far seams"):
        pl.semaphore_wait(hello.at[2], 3)
        for d in (2, 1, 3):
            seam_copy(far_lon(d)).start()

    lane = lax.broadcasted_iota(jnp.int32, (8, rows), 1)
    first_lane, last_lane = lane[:1] == 0, lane[:1] == rows - 1
    loads[7].wait()
    bend = row_ref[0:1]
    centre = row_ref[1:2]
    shrink = row_ref[2:3]
    keep = row_ref[3:4]

    def flat(ref, start, n):
        v = ref[pl.ds(start, n)]
        up, down = ref[pl.ds(start + 1, n)], ref[pl.ds(start - 1, n)]
        lo = jnp.where(first_lane, 0.0, pltpu.roll(v, 1, axis=1))
        hi = jnp.where(last_lane, 0.0, pltpu.roll(v, rows - 1, axis=1))
        return bend * (up + down) + (lo + hi) + centre * v

    own_chunks = [(OFF + c, 72) for c in range(0, N, 72)]
    ext_chunks = [(EXT, 8)] + own_chunks + [(OFF + N, 8)]
    centre_t2 = jnp.where((tm == 0) | (tm == NT - 1), 5.0, 6.0).astype(F32)

    def second(a, b, c):
        return a + b - 2.0 * c

    def second2(a, b, c, d, e):
        return a + e - 4.0 * (b + d) + centre_t2 * c

    def flatten(field):
        for s, n in ext_chunks:
            Y[pl.ds(s, n)] = flat(field, s, n)

    def once(emit=None):
        for s, n in ext_chunks:
            full = TV[pl.ds(s, n)] + Y[pl.ds(s, n)]
            Y[pl.ds(s, n)] = B[pl.ds(s, n)] * full
            if emit is not None and OFF <= s < OFF + N:
                emit(s, n, full)

    def twice(emit):
        for s, n in own_chunks:
            emit(s, n, B[pl.ds(s, n)] * (T2V[pl.ds(s, n)] + flat(TV, s, n)) + flat(Y, s, n))

    with jax.named_scope("weights"):
        for c in loads[2:5]:
            c.wait()
        W[...] = track[...].astype(F32) * (1.0 - land[...].astype(F32))

    with jax.named_scope("guess halo wait"):
        halo_wait(0, E)
    for s, n in ext_chunks:
        r = pl.ds(s, n)
        TV[r] = second(E[1, r], E[3, r], E[2, r])
    for near, _ in beside:
        TV[near:near + 1] = jnp.zeros((1, rows), F32)
    for s, n in own_chunks:
        r = pl.ds(s, n)
        T2V[r] = second2(E[0, r], E[1, r], E[2, r], E[3, r], E[4, r])

    def emit_g(s, n, u):
        l = pl.ds(s - OFF, n)
        g = W[l] * (E[2, pl.ds(s, n)] - obs[l]) + u
        G[2, pl.ds(s, n)] = g
        padded[l] = g

    with jax.named_scope("first operator"):
        for near, _ in beside:
            E[2, near:near + 1] = jnp.zeros((1, rows), F32)
        flatten(E.at[2])
        once()
        for near, _ in beside:
            Y[near:near + 1] = jnp.zeros((1, rows), F32)
        twice(emit_g)
    for c in loads[5:7] + loads[8:]:
        c.wait()

    half = lax.broadcasted_iota(jnp.int32, (MW, rows), 1) < MW

    def rs_copy(p, d):
        q = lax.rem(x + d, 4)
        return remote(amp.at[p, pl.ds(16 * q, 16)], rs_buf.at[p, d], xs.at[p], xr.at[p], tm, q * 2 + zh)

    def rs_all(p):
        return remote(rs_buf.at[p, pl.ds(1, 3)], rs_buf.at[p, pl.ds(1, 3)], xs.at[p], xr.at[p], tm, lon)

    def z_copy(p):
        return remote(quarter.at[p, 0], z_buf.at[p], zs.at[p], zr.at[p], tm, lon + 1 - 2 * zh)

    days = (2, -2, 1, -1, 0)

    def at_copy(p, i, d):
        dt = days[i]
        xx = lax.rem(x + d, 4)
        return remote(
            quarter.at[p, 1], AT.at[p, 2 - dt, pl.ds(16 * x, 16)], ats.at[p, i], atr.at[p, i], tm + dt, xx * 2 + zh
        )

    def at_all(p, i):
        some = AT.at[p, 2 - days[i], pl.ds(0, MW if days[i] else MW - 16)]
        return remote(some, some, ats.at[p, i], atr.at[p, i], tm, lon)

    half16 = lax.broadcasted_iota(jnp.int32, (16, rows), 1) < MW

    def seam_take():
        seam_all().wait_recv()
        er1, er2, ter, ber = (pltpu.roll(ED[:, i, :], 7, axis=0) for i in range(4))
        el1, el2, tel, bel = (ED[:, i, :] for i in range(4, 8))

        def across(v):
            lo = jnp.where(first_lane, 0.0, pltpu.roll(v, 1, axis=1))
            hi = jnp.where(last_lane, 0.0, pltpu.roll(v, rows - 1, axis=1))
            return lo + hi - 2.0 * v

        yl = bel * (tel + across(el1) + bend * (el2 + er1 - 2.0 * el1))
        yr = ber * (ter + across(er1) + bend * (er2 + el1 - 2.0 * er1))
        dr_, dl_ = ber * bend * el1, bel * bend * er1
        seam_rows[0:8] = bend * (yl + ber * tel - 2.0 * dr_) + across(dr_)
        seam_rows[8:16] = bend * dr_
        seam_rows[16:24] = bend * (yr + bel * ter - 2.0 * dl_) + across(dl_)
        seam_rows[24:32] = bend * dl_
        for row, place in (
            (first_row, before), (first_row + 1, 8 + before), (last_row, 16 + lon), (last_row - 1, 24 + lon)
        ):
            G[2, row:row + 1] += seam_rows[pl.ds(place, 1)]
        B[first_row - 1:first_row] = ED[before, 7:8]
        B[last_row + 1:last_row + 2] = ED[lon_at(1), 3:4]
        part = lax.dot(seams[...], seam_rows[...], precision=lax.Precision.HIGH, preferred_element_type=F32)
        seam_amp[...] = jnp.where(half16, pltpu.roll(part[:16], MW, axis=1), part[16:])

    def transform_start(p):
        part = lax.dot(fwd[...], padded[...], precision=lax.Precision.HIGH, preferred_element_type=F32)
        amp[p] = jnp.where(half, pltpu.roll(part[:MW], MW, axis=1), part[MW:])
        for d in (2, 1, 3):
            rs_copy(p, d).start()

    def transform_cross(p):
        total = amp[p, pl.ds(16 * x, 16)]
        rs_all(p).wait_recv()
        for d in (1, 2, 3):
            total = total + rs_buf[p, d]
        quarter[p, 0] = total
        z_copy(p).start()

    def transform_spread(p):
        z_copy(p).wait_recv()
        total = quarter[p, 0] + z_buf[p]
        if p == 0:
            total = total + seam_amp[...]
        quarter[p, 1] = total
        for i, dt in enumerate(days):
            for d in (2, 1, 3, 0) if dt else (2, 1, 3):
                when_t(dt, lambda i=i, d=d: at_copy(p, i, d).start())
        AT[p, 2, pl.ds(16 * x, 16)] = total

    def transform_finish(p, some):
        for i, dt in enumerate(days):
            if dt in some:
                when_t(-dt, lambda i=i: at_all(p, i).wait_recv())

    def transform_done(p):
        rs_all(p).wait_send()
        z_copy(p).wait_send()
        for i, dt in enumerate(days):
            when_t(dt, lambda i=i: at_all(p, i).wait_send())

    def stack(a):
        return jnp.concatenate([pltpu.roll(a, MW, axis=1), a], axis=0) * shrink

    def synthesis(s, n, amplitudes):
        return lax.dot(
            inv[pl.ds(s - EXT, n)], amplitudes, precision=lax.Precision.HIGH, preferred_element_type=F32
        )

    def filter_local(X, field):
        for s, n in ext_chunks:
            r = pl.ds(s, n)
            field[r] = keep * X[2, r]
            TV[r] = keep * second(X[1, r], X[3, r], X[2, r])
            T2V[r] = keep * second2(X[0, r], X[1, r], X[2, r], X[3, r], X[4, r])

    def filter_own(p, field):
        amplitudes = stack(AT[p, 2])
        for s, n in ext_chunks:
            field[pl.ds(s, n)] += synthesis(s, n, amplitudes)
        flatten(field)

    def filter_days(p):
        a = [AT[p, i] for i in range(5)]
        amplitudes = jnp.concatenate([stack(second(a[1], a[3], a[2])), stack(second2(*a))], axis=1)
        for s, n in ext_chunks:
            smooth = synthesis(s, n, amplitudes)
            TV[pl.ds(s, n)] += smooth[:, :rows]
            T2V[pl.ds(s, n)] += smooth[:, rows:]

    sizes = (32, 16)

    def stage_place(stage):
        return (x * 8 + k, z)[stage]

    def stage_device(stage, place):
        if stage == 0:
            return zl * 8 + lax.rem(place, 8), (place // 8) * 2 + zh
        return on_z(place, x)

    def dot_slots(stage):
        return (dots_a, dots_b)[stage]

    def dot_copy(p, stage, d):
        size, mine, slots = sizes[stage], stage_place(stage), dot_slots(stage)
        if stage == 0:
            other = lax.rem(x + d // 8, 4) * 8 + lax.rem(k + d % 8, 8)
        else:
            other = lax.rem(mine + d, size)
        t, l = stage_device(stage, other)
        slot = slots.at[p, mine]
        return remote(slot, slot, ds_.at[p, stage], dr.at[p, stage], t, l)

    def dot_all(p, stage):
        some = dot_slots(stage).at[p, pl.ds(0, sizes[stage] - 1)]
        return remote(some, some, ds_.at[p, stage], dr.at[p, stage], tm, lon)

    steps = (
        [8 * dx + dk for dx in (2, 1, 3, 0) for dk in (4, 3, 5, 2, 6, 1, 7, 0)][:-1],
        [8, 7, 9, 6, 10, 5, 11, 4, 12, 3, 13, 2, 14, 1, 15],
    )

    def dot_send(p, stage, line):
        dot_slots(stage)[p, stage_place(stage)] = line
        for d in steps[stage]:
            dot_copy(p, stage, d).start()

    def dot_take(p, stage):
        dot_all(p, stage).wait_recv()
        total = dot_slots(stage)[p, 0]
        for i in range(1, sizes[stage]):
            total = total + dot_slots(stage)[p, i]
        return total

    def dot_done(p):
        for stage in range(2):
            dot_all(p, stage).wait_send()

    low = lane[:1] < MW

    def pack(slope, curve):
        return jnp.where(low, slope + pltpu.roll(slope, MW, axis=1), curve + pltpu.roll(curve, MW, axis=1))

    def ratio(line):
        slope = jnp.sum(jnp.where(low, line, 0.0), axis=1, keepdims=True)
        return slope / jnp.sum(jnp.where(low, 0.0, line), axis=1, keepdims=True)

    with jax.named_scope("transform zero"):
        transform_start(0)
    with jax.named_scope("rim one send"):
        rim_send(0, G)
    with jax.named_scope("halo one send"):
        halo_send(1, G)
    with jax.named_scope("cross zero"):
        transform_cross(0)
    with jax.named_scope("seams"):
        halo_done(1, G)
        seam_take()
    with jax.named_scope("rim one wait"):
        rim_take(0, G)
    with jax.named_scope("border one send"):
        border_send(0, G)
    with jax.named_scope("hand on one"):
        halo_hand(1, G)
    with jax.named_scope("spread zero"):
        transform_spread(0)
    with jax.named_scope("halo one wait"):
        halo_wait(1, G)
        border_take(0, G)
    with jax.named_scope("filter zero local"):
        filter_local(G, V0)
    with jax.named_scope("finish zero"):
        transform_finish(0, (0,))
    with jax.named_scope("filter zero own"):
        filter_own(0, V0)
    with jax.named_scope("finish zero days"):
        transform_finish(0, (1, -1, 2, -2))
    with jax.named_scope("filter zero days"):
        filter_days(0)
    acc = [jnp.zeros((1, rows), F32), jnp.zeros((1, rows), F32)]

    def emit_first(s, n, full):
        LV0[pl.ds(s - OFF, n)] = full

    def emit_u(s, n, u):
        l, r = pl.ds(s - OFF, n), pl.ds(s, n)
        v = V0[r]
        u = W[l] * v + u
        U[2, r] = u
        padded[l] = u
        acc[0] = acc[0] + jnp.sum(G[2, r] * v, axis=0, keepdims=True)
        acc[1] = acc[1] + jnp.sum(v * u, axis=0, keepdims=True)

    with jax.named_scope("operator one"):
        once(emit_first)
        twice(emit_u)

    with jax.named_scope("transform one"):
        transform_start(1)
    with jax.named_scope("edges two send"):
        dot_send(0, 0, pack(*acc))
    with jax.named_scope("rim two send"):
        rim_send(1, U)
    with jax.named_scope("halo two send"):
        halo_send(2, U)
    with jax.named_scope("cross one"):
        transform_cross(1)
    with jax.named_scope("sums zero"):
        dot_send(0, 1, dot_take(0, 0))
    with jax.named_scope("rim two wait"):
        rim_take(1, U)
    with jax.named_scope("border two send"):
        border_send(1, U)
    with jax.named_scope("hand on two"):
        halo_hand(2, U)
    with jax.named_scope("spread one"):
        transform_spread(1)
    with jax.named_scope("halo two wait"):
        halo_wait(2, U)
        border_take(1, U)
    with jax.named_scope("filter one local"):
        filter_local(U, V)
    with jax.named_scope("finish one"):
        transform_finish(1, (0,))
    with jax.named_scope("filter one own"):
        filter_own(1, V)
    with jax.named_scope("step zero"):
        step0 = ratio(dot_take(0, 1))
    with jax.named_scope("finish one days"):
        transform_finish(1, (1, -1, 2, -2))
    with jax.named_scope("filter one days"):
        filter_days(1)
    acc[0] = acc[1] = jnp.zeros((1, rows), F32)

    def emit_sums(s, n, full):
        l, r = pl.ds(s - OFF, n), pl.ds(s, n)
        search = V0[r] - step0 * V[r]
        gradient = G[2, r] - step0 * U[2, r]
        bent = LV0[l] - step0 * full
        acc[0] = acc[0] + jnp.sum(gradient * search, axis=0, keepdims=True)
        acc[1] = acc[1] + jnp.sum(W[l] * (search * search) + B[r] * (bent * bent), axis=0, keepdims=True)
        out_s[0, l] = search
        out_g[0, l] = gradient

    with jax.named_scope("operator two once"):
        once(emit_sums)
    with jax.named_scope("sums one a"):
        dot_send(1, 0, pack(*acc))

    def emit_last(s, n, u1):
        l, r = pl.ds(s - OFF, n), pl.ds(s, n)
        out_c[0, l] = U[2, r] - step0 * (W[l] * V[r] + u1)
        out_a[0, l] = E[2, r] - step0 * V0[r]

    with jax.named_scope("operator two twice"):
        twice(emit_last)
    with jax.named_scope("sums one b"):
        dot_send(1, 1, dot_take(1, 0))
    halo_done(0, E)
    halo_done(2, U)
    for i, dt in enumerate((1, -1)):
        when_t(dt, lambda i=i: edge_copy(i).wait_send())
    seam_all().wait_send()
    for p in range(2):
        transform_done(p)
        rim_all(p).wait_send()
        border_done(p)
    dot_done(0)
    with jax.named_scope("sums one c"):
        out_step[...] = jnp.broadcast_to(ratio(dot_take(1, 1)), out_step.shape)
    with jax.named_scope("drain"):
        dot_done(1)


def on_device(NT, NL, first, obs, track, land, bw):
    _, N, rows = first.shape
    forward, inverse, row, seams = tables(NL, N, rows)
    plane = pltpu.VMEM((N + 32, rows), F32)
    planes = pltpu.VMEM((5, N + 32, rows), F32)
    flat = pltpu.VMEM((N, rows), F32)
    whole = pltpu.VMEM((N, rows), jnp.int32)
    dma = pltpu.SemaphoreType.DMA
    hbm = pl.BlockSpec(memory_space=pltpu.HBM)
    surface, search, gradient, curved, step = pl.pallas_call(
        functools.partial(kernel, NT, N),
        out_shape=[pltpu.VMEM(first.shape, F32)] * 4 + [pltpu.VMEM((1, rows), F32)],
        in_specs=[hbm] * 9,
        out_specs=[pl.BlockSpec(memory_space=pltpu.VMEM)] * 5,
        scratch_shapes=[
            pltpu.VMEM(row.shape, F32), planes, planes, planes,
            plane, flat, flat, whole, whole,
            pltpu.VMEM(forward.shape[1:], F32), pltpu.VMEM(inverse.shape[1:], F32),
            plane, plane, plane, plane, plane, flat,
            pltpu.VMEM((forward.shape[2], rows), F32),
            pltpu.VMEM(seams.shape[1:], F32), pltpu.VMEM((128, rows), F32),
            pltpu.VMEM((16, rows), F32), pltpu.VMEM((8, 8, rows), F32),
            pltpu.VMEM((2, MW, rows), F32),
            pltpu.VMEM((2, 4, 16, rows), F32),
            pltpu.VMEM((2, 2, 16, rows), F32),
            pltpu.VMEM((2, 16, rows), F32),
            pltpu.VMEM((2, 5, MW, rows), F32),
            pltpu.VMEM((2, 32, 1, rows), F32),
            pltpu.VMEM((2, 16, 1, rows), F32),
            pltpu.VMEM((2, rows), F32),
            pltpu.VMEM((2, 2, rows), F32),
            pltpu.VMEM((2, 2, 2, rows), F32),
            pltpu.VMEM((2, 2, 2, rows), F32),
            pltpu.VMEM((2, 8, rows), F32),
            pltpu.VMEM((2, 4, 8, rows), F32),
            pltpu.SemaphoreType.REGULAR((3,)), dma((2,)), dma((2, 4)), dma((2, 4)), dma((9,)), dma((3, 4)), dma((3, 4)),
            dma((2,)), dma((2,)), dma((2,)), dma((2,)),
            dma((2,)), dma((2,)), dma((2,)), dma((2,)), dma((2, 5)), dma((2, 5)),
            dma((2, 2)), dma((2, 2)),
        ],
        compiler_params=pltpu.CompilerParams(
            collective_id=0, has_side_effects=True, vmem_limit_bytes=56 * 1024 * 1024
        ),
    )(first, obs, track, land, bw, forward, inverse, row, seams)
    return surface - step[None] * search, gradient - step[None] * curved


def solution(mesh):
    in_specs = (
        P("tm", "lon", None),
        P("tm", "lon", None),
        P("tm", "lon", None),
        P("lon", None),
        P("lon", None),
    )
    out_specs = (P("tm", "lon", None), P("tm", "lon", None))
    return jax.shard_map(
        functools.partial(on_device, mesh.shape["tm"], mesh.shape["lon"]),
        mesh=mesh, in_specs=in_specs, out_specs=out_specs, check_vma=False,
    )
```

```python
import functools

import jax
import jax.numpy as jnp
import numpy as np
from jax import lax
from jax.experimental import pallas as pl
from jax.experimental.pallas import tpu as pltpu
from jax.sharding import PartitionSpec as P

CAP = 64
MW = 64
MESH = pl.DeviceIdType.MESH
OFF = 16
EXT = 8
F32 = jnp.float32


def tables(segments, length, rows):
    circle = segments * length
    harmonic = np.arange(MW)
    w = np.where(harmonic == 0, 1.0 / circle, 2.0 / circle)
    padded = -(-length // 128) * 128
    forward = np.zeros((segments, 2 * MW, padded), np.float32)
    inverse = np.zeros((segments, length + 16, 2 * MW), np.float32)
    for s in range(segments):
        a = 2 * np.pi * ((np.arange(length) + s * length)[:, None] * harmonic % circle) / circle
        forward[s, :MW, :length] = np.cos(a).T
        forward[s, MW:, :length] = np.sin(a).T
        a = 2 * np.pi * ((np.arange(length + 16) - 8 + s * length)[:, None] * harmonic % circle) / circle
        inverse[s] = np.concatenate([w * np.cos(a), w * np.sin(a)], axis=1)
    phi = (90.0 - (rows - np.arange(rows) - 0.5) * 0.125) * (np.pi / 180.0)
    bend = 1.0 / (np.cos(phi) + 0.5) ** 2
    shrink = np.zeros(rows)
    shrink[rows - CAP:] = 0.9 * (np.arange(CAP) + 1.0) / CAP
    row = np.zeros((8, rows), np.float32)
    row[0] = bend
    row[1] = -2.0 * (bend + 1.0)
    row[2] = shrink
    row[3] = 1.0 - shrink
    seams = np.zeros((4, 32, 128), np.float32)
    for i, offset in enumerate((0, 1, -1, -2)):
        place = (np.arange(segments) + 1) * length + offset
        a = 2 * np.pi * (place[None, :] * harmonic[:, None] % circle) / circle
        for q in range(4):
            seams[q, :16, 8 * i:8 * i + 8] = np.cos(a[16 * q:16 * q + 16])
            seams[q, 16:, 8 * i:8 * i + 8] = np.sin(a[16 * q:16 * q + 16])
    return forward, inverse, row, seams


def kernel(
    NT, N, first_ref, obs_ref, track_ref, land_ref, bw_ref, fwd_ref, inv_ref, row_hbm, seams_hbm,
    out_a, out_s, out_g, out_c, out_step,
    row_ref, E, G, U, B, W, obs, track, land, fwd, inv, V, TV, T2V, Y, V0, LV0, padded, seams, seam_rows, seam_amp, ED, three, amp3, rs3, sum3, day3, amp, rs_buf, quarter,
    z_buf, AT, dots_a, dots_b, ts, tr, ls, lr, bs, br,
    hello, fs, fr, sems, bsem, brem, lsem, hs, hr, es, er, rs_, rr, xs, xr, zs, zr, ats, atr, ds_, dr,
):
    tm = lax.axis_index("tm")
    lon = lax.axis_index("lon")
    x, zh = lon // 2, lon % 2
    zl, k = tm // 8, tm % 8
    rows = 128

    def inside(t):
        return (t >= 0) & (t < NT)

    def when_t(dt, fn):
        if dt == 0:
            fn()
        else:
            pl.when(inside(tm + dt))(fn)

    def lon_at(d):
        return lax.rem(lon + d + 8, 8)

    own = pl.ds(OFF, N)
    loads = [
        pltpu.make_async_copy(first_ref.at[0], E.at[2, own], lsem.at[0]),
        pltpu.make_async_copy(bw_ref, B.at[own], lsem.at[1]),
        pltpu.make_async_copy(obs_ref.at[0], obs, lsem.at[2]),
        pltpu.make_async_copy(track_ref.at[0], track, lsem.at[3]),
        pltpu.make_async_copy(land_ref, land, lsem.at[4]),
        pltpu.make_async_copy(fwd_ref.at[lon], fwd, lsem.at[5]),
        pltpu.make_async_copy(inv_ref.at[lon], inv, lsem.at[6]),
        pltpu.make_async_copy(row_hbm, row_ref, lsem.at[7]),
        pltpu.make_async_copy(seams_hbm.at[x], seams, lsem.at[8]),
    ]
    loads[0].start()
    loads[7].start()

    barrier = pltpu.get_barrier_semaphore()

    def greet(t, l, sem=barrier):
        pl.semaphore_signal(sem, inc=1, device_id={"tm": t, "lon": l}, device_id_type=MESH)

    z = zh * 8 + zl

    def on_z(place, xx):
        place = lax.rem(place + 16, 16)
        return lax.rem(place, 8) * 8 + k, xx * 2 + place // 8

    for dz in (2, -2, 1, -1):
        greet(*on_z(z + dz, x))
    for d in range(1, 8):
        greet(zl * 8 + lax.rem(k + d, 8), lon)
    for d in range(1, 4):
        greet(tm, lon_at(2 * d))
    count = jnp.int32(4 + 7 + 3)
    for dt in (-2, -1, 1, 2):
        when_t(dt, lambda dt=dt: greet(tm + dt, lon))
        count = count + jnp.where(inside(tm + dt), 1, 0)
    for c in loads[1:7] + loads[8:]:
        c.start()

    for dt in (-2, -1, 1, 2):

        @pl.when(jnp.logical_not(inside(tm + dt)))
        def _(dt=dt):
            for X in (E, G, U):
                X[2 + dt] = jnp.zeros(X.shape[1:], F32)
            for p in range(2):
                AT[p, 2 + dt] = jnp.zeros(AT.shape[2:], F32)
            if abs(dt) == 1:
                tr[(dt + 1) // 2] = jnp.zeros(tr.shape[1:], F32)
            day3[2 + dt] = jnp.zeros(day3.shape[1:], F32)

    seam_rows[...] = jnp.zeros(seam_rows.shape, F32)
    bs[...] = jnp.zeros(bs.shape, F32)
    three[pl.ds(N, three.shape[0] - N)] = jnp.zeros((three.shape[0] - N, 3 * rows), F32)
    padded[pl.ds(N, padded.shape[0] - N)] = jnp.zeros((padded.shape[0] - N, rows), F32)

    lane = lax.broadcasted_iota(jnp.int32, (8, rows), 1)
    first_lane, last_lane = lane[:1] == 0, lane[:1] == rows - 1
    loads[7].wait()
    bend = row_ref[0:1]
    centre = row_ref[1:2]
    shrink = row_ref[2:3]
    keep = row_ref[3:4]

    def flat(ref, start, n):
        v = ref[pl.ds(start, n)]
        up, down = ref[pl.ds(start + 1, n)], ref[pl.ds(start - 1, n)]
        lo = jnp.where(first_lane, 0.0, pltpu.roll(v, 1, axis=1))
        hi = jnp.where(last_lane, 0.0, pltpu.roll(v, rows - 1, axis=1))
        return bend * (up + down) + (lo + hi) + centre * v

    own_chunks = [(OFF + c, 72) for c in range(0, N, 72)]
    ext_chunks = [(EXT, 8)] + own_chunks + [(OFF + N, 8)]
    centre_t2 = jnp.where((tm == 0) | (tm == NT - 1), 5.0, 6.0).astype(F32)

    def second(a, b, c):
        return a + b - 2.0 * c

    def second2(a, b, c, d, e):
        return a + e - 4.0 * (b + d) + centre_t2 * c

    half = lax.broadcasted_iota(jnp.int32, (MW, rows), 1) < MW

    beside = ((OFF - 1, OFF - 2), (OFF + N, OFF + N + 1))
    for c in loads[:6]:
        c.wait()
    W[...] = track[...].astype(F32) * (1.0 - land[...].astype(F32))
    for near, _ in beside:
        for ref in (E.at[2], TV, Y):
            ref[near:near + 1] = jnp.zeros((1, rows), F32)
    for s, n in own_chunks:
        r = pl.ds(s, n)
        TV[r] = B[r] * E[2, r]
        Y[r] = B[r] * flat(E.at[2], s, n)
    for s, n in own_chunks:
        l, r = pl.ds(s - OFF, n), pl.ds(s, n)
        three[l, 0:rows] = W[l] * (E[2, r] - obs[l]) + flat(Y, s, n)
        three[l, rows:2 * rows] = Y[r] + flat(TV, s, n)
        three[l, 2 * rows:3 * rows] = TV[r]
    parts = lax.dot(fwd[...], three[...], precision=lax.Precision.HIGH, preferred_element_type=F32)
    for f in range(3):
        part = parts[:, f * rows:(f + 1) * rows]
        part = jnp.where(half, pltpu.roll(part[:MW], MW, axis=1), part[MW:])
        for q in range(4):
            amp3[q, 16 * f:16 * f + 16] = part[16 * q:16 * q + 16]

    with jax.named_scope("entry barrier"):
        pl.semaphore_wait(barrier, count)
    for dz in (2, -2):
        greet(*on_z(z + dz, x), sem=hello.at[0])

    def remote(src, dst, send, recv, t, l):
        return pltpu.make_async_remote_copy(
            src_ref=src, dst_ref=dst, send_sem=send, recv_sem=recv,
            device_id={"tm": t, "lon": l}, device_id_type=MESH,
        )

    side = 1 - 2 * lax.rem(tm, 2)
    send_days = (-side, 2 * side, side)
    recv_days = (-side, -2 * side, side, 2 * side)

    def plane_copy(p, X, i):
        dt = send_days[i]
        return remote(X.at[2, own], X.at[2 - dt, own], hs.at[p, i], hr.at[p, i], tm + dt, lon)

    def hand_copy(p, X):
        return remote(X.at[2 - side, own], X.at[2 - 2 * side, own], hs.at[p, 3], hr.at[p, 3], tm + side, lon)

    def plane_recv(p, X, i):
        return remote(X.at[2, own], X.at[2 + recv_days[i], own], hs.at[p, i], hr.at[p, i], tm, lon)

    def halo_send(p, X):
        for i in range(3):
            pl.when(inside(tm + send_days[i]))(lambda i=i: plane_copy(p, X, i).start())

    def halo_hand(p, X):
        @pl.when(inside(tm - side))
        def _():
            plane_recv(p, X, 0).wait_recv()
            hand_copy(p, X).start()

    def halo_wait(p, X):
        for i in (1, 2, 3):
            pl.when(inside(tm + recv_days[i]))(lambda i=i: plane_recv(p, X, i).wait_recv())
        pl.when(inside(tm - side))(lambda: hand_copy(p, X).wait_send())

    def halo_done(p, X):
        for i in range(3):
            pl.when(inside(tm + send_days[i]))(lambda i=i: plane_copy(p, X, i).wait_send())

    first_row, last_row = OFF, OFF + N - 1

    def edge_copy(i):
        return remote(ts, tr.at[i], es.at[i], er.at[i], tm + (1, -1)[i], lon)

    def edge_send():
        ts[0:1] = E[2, first_row:first_row + 1]
        ts[1:2] = E[2, last_row:last_row + 1]
        for i, dt in enumerate((1, -1)):
            when_t(dt, lambda i=i: edge_copy(i).start())

    def seam_copy(l):
        return remote(ED.at[lon], ED.at[lon], sems.at[0], sems.at[1], tm, l)

    def seam_all():
        return remote(ED.at[pl.ds(0, 7)], ED.at[pl.ds(0, 7)], sems.at[0], sems.at[1], tm, lon)

    def seam_fill():
        for i, dt in enumerate((1, -1)):
            when_t(-dt, lambda i=i: edge_copy(i).wait_recv())
        bent = tr[0] + tr[1] - 2.0 * ts[...]
        for at, row, inner, side_row in ((0, first_row, first_row + 1, 0), (4, last_row, last_row - 1, 1)):
            ED[lon, at:at + 1] = E[2, row:row + 1]
            ED[lon, at + 1:at + 2] = E[2, inner:inner + 1]
            ED[lon, at + 2:at + 3] = bent[side_row:side_row + 1]
            ED[lon, at + 3:at + 4] = B[row:row + 1]

    def far_lon(d):
        return lax.rem(x + d, 4) * 2 + 1 - zh

    def rim_copy(p, j):
        return remote(ls.at[p, j], lr.at[p, j], rs_.at[p], rr.at[p], tm, lon_at((1, -1)[j]))

    def rim_all(p):
        return remote(lr.at[p], lr.at[p], rs_.at[p], rr.at[p], tm, lon)

    def rim_send(p, X):
        ls[p, 0, 0:1] = X[2, last_row:last_row + 1]
        ls[p, 0, 1:2] = X[2, last_row - 1:last_row]
        ls[p, 1, 0:1] = X[2, first_row:first_row + 1]
        ls[p, 1, 1:2] = X[2, first_row + 1:first_row + 2]
        for j in range(2):
            rim_copy(p, j).start()

    before = lon_at(-1)

    def rim_take(p, X):
        rim_all(p).wait_recv()
        for j, (near, far) in enumerate(beside):
            for i, row in enumerate((near, far)):
                line = lr[p, j, i:i + 1]
                if p == 0:
                    line = line + seam_rows[pl.ds((16, 0)[j] + 8 * i + (before, lon)[j], 1)]
                X[2, row:row + 1] = line

    border_rows = (first_row, first_row + 1, last_row - 1, last_row, first_row - 1, last_row + 1)
    border_days = (2, -2, 1, -1)

    def border_copy(p, i):
        return remote(bs.at[p], br.at[p, i], bsem.at[p, i], brem.at[p, i], tm + border_days[i], lon)

    def border_send(p, X):
        for i, row in enumerate(border_rows):
            bs[p, i:i + 1] = X[2, row:row + 1]
        for i, dt in enumerate(border_days):
            when_t(dt, lambda i=i: border_copy(p, i).start())

    def border_take(p, X):
        for i, dt in enumerate(border_days):

            def take(i=i, dt=dt):
                border_copy(p, i).wait_recv()
                for j, row in enumerate(border_rows[:6 if abs(dt) == 1 else 4]):
                    X[2 - dt, row:row + 1] = br[p, i, j:j + 1]

            when_t(-dt, take)

    def border_done(p):
        for i, dt in enumerate(border_days):
            when_t(dt, lambda i=i: border_copy(p, i).wait_send())

    def first_copy(d):
        q = lax.rem(x + d, 4)
        return remote(amp3.at[q], rs3.at[d], xs.at[0], xr.at[0], tm, q * 2 + zh)

    def first_all():
        return remote(rs3.at[pl.ds(1, 3)], rs3.at[pl.ds(1, 3)], xs.at[0], xr.at[0], tm, lon)

    first_days = (2, -2, 1, -1)

    def first_day_copy(i):
        dt = first_days[i]
        some = pl.ds(16, 32) if abs(dt) == 1 else pl.ds(32, 16)
        return remote(sum3.at[some], day3.at[2 - dt, some], fs.at[i], fr.at[i], tm + dt, lon)

    def first_sum():
        first_all().wait_recv()
        sum3[...] = amp3[x] + rs3[1] + rs3[2] + rs3[3]
        for i, dt in enumerate(first_days):
            when_t(dt, lambda i=i: first_day_copy(i).start())

    def first_cross():
        for i, dt in enumerate(first_days):
            when_t(-dt, lambda i=i: first_day_copy(i).wait_recv())
        one, two = pl.ds(16, 16), pl.ds(32, 16)
        quarter[0, 0] = (
            sum3[0:16]
            + second(day3[1, one], day3[3, one], sum3[one])
            + second2(day3[0, two], day3[1, two], sum3[two], day3[3, two], day3[4, two])
        )
        z_copy(0).start()

    def first_done():
        first_all().wait_send()
        for i, dt in enumerate(first_days):
            when_t(dt, lambda i=i: first_day_copy(i).wait_send())
        z_copy(0).wait_send()

    def z_copy(p):
        return remote(quarter.at[p, 0], z_buf.at[p], zs.at[p], zr.at[p], tm, lon + 1 - 2 * zh)

    with jax.named_scope("first amplitudes"):
        for d in (2, 1, 3):
            first_copy(d).start()
    with jax.named_scope("guess edges"):
        edge_send()
        halo_send(0, E)
    with jax.named_scope("far hello"):
        pl.semaphore_wait(hello.at[0], 2)
        for dz in (4, -4):
            greet(*on_z(z + dz, x), sem=hello.at[1])
    with jax.named_scope("guess seams"):
        seam_fill()
        for d in (2, 1, 3):
            seam_copy(lon_at(2 * d)).start()
    with jax.named_scope("first sum"):
        first_sum()
    with jax.named_scope("guess far seam"):
        pl.semaphore_wait(hello.at[1], 2)
        for d in (2, 1, 3):
            greet(tm, lon_at(2 * d), sem=hello.at[2])
        seam_copy(far_lon(0)).start()
    with jax.named_scope("guess hand on"):
        halo_hand(0, E)
    with jax.named_scope("guess far seams"):
        pl.semaphore_wait(hello.at[2], 3)
        for d in (2, 1, 3):
            seam_copy(far_lon(d)).start()
    with jax.named_scope("first cross"):
        first_cross()

    def flatten(field):
        for s, n in ext_chunks:
            Y[pl.ds(s, n)] = flat(field, s, n)

    def once(emit=None):
        for s, n in ext_chunks:
            full = TV[pl.ds(s, n)] + Y[pl.ds(s, n)]
            Y[pl.ds(s, n)] = B[pl.ds(s, n)] * full
            if emit is not None and OFF <= s < OFF + N:
                emit(s, n, full)

    def twice(emit):
        for s, n in own_chunks:
            emit(s, n, B[pl.ds(s, n)] * (T2V[pl.ds(s, n)] + flat(TV, s, n)) + flat(Y, s, n))

    with jax.named_scope("guess halo wait"):
        halo_wait(0, E)
    for s, n in ext_chunks:
        r = pl.ds(s, n)
        TV[r] = second(E[1, r], E[3, r], E[2, r])
    for near, _ in beside:
        TV[near:near + 1] = jnp.zeros((1, rows), F32)
    for s, n in own_chunks:
        r = pl.ds(s, n)
        T2V[r] = second2(E[0, r], E[1, r], E[2, r], E[3, r], E[4, r])

    def emit_g(s, n, u):
        l = pl.ds(s - OFF, n)
        g = W[l] * (E[2, pl.ds(s, n)] - obs[l]) + u
        G[2, pl.ds(s, n)] = g

    with jax.named_scope("first operator"):
        for near, _ in beside:
            E[2, near:near + 1] = jnp.zeros((1, rows), F32)
        flatten(E.at[2])
        once()
        for near, _ in beside:
            Y[near:near + 1] = jnp.zeros((1, rows), F32)
        twice(emit_g)
    for c in loads[6:7] + loads[8:]:
        c.wait()

    def rs_copy(p, d):
        q = lax.rem(x + d, 4)
        return remote(amp.at[p, pl.ds(16 * q, 16)], rs_buf.at[p, d], xs.at[p], xr.at[p], tm, q * 2 + zh)

    def rs_all(p):
        return remote(rs_buf.at[p, pl.ds(1, 3)], rs_buf.at[p, pl.ds(1, 3)], xs.at[p], xr.at[p], tm, lon)

    days = (2, -2, 1, -1, 0)

    def at_copy(p, i, d):
        dt = days[i]
        xx = lax.rem(x + d, 4)
        return remote(
            quarter.at[p, 1], AT.at[p, 2 - dt, pl.ds(16 * x, 16)], ats.at[p, i], atr.at[p, i], tm + dt, xx * 2 + zh
        )

    def at_all(p, i):
        some = AT.at[p, 2 - days[i], pl.ds(0, MW if days[i] else MW - 16)]
        return remote(some, some, ats.at[p, i], atr.at[p, i], tm, lon)

    half16 = lax.broadcasted_iota(jnp.int32, (16, rows), 1) < MW

    def seam_take():
        seam_all().wait_recv()
        er1, er2, ter, ber = (pltpu.roll(ED[:, i, :], 7, axis=0) for i in range(4))
        el1, el2, tel, bel = (ED[:, i, :] for i in range(4, 8))

        def across(v):
            lo = jnp.where(first_lane, 0.0, pltpu.roll(v, 1, axis=1))
            hi = jnp.where(last_lane, 0.0, pltpu.roll(v, rows - 1, axis=1))
            return lo + hi - 2.0 * v

        yl = bel * (tel + across(el1) + bend * (el2 + er1 - 2.0 * el1))
        yr = ber * (ter + across(er1) + bend * (er2 + el1 - 2.0 * er1))
        dr_, dl_ = ber * bend * el1, bel * bend * er1
        seam_rows[0:8] = bend * (yl + ber * tel - 2.0 * dr_) + across(dr_)
        seam_rows[8:16] = bend * dr_
        seam_rows[16:24] = bend * (yr + bel * ter - 2.0 * dl_) + across(dl_)
        seam_rows[24:32] = bend * dl_
        for row, place in (
            (first_row, before), (first_row + 1, 8 + before), (last_row, 16 + lon), (last_row - 1, 24 + lon)
        ):
            G[2, row:row + 1] += seam_rows[pl.ds(place, 1)]
        B[first_row - 1:first_row] = ED[before, 7:8]
        B[last_row + 1:last_row + 2] = ED[lon_at(1), 3:4]
        part = lax.dot(seams[...], seam_rows[...], precision=lax.Precision.HIGH, preferred_element_type=F32)
        seam_amp[...] = jnp.where(half16, pltpu.roll(part[:16], MW, axis=1), part[16:])

    def transform_start(p):
        part = lax.dot(fwd[...], padded[...], precision=lax.Precision.HIGH, preferred_element_type=F32)
        amp[p] = jnp.where(half, pltpu.roll(part[:MW], MW, axis=1), part[MW:])
        for d in (2, 1, 3):
            rs_copy(p, d).start()

    def transform_cross(p):
        total = amp[p, pl.ds(16 * x, 16)]
        rs_all(p).wait_recv()
        for d in (1, 2, 3):
            total = total + rs_buf[p, d]
        quarter[p, 0] = total
        z_copy(p).start()

    def transform_spread(p):
        z_copy(p).wait_recv()
        total = quarter[p, 0] + z_buf[p]
        if p == 0:
            total = total + seam_amp[...]
        quarter[p, 1] = total
        for i, dt in enumerate(days):
            for d in (2, 1, 3, 0) if dt else (2, 1, 3):
                when_t(dt, lambda i=i, d=d: at_copy(p, i, d).start())
        AT[p, 2, pl.ds(16 * x, 16)] = total

    def transform_finish(p, some):
        for i, dt in enumerate(days):
            if dt in some:
                when_t(-dt, lambda i=i: at_all(p, i).wait_recv())

    def transform_done(p):
        if p == 1:
            rs_all(p).wait_send()
            z_copy(p).wait_send()
        for i, dt in enumerate(days):
            when_t(dt, lambda i=i: at_all(p, i).wait_send())

    def stack(a):
        return jnp.concatenate([pltpu.roll(a, MW, axis=1), a], axis=0) * shrink

    def synthesis(s, n, amplitudes):
        return lax.dot(
            inv[pl.ds(s - EXT, n)], amplitudes, precision=lax.Precision.HIGH, preferred_element_type=F32
        )

    def filter_local(X, field):
        for s, n in ext_chunks:
            r = pl.ds(s, n)
            field[r] = keep * X[2, r]
            TV[r] = keep * second(X[1, r], X[3, r], X[2, r])
            T2V[r] = keep * second2(X[0, r], X[1, r], X[2, r], X[3, r], X[4, r])

    def filter_own(p, field):
        amplitudes = stack(AT[p, 2])
        for s, n in ext_chunks:
            field[pl.ds(s, n)] += synthesis(s, n, amplitudes)
        flatten(field)

    def filter_days(p):
        a = [AT[p, i] for i in range(5)]
        amplitudes = jnp.concatenate([stack(second(a[1], a[3], a[2])), stack(second2(*a))], axis=1)
        for s, n in ext_chunks:
            smooth = synthesis(s, n, amplitudes)
            TV[pl.ds(s, n)] += smooth[:, :rows]
            T2V[pl.ds(s, n)] += smooth[:, rows:]

    sizes = (32, 16)

    def stage_place(stage):
        return (x * 8 + k, z)[stage]

    def stage_device(stage, place):
        if stage == 0:
            return zl * 8 + lax.rem(place, 8), (place // 8) * 2 + zh
        return on_z(place, x)

    def dot_slots(stage):
        return (dots_a, dots_b)[stage]

    def dot_copy(p, stage, d):
        size, mine, slots = sizes[stage], stage_place(stage), dot_slots(stage)
        if stage == 0:
            other = lax.rem(x + d // 8, 4) * 8 + lax.rem(k + d % 8, 8)
        else:
            other = lax.rem(mine + d, size)
        t, l = stage_device(stage, other)
        slot = slots.at[p, mine]
        return remote(slot, slot, ds_.at[p, stage], dr.at[p, stage], t, l)

    def dot_all(p, stage):
        some = dot_slots(stage).at[p, pl.ds(0, sizes[stage] - 1)]
        return remote(some, some, ds_.at[p, stage], dr.at[p, stage], tm, lon)

    steps = (
        [8 * dx + dk for dx in (2, 1, 3, 0) for dk in (4, 3, 5, 2, 6, 1, 7, 0)][:-1],
        [8, 7, 9, 6, 10, 5, 11, 4, 12, 3, 13, 2, 14, 1, 15],
    )

    def dot_send(p, stage, line):
        dot_slots(stage)[p, stage_place(stage)] = line
        for d in steps[stage]:
            dot_copy(p, stage, d).start()

    def dot_take(p, stage):
        dot_all(p, stage).wait_recv()
        total = dot_slots(stage)[p, 0]
        for i in range(1, sizes[stage]):
            total = total + dot_slots(stage)[p, i]
        return total

    def dot_done(p):
        for stage in range(2):
            dot_all(p, stage).wait_send()

    low = lane[:1] < MW

    def pack(slope, curve):
        return jnp.where(low, slope + pltpu.roll(slope, MW, axis=1), curve + pltpu.roll(curve, MW, axis=1))

    def ratio(line):
        slope = jnp.sum(jnp.where(low, line, 0.0), axis=1, keepdims=True)
        return slope / jnp.sum(jnp.where(low, 0.0, line), axis=1, keepdims=True)

    with jax.named_scope("rim one send"):
        rim_send(0, G)
    with jax.named_scope("halo one send"):
        halo_send(1, G)
    with jax.named_scope("seams"):
        halo_done(1, G)
        seam_take()
    with jax.named_scope("rim one wait"):
        rim_take(0, G)
    with jax.named_scope("border one send"):
        border_send(0, G)
    with jax.named_scope("hand on one"):
        halo_hand(1, G)
    with jax.named_scope("spread zero"):
        transform_spread(0)
    with jax.named_scope("halo one wait"):
        halo_wait(1, G)
        border_take(0, G)
    with jax.named_scope("filter zero local"):
        filter_local(G, V0)
    with jax.named_scope("finish zero"):
        transform_finish(0, (0,))
    with jax.named_scope("filter zero own"):
        filter_own(0, V0)
    with jax.named_scope("finish zero days"):
        transform_finish(0, (1, -1, 2, -2))
    with jax.named_scope("filter zero days"):
        filter_days(0)
    acc = [jnp.zeros((1, rows), F32), jnp.zeros((1, rows), F32)]

    def emit_first(s, n, full):
        LV0[pl.ds(s - OFF, n)] = full

    def emit_u(s, n, u):
        l, r = pl.ds(s - OFF, n), pl.ds(s, n)
        v = V0[r]
        u = W[l] * v + u
        U[2, r] = u
        padded[l] = u
        acc[0] = acc[0] + jnp.sum(G[2, r] * v, axis=0, keepdims=True)
        acc[1] = acc[1] + jnp.sum(v * u, axis=0, keepdims=True)

    with jax.named_scope("operator one"):
        once(emit_first)
        twice(emit_u)

    with jax.named_scope("transform one"):
        transform_start(1)
    with jax.named_scope("edges two send"):
        dot_send(0, 0, pack(*acc))
    with jax.named_scope("rim two send"):
        rim_send(1, U)
    with jax.named_scope("halo two send"):
        halo_send(2, U)
    with jax.named_scope("cross one"):
        transform_cross(1)
    with jax.named_scope("sums zero"):
        dot_send(0, 1, dot_take(0, 0))
    with jax.named_scope("rim two wait"):
        rim_take(1, U)
    with jax.named_scope("border two send"):
        border_send(1, U)
    with jax.named_scope("hand on two"):
        halo_hand(2, U)
    with jax.named_scope("spread one"):
        transform_spread(1)
    with jax.named_scope("halo two wait"):
        halo_wait(2, U)
        border_take(1, U)
    with jax.named_scope("filter one local"):
        filter_local(U, V)
    with jax.named_scope("finish one"):
        transform_finish(1, (0,))
    with jax.named_scope("filter one own"):
        filter_own(1, V)
    with jax.named_scope("step zero"):
        step0 = ratio(dot_take(0, 1))
    with jax.named_scope("finish one days"):
        transform_finish(1, (1, -1, 2, -2))
    with jax.named_scope("filter one days"):
        filter_days(1)
    acc[0] = acc[1] = jnp.zeros((1, rows), F32)

    def emit_sums(s, n, full):
        l, r = pl.ds(s - OFF, n), pl.ds(s, n)
        search = V0[r] - step0 * V[r]
        gradient = G[2, r] - step0 * U[2, r]
        bent = LV0[l] - step0 * full
        acc[0] = acc[0] + jnp.sum(gradient * search, axis=0, keepdims=True)
        acc[1] = acc[1] + jnp.sum(W[l] * (search * search) + B[r] * (bent * bent), axis=0, keepdims=True)
        out_s[0, l] = search
        out_g[0, l] = gradient

    with jax.named_scope("operator two once"):
        once(emit_sums)
    with jax.named_scope("sums one a"):
        dot_send(1, 0, pack(*acc))

    def emit_last(s, n, u1):
        l, r = pl.ds(s - OFF, n), pl.ds(s, n)
        out_c[0, l] = U[2, r] - step0 * (W[l] * V[r] + u1)
        out_a[0, l] = E[2, r] - step0 * V0[r]

    with jax.named_scope("operator two twice"):
        twice(emit_last)
    with jax.named_scope("sums one b"):
        dot_send(1, 1, dot_take(1, 0))
    halo_done(0, E)
    halo_done(2, U)
    for i, dt in enumerate((1, -1)):
        when_t(dt, lambda i=i: edge_copy(i).wait_send())
    seam_all().wait_send()
    first_done()
    for p in range(2):
        transform_done(p)
        rim_all(p).wait_send()
        border_done(p)
    dot_done(0)
    with jax.named_scope("sums one c"):
        out_step[...] = jnp.broadcast_to(ratio(dot_take(1, 1)), out_step.shape)
    with jax.named_scope("drain"):
        dot_done(1)


def on_device(NT, NL, first, obs, track, land, bw):
    _, N, rows = first.shape
    forward, inverse, row, seams = tables(NL, N, rows)
    plane = pltpu.VMEM((N + 32, rows), F32)
    planes = pltpu.VMEM((5, N + 32, rows), F32)
    flat = pltpu.VMEM((N, rows), F32)
    whole = pltpu.VMEM((N, rows), jnp.int32)
    dma = pltpu.SemaphoreType.DMA
    hbm = pl.BlockSpec(memory_space=pltpu.HBM)
    surface, search, gradient, curved, step = pl.pallas_call(
        functools.partial(kernel, NT, N),
        out_shape=[pltpu.VMEM(first.shape, F32)] * 4 + [pltpu.VMEM((1, rows), F32)],
        in_specs=[hbm] * 9,
        out_specs=[pl.BlockSpec(memory_space=pltpu.VMEM)] * 5,
        scratch_shapes=[
            pltpu.VMEM(row.shape, F32), planes, planes, planes,
            plane, flat, flat, whole, whole,
            pltpu.VMEM(forward.shape[1:], F32), pltpu.VMEM(inverse.shape[1:], F32),
            plane, plane, plane, plane, plane, flat,
            pltpu.VMEM((forward.shape[2], rows), F32),
            pltpu.VMEM(seams.shape[1:], F32), pltpu.VMEM((128, rows), F32),
            pltpu.VMEM((16, rows), F32), pltpu.VMEM((8, 8, rows), F32),
            pltpu.VMEM((forward.shape[2], 3 * rows), F32),
            pltpu.VMEM((4, 48, rows), F32), pltpu.VMEM((4, 48, rows), F32),
            pltpu.VMEM((48, rows), F32), pltpu.VMEM((5, 48, rows), F32),
            pltpu.VMEM((2, MW, rows), F32),
            pltpu.VMEM((2, 4, 16, rows), F32),
            pltpu.VMEM((2, 2, 16, rows), F32),
            pltpu.VMEM((2, 16, rows), F32),
            pltpu.VMEM((2, 5, MW, rows), F32),
            pltpu.VMEM((2, 32, 1, rows), F32),
            pltpu.VMEM((2, 16, 1, rows), F32),
            pltpu.VMEM((2, rows), F32),
            pltpu.VMEM((2, 2, rows), F32),
            pltpu.VMEM((2, 2, 2, rows), F32),
            pltpu.VMEM((2, 2, 2, rows), F32),
            pltpu.VMEM((2, 8, rows), F32),
            pltpu.VMEM((2, 4, 8, rows), F32),
            pltpu.SemaphoreType.REGULAR((3,)), dma((4,)), dma((4,)), dma((2,)), dma((2, 4)), dma((2, 4)), dma((9,)), dma((3, 4)), dma((3, 4)),
            dma((2,)), dma((2,)), dma((2,)), dma((2,)),
            dma((2,)), dma((2,)), dma((2,)), dma((2,)), dma((2, 5)), dma((2, 5)),
            dma((2, 2)), dma((2, 2)),
        ],
        compiler_params=pltpu.CompilerParams(
            collective_id=0, has_side_effects=True, vmem_limit_bytes=56 * 1024 * 1024
        ),
    )(first, obs, track, land, bw, forward, inverse, row, seams)
    return surface - step[None] * search, gradient - step[None] * curved


def solution(mesh):
    in_specs = (
        P("tm", "lon", None),
        P("tm", "lon", None),
        P("tm", "lon", None),
        P("lon", None),
        P("lon", None),
    )
    out_specs = (P("tm", "lon", None), P("tm", "lon", None))
    return jax.shard_map(
        functools.partial(on_device, mesh.shape["tm"], mesh.shape["lon"]),
        mesh=mesh, in_specs=in_specs, out_specs=out_specs, check_vma=False,
    )
```

```python
import functools

import jax
import jax.numpy as jnp
import numpy as np
from jax import lax
from jax.experimental import pallas as pl
from jax.experimental.pallas import tpu as pltpu
from jax.sharding import PartitionSpec as P

CAP = 64
MW = 64
MESH = pl.DeviceIdType.MESH
OFF = 16
EXT = 8
F32 = jnp.float32


def tables(segments, length, rows):
    circle = segments * length
    harmonic = np.arange(MW)
    w = np.where(harmonic == 0, 1.0 / circle, 2.0 / circle)
    padded = -(-length // 128) * 128
    forward = np.zeros((segments, 2 * MW, padded), np.float32)
    inverse = np.zeros((segments, length + 16, 2 * MW), np.float32)
    for s in range(segments):
        a = 2 * np.pi * ((np.arange(length) + s * length)[:, None] * harmonic % circle) / circle
        forward[s, :MW, :length] = np.cos(a).T
        forward[s, MW:, :length] = np.sin(a).T
        a = 2 * np.pi * ((np.arange(length + 16) - 8 + s * length)[:, None] * harmonic % circle) / circle
        inverse[s] = np.concatenate([w * np.cos(a), w * np.sin(a)], axis=1)
    phi = (90.0 - (rows - np.arange(rows) - 0.5) * 0.125) * (np.pi / 180.0)
    bend = 1.0 / (np.cos(phi) + 0.5) ** 2
    shrink = np.zeros(rows)
    shrink[rows - CAP:] = 0.9 * (np.arange(CAP) + 1.0) / CAP
    row = np.zeros((8, rows), np.float32)
    row[0] = bend
    row[1] = -2.0 * (bend + 1.0)
    row[2] = shrink
    row[3] = 1.0 - shrink
    seams = np.zeros((4, 32, 128), np.float32)
    for i, offset in enumerate((0, 1, -1, -2)):
        place = (np.arange(segments) + 1) * length + offset
        a = 2 * np.pi * (place[None, :] * harmonic[:, None] % circle) / circle
        for q in range(4):
            seams[q, :16, 8 * i:8 * i + 8] = np.cos(a[16 * q:16 * q + 16])
            seams[q, 16:, 8 * i:8 * i + 8] = np.sin(a[16 * q:16 * q + 16])
    return forward, inverse, row, seams


def kernel(
    NT, N, first_ref, obs_ref, track_ref, land_ref, bw_ref, fwd_ref, inv_ref, row_hbm, seams_hbm,
    out_a, out_s, out_g, out_c, out_step,
    row_ref, E, G, U, B, W, obs, track, land, fwd, inv, V, TV, T2V, Y, V0, LV0, padded, seams, seam_rows, seam_amp, ED, three, amp3, rs3, sum3, day3, amp, rs_buf, quarter,
    z_buf, AT, dots_a, dots_b, ts, tr, ls, lr, bs, br,
    hello, fs, fr, sems, bsem, brem, lsem, hs, hr, es, er, rs_, rr, xs, xr, zs, zr, ats, atr, ds_, dr,
):
    tm = lax.axis_index("tm")
    lon = lax.axis_index("lon")
    x, zh = lon // 2, lon % 2
    zl, k = tm // 8, tm % 8
    rows = 128

    def inside(t):
        return (t >= 0) & (t < NT)

    def when_t(dt, fn):
        if dt == 0:
            fn()
        else:
            pl.when(inside(tm + dt))(fn)

    def lon_at(d):
        return lax.rem(lon + d + 8, 8)

    own = pl.ds(OFF, N)
    loads = [
        pltpu.make_async_copy(first_ref.at[0], E.at[2, own], lsem.at[0]),
        pltpu.make_async_copy(bw_ref, B.at[own], lsem.at[1]),
        pltpu.make_async_copy(obs_ref.at[0], obs, lsem.at[2]),
        pltpu.make_async_copy(track_ref.at[0], track, lsem.at[3]),
        pltpu.make_async_copy(land_ref, land, lsem.at[4]),
        pltpu.make_async_copy(fwd_ref.at[lon], fwd, lsem.at[5]),
        pltpu.make_async_copy(inv_ref.at[lon], inv, lsem.at[6]),
        pltpu.make_async_copy(row_hbm, row_ref, lsem.at[7]),
        pltpu.make_async_copy(seams_hbm.at[x], seams, lsem.at[8]),
    ]
    loads[0].start()
    loads[7].start()

    barrier = pltpu.get_barrier_semaphore()

    def greet(t, l, sem=barrier):
        pl.semaphore_signal(sem, inc=1, device_id={"tm": t, "lon": l}, device_id_type=MESH)

    z = zh * 8 + zl

    def on_z(place, xx):
        place = lax.rem(place + 16, 16)
        return lax.rem(place, 8) * 8 + k, xx * 2 + place // 8

    for dz in (2, -2, 1, -1):
        greet(*on_z(z + dz, x))
    for d in range(1, 8):
        greet(zl * 8 + lax.rem(k + d, 8), lon)
    for d in range(1, 4):
        greet(tm, lon_at(2 * d))
    count = jnp.int32(4 + 7 + 3)
    for dt in (-2, -1, 1, 2):
        when_t(dt, lambda dt=dt: greet(tm + dt, lon))
        count = count + jnp.where(inside(tm + dt), 1, 0)
    for c in loads[1:7] + loads[8:]:
        c.start()

    for dt in (-2, -1, 1, 2):

        @pl.when(jnp.logical_not(inside(tm + dt)))
        def _(dt=dt):
            for X in (E, G, U):
                X[2 + dt] = jnp.zeros(X.shape[1:], F32)
            for p in range(2):
                AT[p, 2 + dt] = jnp.zeros(AT.shape[2:], F32)
            if abs(dt) == 1:
                tr[(dt + 1) // 2] = jnp.zeros(tr.shape[1:], F32)
            day3[2 + dt] = jnp.zeros(day3.shape[1:], F32)

    seam_rows[...] = jnp.zeros(seam_rows.shape, F32)
    bs[...] = jnp.zeros(bs.shape, F32)
    three[pl.ds(N, three.shape[0] - N)] = jnp.zeros((three.shape[0] - N, 3 * rows), F32)
    padded[pl.ds(N, padded.shape[0] - N)] = jnp.zeros((padded.shape[0] - N, rows), F32)

    lane = lax.broadcasted_iota(jnp.int32, (8, rows), 1)
    first_lane, last_lane = lane[:1] == 0, lane[:1] == rows - 1
    loads[7].wait()
    bend = row_ref[0:1]
    centre = row_ref[1:2]
    shrink = row_ref[2:3]
    keep = row_ref[3:4]

    def flat(ref, start, n):
        v = ref[pl.ds(start, n)]
        up, down = ref[pl.ds(start + 1, n)], ref[pl.ds(start - 1, n)]
        lo = jnp.where(first_lane, 0.0, pltpu.roll(v, 1, axis=1))
        hi = jnp.where(last_lane, 0.0, pltpu.roll(v, rows - 1, axis=1))
        return bend * (up + down) + (lo + hi) + centre * v

    own_chunks = [(OFF + c, 72) for c in range(0, N, 72)]
    ext_chunks = [(EXT, 8)] + own_chunks + [(OFF + N, 8)]
    centre_t2 = jnp.where((tm == 0) | (tm == NT - 1), 5.0, 6.0).astype(F32)

    def second(a, b, c):
        return a + b - 2.0 * c

    def second2(a, b, c, d, e):
        return a + e - 4.0 * (b + d) + centre_t2 * c

    half = lax.broadcasted_iota(jnp.int32, (MW, rows), 1) < MW

    beside = ((OFF - 1, OFF - 2), (OFF + N, OFF + N + 1))
    for c in loads[:6]:
        c.wait()
    W[...] = track[...].astype(F32) * (1.0 - land[...].astype(F32))
    for near, _ in beside:
        for ref in (E.at[2], TV, Y):
            ref[near:near + 1] = jnp.zeros((1, rows), F32)
    for s, n in own_chunks:
        r = pl.ds(s, n)
        TV[r] = B[r] * E[2, r]
        Y[r] = B[r] * flat(E.at[2], s, n)
    for s, n in own_chunks:
        l, r = pl.ds(s - OFF, n), pl.ds(s, n)
        three[l, 0:rows] = W[l] * (E[2, r] - obs[l]) + flat(Y, s, n)
        three[l, rows:2 * rows] = Y[r] + flat(TV, s, n)
        three[l, 2 * rows:3 * rows] = TV[r]
    parts = lax.dot(fwd[...], three[...], precision=lax.Precision.HIGH, preferred_element_type=F32)
    for f in range(3):
        part = parts[:, f * rows:(f + 1) * rows]
        part = jnp.where(half, pltpu.roll(part[:MW], MW, axis=1), part[MW:])
        for q in range(4):
            amp3[q, 16 * f:16 * f + 16] = part[16 * q:16 * q + 16]

    with jax.named_scope("entry barrier"):
        pl.semaphore_wait(barrier, count)
    for dz in (2, -2):
        greet(*on_z(z + dz, x), sem=hello.at[0])

    def remote(src, dst, send, recv, t, l):
        return pltpu.make_async_remote_copy(
            src_ref=src, dst_ref=dst, send_sem=send, recv_sem=recv,
            device_id={"tm": t, "lon": l}, device_id_type=MESH,
        )

    side = 1 - 2 * lax.rem(tm, 2)
    send_days = (-side, 2 * side, side)
    recv_days = (-side, -2 * side, side, 2 * side)

    def plane_copy(p, X, i):
        dt = send_days[i]
        return remote(X.at[2, own], X.at[2 - dt, own], hs.at[p, i], hr.at[p, i], tm + dt, lon)

    def hand_copy(p, X):
        return remote(X.at[2 - side, own], X.at[2 - 2 * side, own], hs.at[p, 3], hr.at[p, 3], tm + side, lon)

    def plane_recv(p, X, i):
        return remote(X.at[2, own], X.at[2 + recv_days[i], own], hs.at[p, i], hr.at[p, i], tm, lon)

    def halo_send(p, X):
        for i in range(3):
            pl.when(inside(tm + send_days[i]))(lambda i=i: plane_copy(p, X, i).start())

    def halo_hand(p, X):
        @pl.when(inside(tm - side))
        def _():
            plane_recv(p, X, 0).wait_recv()
            hand_copy(p, X).start()

    def halo_wait(p, X):
        for i in (1, 2, 3):
            pl.when(inside(tm + recv_days[i]))(lambda i=i: plane_recv(p, X, i).wait_recv())
        pl.when(inside(tm - side))(lambda: hand_copy(p, X).wait_send())

    def halo_done(p, X):
        for i in range(3):
            pl.when(inside(tm + send_days[i]))(lambda i=i: plane_copy(p, X, i).wait_send())

    first_row, last_row = OFF, OFF + N - 1

    def edge_copy(i):
        return remote(ts, tr.at[i], es.at[i], er.at[i], tm + (1, -1)[i], lon)

    def edge_send():
        ts[0:1] = E[2, first_row:first_row + 1]
        ts[1:2] = E[2, last_row:last_row + 1]
        for i, dt in enumerate((1, -1)):
            when_t(dt, lambda i=i: edge_copy(i).start())

    def seam_copy(l):
        return remote(ED.at[lon], ED.at[lon], sems.at[0], sems.at[1], tm, l)

    def seam_near():
        return remote(ED.at[pl.ds(0, 3)], ED.at[pl.ds(0, 3)], sems.at[0], sems.at[1], tm, lon)

    def seam_on(d):
        slot = ED.at[lon_at(2 * d)]
        return remote(slot, slot, sems.at[2], sems.at[3], tm, lon + 1 - 2 * zh)

    def seam_far():
        return remote(ED.at[pl.ds(0, 4)], ED.at[pl.ds(0, 4)], sems.at[2], sems.at[3], tm, lon)

    def seam_fill():
        for i, dt in enumerate((1, -1)):
            when_t(-dt, lambda i=i: edge_copy(i).wait_recv())
        bent = tr[0] + tr[1] - 2.0 * ts[...]
        for at, row, inner, side_row in ((0, first_row, first_row + 1, 0), (4, last_row, last_row - 1, 1)):
            ED[lon, at:at + 1] = E[2, row:row + 1]
            ED[lon, at + 1:at + 2] = E[2, inner:inner + 1]
            ED[lon, at + 2:at + 3] = bent[side_row:side_row + 1]
            ED[lon, at + 3:at + 4] = B[row:row + 1]

    def rim_copy(p, j):
        return remote(ls.at[p, j], lr.at[p, j], rs_.at[p], rr.at[p], tm, lon_at((1, -1)[j]))

    def rim_all(p):
        return remote(lr.at[p], lr.at[p], rs_.at[p], rr.at[p], tm, lon)

    def rim_send(p, X):
        ls[p, 0, 0:1] = X[2, last_row:last_row + 1]
        ls[p, 0, 1:2] = X[2, last_row - 1:last_row]
        ls[p, 1, 0:1] = X[2, first_row:first_row + 1]
        ls[p, 1, 1:2] = X[2, first_row + 1:first_row + 2]
        for j in range(2):
            rim_copy(p, j).start()

    before = lon_at(-1)

    def rim_take(p, X):
        rim_all(p).wait_recv()
        for j, (near, far) in enumerate(beside):
            for i, row in enumerate((near, far)):
                line = lr[p, j, i:i + 1]
                if p == 0:
                    line = line + seam_rows[pl.ds((16, 0)[j] + 8 * i + (before, lon)[j], 1)]
                X[2, row:row + 1] = line

    border_rows = (first_row, first_row + 1, last_row - 1, last_row, first_row - 1, last_row + 1)
    border_days = (2, -2, 1, -1)

    def border_copy(p, i):
        return remote(bs.at[p], br.at[p, i], bsem.at[p, i], brem.at[p, i], tm + border_days[i], lon)

    def border_send(p, X):
        for i, row in enumerate(border_rows):
            bs[p, i:i + 1] = X[2, row:row + 1]
        for i, dt in enumerate(border_days):
            when_t(dt, lambda i=i: border_copy(p, i).start())

    def border_take(p, X):
        for i, dt in enumerate(border_days):

            def take(i=i, dt=dt):
                border_copy(p, i).wait_recv()
                for j, row in enumerate(border_rows[:6 if abs(dt) == 1 else 4]):
                    X[2 - dt, row:row + 1] = br[p, i, j:j + 1]

            when_t(-dt, take)

    def border_done(p):
        for i, dt in enumerate(border_days):
            when_t(dt, lambda i=i: border_copy(p, i).wait_send())

    def first_copy(d):
        q = lax.rem(x + d, 4)
        return remote(amp3.at[q], rs3.at[d], xs.at[0], xr.at[0], tm, q * 2 + zh)

    def first_all():
        return remote(rs3.at[pl.ds(1, 3)], rs3.at[pl.ds(1, 3)], xs.at[0], xr.at[0], tm, lon)

    first_days = (2, -2, 1, -1)

    def first_day_copy(i):
        dt = first_days[i]
        some = pl.ds(16, 32) if abs(dt) == 1 else pl.ds(32, 16)
        return remote(sum3.at[some], day3.at[2 - dt, some], fs.at[i], fr.at[i], tm + dt, lon)

    def first_sum():
        first_all().wait_recv()
        sum3[...] = amp3[x] + rs3[1] + rs3[2] + rs3[3]
        for i, dt in enumerate(first_days):
            when_t(dt, lambda i=i: first_day_copy(i).start())

    def first_cross():
        for i, dt in enumerate(first_days):
            when_t(-dt, lambda i=i: first_day_copy(i).wait_recv())
        one, two = pl.ds(16, 16), pl.ds(32, 16)
        quarter[0, 0] = (
            sum3[0:16]
            + second(day3[1, one], day3[3, one], sum3[one])
            + second2(day3[0, two], day3[1, two], sum3[two], day3[3, two], day3[4, two])
        )
        z_copy(0).start()

    def first_done():
        first_all().wait_send()
        for i, dt in enumerate(first_days):
            when_t(dt, lambda i=i: first_day_copy(i).wait_send())
        z_copy(0).wait_send()

    def z_copy(p):
        return remote(quarter.at[p, 0], z_buf.at[p], zs.at[p], zr.at[p], tm, lon + 1 - 2 * zh)

    with jax.named_scope("first amplitudes"):
        for d in (2, 1, 3):
            first_copy(d).start()
    with jax.named_scope("guess edges"):
        edge_send()
        halo_send(0, E)
    with jax.named_scope("far hello"):
        pl.semaphore_wait(hello.at[0], 2)
        for dz in (4, -4):
            greet(*on_z(z + dz, x), sem=hello.at[1])
    with jax.named_scope("guess seams"):
        seam_fill()
        for d in (2, 1, 3):
            seam_copy(lon_at(2 * d)).start()
    with jax.named_scope("first sum"):
        first_sum()
    with jax.named_scope("guess far seam"):
        pl.semaphore_wait(hello.at[1], 2)
        for d in (2, 1, 3):
            greet(tm, lon_at(2 * d), sem=hello.at[2])
        seam_on(0).start()
    with jax.named_scope("guess hand on"):
        halo_hand(0, E)
    with jax.named_scope("guess far seams"):
        seam_near().wait_recv()
        for d in (2, 1, 3):
            seam_on(d).start()
    with jax.named_scope("first cross"):
        first_cross()

    def flatten(field):
        for s, n in ext_chunks:
            Y[pl.ds(s, n)] = flat(field, s, n)

    def once(emit=None):
        for s, n in ext_chunks:
            full = TV[pl.ds(s, n)] + Y[pl.ds(s, n)]
            Y[pl.ds(s, n)] = B[pl.ds(s, n)] * full
            if emit is not None and OFF <= s < OFF + N:
                emit(s, n, full)

    def twice(emit):
        for s, n in own_chunks:
            emit(s, n, B[pl.ds(s, n)] * (T2V[pl.ds(s, n)] + flat(TV, s, n)) + flat(Y, s, n))

    with jax.named_scope("guess halo wait"):
        halo_wait(0, E)
    for s, n in ext_chunks:
        r = pl.ds(s, n)
        TV[r] = second(E[1, r], E[3, r], E[2, r])
    for near, _ in beside:
        TV[near:near + 1] = jnp.zeros((1, rows), F32)
    for s, n in own_chunks:
        r = pl.ds(s, n)
        T2V[r] = second2(E[0, r], E[1, r], E[2, r], E[3, r], E[4, r])

    def emit_g(s, n, u):
        l = pl.ds(s - OFF, n)
        g = W[l] * (E[2, pl.ds(s, n)] - obs[l]) + u
        G[2, pl.ds(s, n)] = g

    with jax.named_scope("first operator"):
        for near, _ in beside:
            E[2, near:near + 1] = jnp.zeros((1, rows), F32)
        flatten(E.at[2])
        once()
        for near, _ in beside:
            Y[near:near + 1] = jnp.zeros((1, rows), F32)
        twice(emit_g)
    for c in loads[6:7] + loads[8:]:
        c.wait()

    def rs_copy(p, d):
        q = lax.rem(x + d, 4)
        return remote(amp.at[p, pl.ds(16 * q, 16)], rs_buf.at[p, d], xs.at[p], xr.at[p], tm, q * 2 + zh)

    def rs_all(p):
        return remote(rs_buf.at[p, pl.ds(1, 3)], rs_buf.at[p, pl.ds(1, 3)], xs.at[p], xr.at[p], tm, lon)

    days = (2, -2, 1, -1, 0)

    def at_copy(p, i, d):
        dt = days[i]
        xx = lax.rem(x + d, 4)
        return remote(
            quarter.at[p, 1], AT.at[p, 2 - dt, pl.ds(16 * x, 16)], ats.at[p, i], atr.at[p, i], tm + dt, xx * 2 + zh
        )

    def at_all(p, i):
        some = AT.at[p, 2 - days[i], pl.ds(0, MW if days[i] else MW - 16)]
        return remote(some, some, ats.at[p, i], atr.at[p, i], tm, lon)

    half16 = lax.broadcasted_iota(jnp.int32, (16, rows), 1) < MW

    def seam_take():
        seam_far().wait_recv()
        er1, er2, ter, ber = (pltpu.roll(ED[:, i, :], 7, axis=0) for i in range(4))
        el1, el2, tel, bel = (ED[:, i, :] for i in range(4, 8))

        def across(v):
            lo = jnp.where(first_lane, 0.0, pltpu.roll(v, 1, axis=1))
            hi = jnp.where(last_lane, 0.0, pltpu.roll(v, rows - 1, axis=1))
            return lo + hi - 2.0 * v

        yl = bel * (tel + across(el1) + bend * (el2 + er1 - 2.0 * el1))
        yr = ber * (ter + across(er1) + bend * (er2 + el1 - 2.0 * er1))
        dr_, dl_ = ber * bend * el1, bel * bend * er1
        seam_rows[0:8] = bend * (yl + ber * tel - 2.0 * dr_) + across(dr_)
        seam_rows[8:16] = bend * dr_
        seam_rows[16:24] = bend * (yr + bel * ter - 2.0 * dl_) + across(dl_)
        seam_rows[24:32] = bend * dl_
        for row, place in (
            (first_row, before), (first_row + 1, 8 + before), (last_row, 16 + lon), (last_row - 1, 24 + lon)
        ):
            G[2, row:row + 1] += seam_rows[pl.ds(place, 1)]
        B[first_row - 1:first_row] = ED[before, 7:8]
        B[last_row + 1:last_row + 2] = ED[lon_at(1), 3:4]
        part = lax.dot(seams[...], seam_rows[...], precision=lax.Precision.HIGH, preferred_element_type=F32)
        seam_amp[...] = jnp.where(half16, pltpu.roll(part[:16], MW, axis=1), part[16:])

    def transform_start(p):
        part = lax.dot(fwd[...], padded[...], precision=lax.Precision.HIGH, preferred_element_type=F32)
        amp[p] = jnp.where(half, pltpu.roll(part[:MW], MW, axis=1), part[MW:])
        for d in (2, 1, 3):
            rs_copy(p, d).start()

    def transform_cross(p):
        total = amp[p, pl.ds(16 * x, 16)]
        rs_all(p).wait_recv()
        for d in (1, 2, 3):
            total = total + rs_buf[p, d]
        quarter[p, 0] = total
        z_copy(p).start()

    def transform_spread(p):
        z_copy(p).wait_recv()
        total = quarter[p, 0] + z_buf[p]
        if p == 0:
            total = total + seam_amp[...]
        quarter[p, 1] = total
        for i, dt in enumerate(days):
            for d in (2, 1, 3, 0) if dt else (2, 1, 3):
                when_t(dt, lambda i=i, d=d: at_copy(p, i, d).start())
        AT[p, 2, pl.ds(16 * x, 16)] = total

    def transform_finish(p, some):
        for i, dt in enumerate(days):
            if dt in some:
                when_t(-dt, lambda i=i: at_all(p, i).wait_recv())

    def transform_done(p):
        if p == 1:
            rs_all(p).wait_send()
            z_copy(p).wait_send()
        for i, dt in enumerate(days):
            when_t(dt, lambda i=i: at_all(p, i).wait_send())

    def stack(a):
        return jnp.concatenate([pltpu.roll(a, MW, axis=1), a], axis=0) * shrink

    def synthesis(s, n, amplitudes):
        return lax.dot(
            inv[pl.ds(s - EXT, n)], amplitudes, precision=lax.Precision.HIGH, preferred_element_type=F32
        )

    def filter_local(X, field):
        for s, n in ext_chunks:
            r = pl.ds(s, n)
            field[r] = keep * X[2, r]
            TV[r] = keep * second(X[1, r], X[3, r], X[2, r])
            T2V[r] = keep * second2(X[0, r], X[1, r], X[2, r], X[3, r], X[4, r])

    def filter_own(p, field):
        amplitudes = stack(AT[p, 2])
        for s, n in ext_chunks:
            field[pl.ds(s, n)] += synthesis(s, n, amplitudes)
        flatten(field)

    def filter_days(p):
        a = [AT[p, i] for i in range(5)]
        amplitudes = jnp.concatenate([stack(second(a[1], a[3], a[2])), stack(second2(*a))], axis=1)
        for s, n in ext_chunks:
            smooth = synthesis(s, n, amplitudes)
            TV[pl.ds(s, n)] += smooth[:, :rows]
            T2V[pl.ds(s, n)] += smooth[:, rows:]

    sizes = (32, 16)

    def stage_place(stage):
        return (x * 8 + k, z)[stage]

    def stage_device(stage, place):
        if stage == 0:
            return zl * 8 + lax.rem(place, 8), (place // 8) * 2 + zh
        return on_z(place, x)

    def dot_slots(stage):
        return (dots_a, dots_b)[stage]

    def dot_copy(p, stage, d):
        size, mine, slots = sizes[stage], stage_place(stage), dot_slots(stage)
        if stage == 0:
            other = lax.rem(x + d // 8, 4) * 8 + lax.rem(k + d % 8, 8)
        else:
            other = lax.rem(mine + d, size)
        t, l = stage_device(stage, other)
        slot = slots.at[p, mine]
        return remote(slot, slot, ds_.at[p, stage], dr.at[p, stage], t, l)

    def dot_all(p, stage):
        some = dot_slots(stage).at[p, pl.ds(0, sizes[stage] - 1)]
        return remote(some, some, ds_.at[p, stage], dr.at[p, stage], tm, lon)

    steps = (
        [8 * dx + dk for dx in (2, 1, 3, 0) for dk in (4, 3, 5, 2, 6, 1, 7, 0)][:-1],
        [8, 7, 9, 6, 10, 5, 11, 4, 12, 3, 13, 2, 14, 1, 15],
    )

    def dot_send(p, stage, line):
        dot_slots(stage)[p, stage_place(stage)] = line
        for d in steps[stage]:
            dot_copy(p, stage, d).start()

    def dot_take(p, stage):
        dot_all(p, stage).wait_recv()
        total = dot_slots(stage)[p, 0]
        for i in range(1, sizes[stage]):
            total = total + dot_slots(stage)[p, i]
        return total

    def dot_done(p):
        for stage in range(2):
            dot_all(p, stage).wait_send()

    low = lane[:1] < MW

    def pack(slope, curve):
        return jnp.where(low, slope + pltpu.roll(slope, MW, axis=1), curve + pltpu.roll(curve, MW, axis=1))

    def ratio(line):
        slope = jnp.sum(jnp.where(low, line, 0.0), axis=1, keepdims=True)
        return slope / jnp.sum(jnp.where(low, 0.0, line), axis=1, keepdims=True)

    with jax.named_scope("rim one send"):
        pl.semaphore_wait(hello.at[2], 3)
        rim_send(0, G)
    with jax.named_scope("halo one send"):
        halo_send(1, G)
    with jax.named_scope("seams"):
        halo_done(1, G)
        seam_take()
    with jax.named_scope("spread zero"):
        transform_spread(0)
    with jax.named_scope("rim one wait"):
        rim_take(0, G)
    with jax.named_scope("border one send"):
        border_send(0, G)
    with jax.named_scope("hand on one"):
        halo_hand(1, G)
    with jax.named_scope("halo one wait"):
        halo_wait(1, G)
        border_take(0, G)
    with jax.named_scope("filter zero local"):
        filter_local(G, V0)
    with jax.named_scope("finish zero"):
        transform_finish(0, (0,))
    with jax.named_scope("filter zero own"):
        filter_own(0, V0)
    with jax.named_scope("finish zero days"):
        transform_finish(0, (1, -1, 2, -2))
    with jax.named_scope("filter zero days"):
        filter_days(0)
    acc = [jnp.zeros((1, rows), F32), jnp.zeros((1, rows), F32)]

    def emit_first(s, n, full):
        LV0[pl.ds(s - OFF, n)] = full

    def emit_u(s, n, u):
        l, r = pl.ds(s - OFF, n), pl.ds(s, n)
        v = V0[r]
        u = W[l] * v + u
        U[2, r] = u
        padded[l] = u
        acc[0] = acc[0] + jnp.sum(G[2, r] * v, axis=0, keepdims=True)
        acc[1] = acc[1] + jnp.sum(v * u, axis=0, keepdims=True)

    with jax.named_scope("operator one"):
        once(emit_first)
        twice(emit_u)

    with jax.named_scope("transform one"):
        transform_start(1)
    with jax.named_scope("edges two send"):
        dot_send(0, 0, pack(*acc))
    with jax.named_scope("rim two send"):
        rim_send(1, U)
    with jax.named_scope("halo two send"):
        halo_send(2, U)
    with jax.named_scope("cross one"):
        transform_cross(1)
    with jax.named_scope("sums zero"):
        dot_send(0, 1, dot_take(0, 0))
    with jax.named_scope("rim two wait"):
        rim_take(1, U)
    with jax.named_scope("border two send"):
        border_send(1, U)
    with jax.named_scope("hand on two"):
        halo_hand(2, U)
    with jax.named_scope("spread one"):
        transform_spread(1)
    with jax.named_scope("halo two wait"):
        halo_wait(2, U)
        border_take(1, U)
    with jax.named_scope("filter one local"):
        filter_local(U, V)
    with jax.named_scope("finish one"):
        transform_finish(1, (0,))
    with jax.named_scope("filter one own"):
        filter_own(1, V)
    with jax.named_scope("step zero"):
        step0 = ratio(dot_take(0, 1))
    with jax.named_scope("finish one days"):
        transform_finish(1, (1, -1, 2, -2))
    with jax.named_scope("filter one days"):
        filter_days(1)
    acc[0] = acc[1] = jnp.zeros((1, rows), F32)

    def emit_sums(s, n, full):
        l, r = pl.ds(s - OFF, n), pl.ds(s, n)
        search = V0[r] - step0 * V[r]
        gradient = G[2, r] - step0 * U[2, r]
        bent = LV0[l] - step0 * full
        acc[0] = acc[0] + jnp.sum(gradient * search, axis=0, keepdims=True)
        acc[1] = acc[1] + jnp.sum(W[l] * (search * search) + B[r] * (bent * bent), axis=0, keepdims=True)
        out_s[0, l] = search
        out_g[0, l] = gradient

    with jax.named_scope("operator two once"):
        once(emit_sums)
    with jax.named_scope("sums one a"):
        dot_send(1, 0, pack(*acc))

    def emit_last(s, n, u1):
        l, r = pl.ds(s - OFF, n), pl.ds(s, n)
        out_c[0, l] = U[2, r] - step0 * (W[l] * V[r] + u1)
        out_a[0, l] = E[2, r] - step0 * V0[r]

    with jax.named_scope("operator two twice"):
        twice(emit_last)
    with jax.named_scope("sums one b"):
        dot_send(1, 1, dot_take(1, 0))
    halo_done(0, E)
    halo_done(2, U)
    for i, dt in enumerate((1, -1)):
        when_t(dt, lambda i=i: edge_copy(i).wait_send())
    seam_near().wait_send()
    seam_far().wait_send()
    first_done()
    for p in range(2):
        transform_done(p)
        rim_all(p).wait_send()
        border_done(p)
    dot_done(0)
    with jax.named_scope("sums one c"):
        out_step[...] = jnp.broadcast_to(ratio(dot_take(1, 1)), out_step.shape)
    with jax.named_scope("drain"):
        dot_done(1)


def on_device(NT, NL, first, obs, track, land, bw):
    _, N, rows = first.shape
    forward, inverse, row, seams = tables(NL, N, rows)
    plane = pltpu.VMEM((N + 32, rows), F32)
    planes = pltpu.VMEM((5, N + 32, rows), F32)
    flat = pltpu.VMEM((N, rows), F32)
    whole = pltpu.VMEM((N, rows), jnp.int32)
    dma = pltpu.SemaphoreType.DMA
    hbm = pl.BlockSpec(memory_space=pltpu.HBM)
    surface, search, gradient, curved, step = pl.pallas_call(
        functools.partial(kernel, NT, N),
        out_shape=[pltpu.VMEM(first.shape, F32)] * 4 + [pltpu.VMEM((1, rows), F32)],
        in_specs=[hbm] * 9,
        out_specs=[pl.BlockSpec(memory_space=pltpu.VMEM)] * 5,
        scratch_shapes=[
            pltpu.VMEM(row.shape, F32), planes, planes, planes,
            plane, flat, flat, whole, whole,
            pltpu.VMEM(forward.shape[1:], F32), pltpu.VMEM(inverse.shape[1:], F32),
            plane, plane, plane, plane, plane, flat,
            pltpu.VMEM((forward.shape[2], rows), F32),
            pltpu.VMEM(seams.shape[1:], F32), pltpu.VMEM((128, rows), F32),
            pltpu.VMEM((16, rows), F32), pltpu.VMEM((8, 8, rows), F32),
            pltpu.VMEM((forward.shape[2], 3 * rows), F32),
            pltpu.VMEM((4, 48, rows), F32), pltpu.VMEM((4, 48, rows), F32),
            pltpu.VMEM((48, rows), F32), pltpu.VMEM((5, 48, rows), F32),
            pltpu.VMEM((2, MW, rows), F32),
            pltpu.VMEM((2, 4, 16, rows), F32),
            pltpu.VMEM((2, 2, 16, rows), F32),
            pltpu.VMEM((2, 16, rows), F32),
            pltpu.VMEM((2, 5, MW, rows), F32),
            pltpu.VMEM((2, 32, 1, rows), F32),
            pltpu.VMEM((2, 16, 1, rows), F32),
            pltpu.VMEM((2, rows), F32),
            pltpu.VMEM((2, 2, rows), F32),
            pltpu.VMEM((2, 2, 2, rows), F32),
            pltpu.VMEM((2, 2, 2, rows), F32),
            pltpu.VMEM((2, 8, rows), F32),
            pltpu.VMEM((2, 4, 8, rows), F32),
            pltpu.SemaphoreType.REGULAR((3,)), dma((4,)), dma((4,)), dma((4,)), dma((2, 4)), dma((2, 4)), dma((9,)), dma((3, 4)), dma((3, 4)),
            dma((2,)), dma((2,)), dma((2,)), dma((2,)),
            dma((2,)), dma((2,)), dma((2,)), dma((2,)), dma((2, 5)), dma((2, 5)),
            dma((2, 2)), dma((2, 2)),
        ],
        compiler_params=pltpu.CompilerParams(
            collective_id=0, has_side_effects=True, vmem_limit_bytes=56 * 1024 * 1024
        ),
    )(first, obs, track, land, bw, forward, inverse, row, seams)
    return surface - step[None] * search, gradient - step[None] * curved


def solution(mesh):
    in_specs = (
        P("tm", "lon", None),
        P("tm", "lon", None),
        P("tm", "lon", None),
        P("lon", None),
        P("lon", None),
    )
    out_specs = (P("tm", "lon", None), P("tm", "lon", None))
    return jax.shard_map(
        functools.partial(on_device, mesh.shape["tm"], mesh.shape["lon"]),
        mesh=mesh, in_specs=in_specs, out_specs=out_specs, check_vma=False,
    )
```

```python
import functools

import jax
import jax.numpy as jnp
import numpy as np
from jax import lax
from jax.experimental import pallas as pl
from jax.experimental.pallas import tpu as pltpu
from jax.sharding import PartitionSpec as P

CAP = 64
MW = 64
MESH = pl.DeviceIdType.MESH
OFF = 16
EXT = 8
F32 = jnp.float32


def tables(segments, length, rows):
    circle = segments * length
    harmonic = np.arange(MW)
    w = np.where(harmonic == 0, 1.0 / circle, 2.0 / circle)
    padded = -(-length // 128) * 128
    forward = np.zeros((segments, 2 * MW, padded), np.float32)
    inverse = np.zeros((segments, length + 16, 2 * MW), np.float32)
    for s in range(segments):
        a = 2 * np.pi * ((np.arange(length) + s * length)[:, None] * harmonic % circle) / circle
        forward[s, :MW, :length] = np.cos(a).T
        forward[s, MW:, :length] = np.sin(a).T
        a = 2 * np.pi * ((np.arange(length + 16) - 8 + s * length)[:, None] * harmonic % circle) / circle
        inverse[s] = np.concatenate([w * np.cos(a), w * np.sin(a)], axis=1)
    phi = (90.0 - (rows - np.arange(rows) - 0.5) * 0.125) * (np.pi / 180.0)
    bend = 1.0 / (np.cos(phi) + 0.5) ** 2
    shrink = np.zeros(rows)
    shrink[rows - CAP:] = 0.9 * (np.arange(CAP) + 1.0) / CAP
    row = np.zeros((8, rows), np.float32)
    row[0] = bend
    row[1] = -2.0 * (bend + 1.0)
    row[2] = shrink
    row[3] = 1.0 - shrink
    seams = np.zeros((4, 32, 128), np.float32)
    for i, offset in enumerate((0, 1, -1, -2)):
        place = (np.arange(segments) + 1) * length + offset
        a = 2 * np.pi * (place[None, :] * harmonic[:, None] % circle) / circle
        for q in range(4):
            seams[q, :16, 8 * i:8 * i + 8] = np.cos(a[16 * q:16 * q + 16])
            seams[q, 16:, 8 * i:8 * i + 8] = np.sin(a[16 * q:16 * q + 16])
    return forward, inverse, row, seams


def kernel(
    NT, N, first_ref, obs_ref, track_ref, land_ref, bw_ref, fwd_ref, inv_ref, row_hbm, seams_hbm,
    out_a, out_s, out_g, out_c, out_step,
    row_ref, E, G, U, B, W, obs, track, land, fwd, inv, V, TV, T2V, Y, V0, LV0, padded, seams, seam_rows, seam_amp, ED, three, amp3, rs3, sum3, day3, own_buf, own_sum, own_z_buf, amp, quarter,
    z_buf, AT, dots_a, dots_b, ts, tr, ls, lr, bs, br,
    hello, ow, osend, fs, fr, sems, bsem, brem, lsem, hs, hr, es, er, rs_, rr, xs, xr, zs, zr, ats, atr, ds_, dr,
):
    tm = lax.axis_index("tm")
    lon = lax.axis_index("lon")
    x, zh = lon // 2, lon % 2
    zl, k = tm // 8, tm % 8
    rows = 128

    def inside(t):
        return (t >= 0) & (t < NT)

    def when_t(dt, fn):
        if dt == 0:
            fn()
        else:
            pl.when(inside(tm + dt))(fn)

    def lon_at(d):
        return lax.rem(lon + d + 8, 8)

    own = pl.ds(OFF, N)
    loads = [
        pltpu.make_async_copy(first_ref.at[0], E.at[2, own], lsem.at[0]),
        pltpu.make_async_copy(bw_ref, B.at[own], lsem.at[1]),
        pltpu.make_async_copy(obs_ref.at[0], obs, lsem.at[2]),
        pltpu.make_async_copy(track_ref.at[0], track, lsem.at[3]),
        pltpu.make_async_copy(land_ref, land, lsem.at[4]),
        pltpu.make_async_copy(fwd_ref.at[lon], fwd, lsem.at[5]),
        pltpu.make_async_copy(inv_ref.at[lon], inv, lsem.at[6]),
        pltpu.make_async_copy(row_hbm, row_ref, lsem.at[7]),
        pltpu.make_async_copy(seams_hbm.at[x], seams, lsem.at[8]),
    ]
    loads[0].start()
    loads[7].start()

    barrier = pltpu.get_barrier_semaphore()

    def greet(t, l, sem=barrier):
        pl.semaphore_signal(sem, inc=1, device_id={"tm": t, "lon": l}, device_id_type=MESH)

    z = zh * 8 + zl

    def on_z(place, xx):
        place = lax.rem(place + 16, 16)
        return lax.rem(place, 8) * 8 + k, xx * 2 + place // 8

    for dz in (2, -2, 1, -1):
        greet(*on_z(z + dz, x))
    for d in range(1, 8):
        greet(zl * 8 + lax.rem(k + d, 8), lon)
    for d in range(1, 4):
        greet(tm, lon_at(2 * d))
    count = jnp.int32(4 + 7 + 3)
    for dt in (-2, -1, 1, 2):
        when_t(dt, lambda dt=dt: greet(tm + dt, lon))
        count = count + jnp.where(inside(tm + dt), 1, 0)
    for c in loads[1:7] + loads[8:]:
        c.start()

    for dt in (-2, -1, 1, 2):

        @pl.when(jnp.logical_not(inside(tm + dt)))
        def _(dt=dt):
            for X in (E, G, U):
                X[2 + dt] = jnp.zeros(X.shape[1:], F32)
            for p in range(2):
                AT[p, 2 + dt] = jnp.zeros(AT.shape[2:], F32)
            if abs(dt) == 1:
                tr[(dt + 1) // 2] = jnp.zeros(tr.shape[1:], F32)
            day3[2 + dt] = jnp.zeros(day3.shape[1:], F32)

    seam_rows[...] = jnp.zeros(seam_rows.shape, F32)
    bs[...] = jnp.zeros(bs.shape, F32)
    three[pl.ds(N, three.shape[0] - N)] = jnp.zeros((three.shape[0] - N, 3 * rows), F32)
    padded[pl.ds(N, padded.shape[0] - N)] = jnp.zeros((padded.shape[0] - N, rows), F32)

    lane = lax.broadcasted_iota(jnp.int32, (8, rows), 1)
    first_lane, last_lane = lane[:1] == 0, lane[:1] == rows - 1
    loads[7].wait()
    bend = row_ref[0:1]
    centre = row_ref[1:2]
    shrink = row_ref[2:3]
    keep = row_ref[3:4]

    def flat(ref, start, n):
        v = ref[pl.ds(start, n)]
        up, down = ref[pl.ds(start + 1, n)], ref[pl.ds(start - 1, n)]
        lo = jnp.where(first_lane, 0.0, pltpu.roll(v, 1, axis=1))
        hi = jnp.where(last_lane, 0.0, pltpu.roll(v, rows - 1, axis=1))
        return bend * (up + down) + (lo + hi) + centre * v

    own_chunks = [(OFF + c, 72) for c in range(0, N, 72)]
    ext_chunks = [(EXT, 8)] + own_chunks + [(OFF + N, 8)]
    centre_t2 = jnp.where((tm == 0) | (tm == NT - 1), 5.0, 6.0).astype(F32)

    def second(a, b, c):
        return a + b - 2.0 * c

    def second2(a, b, c, d, e):
        return a + e - 4.0 * (b + d) + centre_t2 * c

    half = lax.broadcasted_iota(jnp.int32, (MW, rows), 1) < MW

    beside = ((OFF - 1, OFF - 2), (OFF + N, OFF + N + 1))
    for c in loads[:6]:
        c.wait()
    W[...] = track[...].astype(F32) * (1.0 - land[...].astype(F32))
    for near, _ in beside:
        for ref in (E.at[2], TV, Y):
            ref[near:near + 1] = jnp.zeros((1, rows), F32)
    for s, n in own_chunks:
        r = pl.ds(s, n)
        TV[r] = B[r] * E[2, r]
        Y[r] = B[r] * flat(E.at[2], s, n)
    for s, n in own_chunks:
        l, r = pl.ds(s - OFF, n), pl.ds(s, n)
        three[l, 0:rows] = W[l] * (E[2, r] - obs[l]) + flat(Y, s, n)
        three[l, rows:2 * rows] = Y[r] + flat(TV, s, n)
        three[l, 2 * rows:3 * rows] = TV[r]
    parts = lax.dot(fwd[...], three[...], precision=lax.Precision.HIGH, preferred_element_type=F32)
    for f in range(3):
        part = parts[:, f * rows:(f + 1) * rows]
        part = jnp.where(half, pltpu.roll(part[:MW], MW, axis=1), part[MW:])
        for q in range(4):
            amp3[q, 16 * f:16 * f + 16] = part[16 * q:16 * q + 16]

    with jax.named_scope("entry barrier"):
        pl.semaphore_wait(barrier, count)
    for dz in (2, -2):
        greet(*on_z(z + dz, x), sem=hello.at[0])

    def remote(src, dst, send, recv, t, l):
        return pltpu.make_async_remote_copy(
            src_ref=src, dst_ref=dst, send_sem=send, recv_sem=recv,
            device_id={"tm": t, "lon": l}, device_id_type=MESH,
        )

    side = 1 - 2 * lax.rem(tm, 2)
    send_days = (-side, 2 * side, side)
    recv_days = (-side, -2 * side, side, 2 * side)

    def plane_copy(p, X, i):
        dt = send_days[i]
        return remote(X.at[2, own], X.at[2 - dt, own], hs.at[p, i], hr.at[p, i], tm + dt, lon)

    def hand_copy(p, X):
        return remote(X.at[2 - side, own], X.at[2 - 2 * side, own], hs.at[p, 3], hr.at[p, 3], tm + side, lon)

    def plane_recv(p, X, i):
        return remote(X.at[2, own], X.at[2 + recv_days[i], own], hs.at[p, i], hr.at[p, i], tm, lon)

    def halo_send(p, X):
        for i in range(3):
            pl.when(inside(tm + send_days[i]))(lambda i=i: plane_copy(p, X, i).start())

    def halo_hand(p, X):
        @pl.when(inside(tm - side))
        def _():
            plane_recv(p, X, 0).wait_recv()
            hand_copy(p, X).start()

    def halo_wait(p, X):
        for i in (1, 2, 3):
            pl.when(inside(tm + recv_days[i]))(lambda i=i: plane_recv(p, X, i).wait_recv())
        pl.when(inside(tm - side))(lambda: hand_copy(p, X).wait_send())

    def halo_done(p, X):
        for i in range(3):
            pl.when(inside(tm + send_days[i]))(lambda i=i: plane_copy(p, X, i).wait_send())

    first_row, last_row = OFF, OFF + N - 1

    def edge_copy(i):
        return remote(ts, tr.at[i], es.at[i], er.at[i], tm + (1, -1)[i], lon)

    def edge_send():
        ts[0:1] = E[2, first_row:first_row + 1]
        ts[1:2] = E[2, last_row:last_row + 1]
        for i, dt in enumerate((1, -1)):
            when_t(dt, lambda i=i: edge_copy(i).start())

    def seam_copy(l):
        return remote(ED.at[lon], ED.at[lon], sems.at[0], sems.at[1], tm, l)

    def seam_near():
        return remote(ED.at[pl.ds(0, 3)], ED.at[pl.ds(0, 3)], sems.at[0], sems.at[1], tm, lon)

    def seam_on(d):
        slot = ED.at[lon_at(2 * d)]
        return remote(slot, slot, sems.at[2], sems.at[3], tm, lon + 1 - 2 * zh)

    def seam_far():
        return remote(ED.at[pl.ds(0, 4)], ED.at[pl.ds(0, 4)], sems.at[2], sems.at[3], tm, lon)

    def seam_fill():
        for i, dt in enumerate((1, -1)):
            when_t(-dt, lambda i=i: edge_copy(i).wait_recv())
        bent = tr[0] + tr[1] - 2.0 * ts[...]
        for at, row, inner, side_row in ((0, first_row, first_row + 1, 0), (4, last_row, last_row - 1, 1)):
            ED[lon, at:at + 1] = E[2, row:row + 1]
            ED[lon, at + 1:at + 2] = E[2, inner:inner + 1]
            ED[lon, at + 2:at + 3] = bent[side_row:side_row + 1]
            ED[lon, at + 3:at + 4] = B[row:row + 1]

    def rim_copy(p, j):
        return remote(ls.at[p, j], lr.at[p, j], rs_.at[p], rr.at[p], tm, lon_at((1, -1)[j]))

    def rim_all(p):
        return remote(lr.at[p], lr.at[p], rs_.at[p], rr.at[p], tm, lon)

    def rim_send(p, X):
        ls[p, 0, 0:1] = X[2, last_row:last_row + 1]
        ls[p, 0, 1:2] = X[2, last_row - 1:last_row]
        ls[p, 1, 0:1] = X[2, first_row:first_row + 1]
        ls[p, 1, 1:2] = X[2, first_row + 1:first_row + 2]
        for j in range(2):
            rim_copy(p, j).start()

    before = lon_at(-1)

    def rim_take(p, X):
        rim_all(p).wait_recv()
        for j, (near, far) in enumerate(beside):
            for i, row in enumerate((near, far)):
                line = lr[p, j, i:i + 1]
                if p == 0:
                    line = line + seam_rows[pl.ds((16, 0)[j] + 8 * i + (before, lon)[j], 1)]
                X[2, row:row + 1] = line

    border_rows = (first_row, first_row + 1, last_row - 1, last_row, first_row - 1, last_row + 1)
    border_days = (2, -2, 1, -1)

    def border_copy(p, i):
        return remote(bs.at[p], br.at[p, i], bsem.at[p, i], brem.at[p, i], tm + border_days[i], lon)

    def border_send(p, X):
        for i, row in enumerate(border_rows):
            bs[p, i:i + 1] = X[2, row:row + 1]
        for i, dt in enumerate(border_days):
            when_t(dt, lambda i=i: border_copy(p, i).start())

    def border_take(p, X):
        for i, dt in enumerate(border_days):

            def take(i=i, dt=dt):
                border_copy(p, i).wait_recv()
                for j, row in enumerate(border_rows[:6 if abs(dt) == 1 else 4]):
                    X[2 - dt, row:row + 1] = br[p, i, j:j + 1]

            when_t(-dt, take)

    def border_done(p):
        for i, dt in enumerate(border_days):
            when_t(dt, lambda i=i: border_copy(p, i).wait_send())

    def first_copy(d):
        q = lax.rem(x + d, 4)
        return remote(amp3.at[q], rs3.at[d], xs.at[0], xr.at[0], tm, q * 2 + zh)

    def first_all():
        return remote(rs3.at[pl.ds(1, 3)], rs3.at[pl.ds(1, 3)], xs.at[0], xr.at[0], tm, lon)

    first_days = (2, -2, 1, -1)

    def first_day_copy(i):
        dt = first_days[i]
        some = pl.ds(16, 32) if abs(dt) == 1 else pl.ds(32, 16)
        return remote(sum3.at[some], day3.at[2 - dt, some], fs.at[i], fr.at[i], tm + dt, lon)

    def first_sum():
        first_all().wait_recv()
        sum3[...] = amp3[x] + rs3[1] + rs3[2] + rs3[3]
        for i, dt in enumerate(first_days):
            when_t(dt, lambda i=i: first_day_copy(i).start())

    def first_cross():
        for i, dt in enumerate(first_days):
            when_t(-dt, lambda i=i: first_day_copy(i).wait_recv())
        one, two = pl.ds(16, 16), pl.ds(32, 16)
        quarter[0, 0] = (
            sum3[0:16]
            + second(day3[1, one], day3[3, one], sum3[one])
            + second2(day3[0, two], day3[1, two], sum3[two], day3[3, two], day3[4, two])
        )
        z_copy(0).start()

    def first_done():
        first_all().wait_send()
        for i, dt in enumerate(first_days):
            when_t(dt, lambda i=i: first_day_copy(i).wait_send())
        z_copy(0).wait_send()

    def z_copy(p):
        return remote(quarter.at[p, 0], z_buf.at[p], zs.at[p], zr.at[p], tm, lon + 1 - 2 * zh)

    with jax.named_scope("first amplitudes"):
        for d in (2, 1, 3):
            first_copy(d).start()
    with jax.named_scope("guess edges"):
        edge_send()
        halo_send(0, E)
    with jax.named_scope("far hello"):
        pl.semaphore_wait(hello.at[0], 2)
        for dz in (4, -4):
            greet(*on_z(z + dz, x), sem=hello.at[1])
    with jax.named_scope("guess seams"):
        seam_fill()
        for d in (2, 1, 3):
            seam_copy(lon_at(2 * d)).start()
    with jax.named_scope("first sum"):
        first_sum()
    with jax.named_scope("guess far seam"):
        pl.semaphore_wait(hello.at[1], 2)
        for d in (2, 1, 3):
            greet(tm, lon_at(2 * d), sem=hello.at[2])
        seam_on(0).start()
    with jax.named_scope("guess hand on"):
        halo_hand(0, E)
    with jax.named_scope("guess far seams"):
        seam_near().wait_recv()
        for d in (2, 1, 3):
            seam_on(d).start()
    with jax.named_scope("first cross"):
        first_cross()

    def flatten(field):
        for s, n in ext_chunks:
            Y[pl.ds(s, n)] = flat(field, s, n)

    def once(emit=None):
        for s, n in ext_chunks:
            full = TV[pl.ds(s, n)] + Y[pl.ds(s, n)]
            Y[pl.ds(s, n)] = B[pl.ds(s, n)] * full
            if emit is not None and OFF <= s < OFF + N:
                emit(s, n, full)

    def twice(emit):
        for s, n in own_chunks:
            emit(s, n, B[pl.ds(s, n)] * (T2V[pl.ds(s, n)] + flat(TV, s, n)) + flat(Y, s, n))

    with jax.named_scope("guess halo wait"):
        halo_wait(0, E)
    for s, n in ext_chunks:
        r = pl.ds(s, n)
        TV[r] = second(E[1, r], E[3, r], E[2, r])
    for near, _ in beside:
        TV[near:near + 1] = jnp.zeros((1, rows), F32)
    for s, n in own_chunks:
        r = pl.ds(s, n)
        T2V[r] = second2(E[0, r], E[1, r], E[2, r], E[3, r], E[4, r])

    def emit_g(s, n, u):
        l = pl.ds(s - OFF, n)
        g = W[l] * (E[2, pl.ds(s, n)] - obs[l]) + u
        G[2, pl.ds(s, n)] = g

    with jax.named_scope("first operator"):
        for near, _ in beside:
            E[2, near:near + 1] = jnp.zeros((1, rows), F32)
        flatten(E.at[2])
        once()
        for near, _ in beside:
            Y[near:near + 1] = jnp.zeros((1, rows), F32)
        twice(emit_g)
    for c in loads[6:7] + loads[8:]:
        c.wait()

    days = (2, -2, 1, -1, 0)

    def at_copy(p, i, d):
        dt = days[i]
        xx = lax.rem(x + d, 4)
        return remote(
            quarter.at[p, 1], AT.at[p, 2 - dt, pl.ds(16 * x, 16)], ats.at[p, i], atr.at[p, i], tm + dt, xx * 2 + zh
        )

    def at_all(p, i):
        some = AT.at[p, 2 - days[i], pl.ds(0, MW if days[i] else MW - 16)]
        return remote(some, some, ats.at[p, i], atr.at[p, i], tm, lon)

    half16 = lax.broadcasted_iota(jnp.int32, (16, rows), 1) < MW

    def seam_take():
        seam_far().wait_recv()
        er1, er2, ter, ber = (pltpu.roll(ED[:, i, :], 7, axis=0) for i in range(4))
        el1, el2, tel, bel = (ED[:, i, :] for i in range(4, 8))

        def across(v):
            lo = jnp.where(first_lane, 0.0, pltpu.roll(v, 1, axis=1))
            hi = jnp.where(last_lane, 0.0, pltpu.roll(v, rows - 1, axis=1))
            return lo + hi - 2.0 * v

        yl = bel * (tel + across(el1) + bend * (el2 + er1 - 2.0 * el1))
        yr = ber * (ter + across(er1) + bend * (er2 + el1 - 2.0 * er1))
        dr_, dl_ = ber * bend * el1, bel * bend * er1
        seam_rows[0:8] = bend * (yl + ber * tel - 2.0 * dr_) + across(dr_)
        seam_rows[8:16] = bend * dr_
        seam_rows[16:24] = bend * (yr + bel * ter - 2.0 * dl_) + across(dl_)
        seam_rows[24:32] = bend * dl_
        for row, place in (
            (first_row, before), (first_row + 1, 8 + before), (last_row, 16 + lon), (last_row - 1, 24 + lon)
        ):
            G[2, row:row + 1] += seam_rows[pl.ds(place, 1)]
        B[first_row - 1:first_row] = ED[before, 7:8]
        B[last_row + 1:last_row + 2] = ED[lon_at(1), 3:4]
        part = lax.dot(seams[...], seam_rows[...], precision=lax.Precision.HIGH, preferred_element_type=F32)
        seam_amp[...] = jnp.where(half16, pltpu.roll(part[:16], MW, axis=1), part[16:])

    def transform_start(p):
        part = lax.dot(fwd[...], padded[...], precision=lax.Precision.HIGH, preferred_element_type=F32)
        amp[p] = jnp.where(half, pltpu.roll(part[:MW], MW, axis=1), part[MW:])
        own_start()

    def transform_spread(p):
        z_copy(p).wait_recv()
        total = quarter[p, 0] + z_buf[p]
        if p == 0:
            total = total + seam_amp[...]
        quarter[p, 1] = total
        for i, dt in enumerate(days):
            for d in (2, 1, 3, 0) if dt else (2, 1, 3):
                when_t(dt, lambda i=i, d=d: at_copy(p, i, d).start())
        AT[p, 2, pl.ds(16 * x, 16)] = total

    core = lax.rem(tm, 2)
    odd, even = core == 1, core == 0
    top = tm + 1 - core

    def own_send(d):
        q = lax.rem(x + d, 4)
        return remote(amp.at[1, pl.ds(16 * q, 16)], own_buf.at[core, d], xs.at[1], ow.at[core], top, q * 2 + zh)

    def own_part(day, some):
        return remote(own_buf.at[day, some], own_buf.at[day, some], xs.at[1], ow.at[day], tm, lon)

    def own_z():
        return remote(own_sum.at[0], own_z_buf, zs.at[1], zr.at[1], tm, lon + 1 - 2 * zh)

    def own_start():
        for d in (2, 1, 3):
            own_send(d).start()
        pl.when(even)(lambda: own_send(0).start())

    def own_cross():
        @pl.when(odd)
        def _():
            own_buf[1, 0] = amp[1, pl.ds(16 * x, 16)]
            own_part(0, pl.ds(0, 4)).wait_recv()
            own_part(1, pl.ds(1, 3)).wait_recv()
            for day in range(2):
                own_sum[0, day] = own_buf[day, 0] + own_buf[day, 1] + own_buf[day, 2] + own_buf[day, 3]
            own_z().start()

    def own_copy(day, i, d):
        xx = lax.rem(x + d, 4)
        return remote(
            own_sum.at[1, day], AT.at[1, 2 - days[i], pl.ds(16 * x, 16)], osend.at[day, i], atr.at[1, i],
            tm - 1 + day + days[i], xx * 2 + zh,
        )

    def mine(day, dt):
        return day - 1 + dt == 0

    def own_spread():
        @pl.when(odd)
        def _():
            own_z().wait_recv()
            own_sum[1] = own_sum[0] + own_z_buf[...]
            for i, dt in enumerate(days):
                for day in range(2):

                    @pl.when(inside(tm - 1 + day + dt))
                    def _(i=i, dt=dt, day=day):
                        for d in (2, 1, 3) if mine(day, dt) else (2, 1, 3, 0):
                            own_copy(day, i, d).start()

            for day in range(2):
                AT[1, 1 + day, pl.ds(16 * x, 16)] = own_sum[1, day]

    def own_all(i, count, sem):
        some = AT.at[1, 2 - days[i], pl.ds(0, 16 * count)]
        return remote(some, some, sem, atr.at[1, i], tm, lon)

    def own_finish(some):
        for i, dt in enumerate(days):
            if dt not in some:
                continue
            here = inside(tm - dt)
            if dt in (0, 1):
                pl.when(here & odd)(lambda i=i: own_all(i, 3, osend.at[0, 0]).wait_recv())
                pl.when(here & even)(lambda i=i: own_all(i, 4, osend.at[0, 0]).wait_recv())
            else:
                pl.when(here)(lambda i=i: own_all(i, 4, osend.at[0, 0]).wait_recv())

    def own_done():
        pl.when(even)(lambda: own_part(0, pl.ds(0, 4)).wait_send())

        @pl.when(odd)
        def _():
            own_part(0, pl.ds(0, 3)).wait_send()
            own_z().wait_send()
            for i, dt in enumerate(days):
                for day in range(2):

                    @pl.when(inside(tm - 1 + day + dt))
                    def _(i=i, dt=dt, day=day):
                        own_all(i, 3 if mine(day, dt) else 4, osend.at[day, i]).wait_send()

    def transform_finish(p, some):
        if p == 1:
            own_finish(some)
            return
        for i, dt in enumerate(days):
            if dt in some:
                when_t(-dt, lambda i=i: at_all(p, i).wait_recv())

    def transform_done(p):
        if p == 1:
            own_done()
            return
        for i, dt in enumerate(days):
            when_t(dt, lambda i=i: at_all(p, i).wait_send())

    def stack(a):
        return jnp.concatenate([pltpu.roll(a, MW, axis=1), a], axis=0) * shrink

    def synthesis(s, n, amplitudes):
        return lax.dot(
            inv[pl.ds(s - EXT, n)], amplitudes, precision=lax.Precision.HIGH, preferred_element_type=F32
        )

    def filter_local(X, field):
        for s, n in ext_chunks:
            r = pl.ds(s, n)
            field[r] = keep * X[2, r]
            TV[r] = keep * second(X[1, r], X[3, r], X[2, r])
            T2V[r] = keep * second2(X[0, r], X[1, r], X[2, r], X[3, r], X[4, r])

    def filter_own(p, field):
        amplitudes = stack(AT[p, 2])
        for s, n in ext_chunks:
            field[pl.ds(s, n)] += synthesis(s, n, amplitudes)
        flatten(field)

    def filter_days(p):
        a = [AT[p, i] for i in range(5)]
        amplitudes = jnp.concatenate([stack(second(a[1], a[3], a[2])), stack(second2(*a))], axis=1)
        for s, n in ext_chunks:
            smooth = synthesis(s, n, amplitudes)
            TV[pl.ds(s, n)] += smooth[:, :rows]
            T2V[pl.ds(s, n)] += smooth[:, rows:]

    sizes = (32, 16)

    def stage_place(stage):
        return (x * 8 + k, z)[stage]

    def stage_device(stage, place):
        if stage == 0:
            return zl * 8 + lax.rem(place, 8), (place // 8) * 2 + zh
        return on_z(place, x)

    def dot_slots(stage):
        return (dots_a, dots_b)[stage]

    def dot_copy(p, stage, d):
        size, mine, slots = sizes[stage], stage_place(stage), dot_slots(stage)
        if stage == 0:
            other = lax.rem(x + d // 8, 4) * 8 + lax.rem(k + d % 8, 8)
        else:
            other = lax.rem(mine + d, size)
        t, l = stage_device(stage, other)
        slot = slots.at[p, mine]
        return remote(slot, slot, ds_.at[p, stage], dr.at[p, stage], t, l)

    def dot_all(p, stage):
        some = dot_slots(stage).at[p, pl.ds(0, sizes[stage] - 1)]
        return remote(some, some, ds_.at[p, stage], dr.at[p, stage], tm, lon)

    steps = (
        [8 * dx + dk for dx in (2, 1, 3, 0) for dk in (4, 3, 5, 2, 6, 1, 7, 0)][:-1],
        [8, 7, 9, 6, 10, 5, 11, 4, 12, 3, 13, 2, 14, 1, 15],
    )

    def dot_send(p, stage, line):
        dot_slots(stage)[p, stage_place(stage)] = line
        for d in steps[stage]:
            dot_copy(p, stage, d).start()

    def dot_take(p, stage):
        dot_all(p, stage).wait_recv()
        total = dot_slots(stage)[p, 0]
        for i in range(1, sizes[stage]):
            total = total + dot_slots(stage)[p, i]
        return total

    def dot_done(p):
        for stage in range(2):
            dot_all(p, stage).wait_send()

    low = lane[:1] < MW

    def pack(slope, curve):
        return jnp.where(low, slope + pltpu.roll(slope, MW, axis=1), curve + pltpu.roll(curve, MW, axis=1))

    def ratio(line):
        slope = jnp.sum(jnp.where(low, line, 0.0), axis=1, keepdims=True)
        return slope / jnp.sum(jnp.where(low, 0.0, line), axis=1, keepdims=True)

    with jax.named_scope("rim one send"):
        pl.semaphore_wait(hello.at[2], 3)
        rim_send(0, G)
    with jax.named_scope("halo one send"):
        halo_send(1, G)
    with jax.named_scope("seams"):
        halo_done(1, G)
        seam_take()
    with jax.named_scope("spread zero"):
        transform_spread(0)
    with jax.named_scope("rim one wait"):
        rim_take(0, G)
    with jax.named_scope("border one send"):
        border_send(0, G)
    with jax.named_scope("hand on one"):
        halo_hand(1, G)
    with jax.named_scope("halo one wait"):
        halo_wait(1, G)
        border_take(0, G)
    with jax.named_scope("filter zero local"):
        filter_local(G, V0)
    with jax.named_scope("finish zero"):
        transform_finish(0, (0,))
    with jax.named_scope("filter zero own"):
        filter_own(0, V0)
    with jax.named_scope("finish zero days"):
        transform_finish(0, (1, -1, 2, -2))
    with jax.named_scope("filter zero days"):
        filter_days(0)
    acc = [jnp.zeros((1, rows), F32), jnp.zeros((1, rows), F32)]

    def emit_first(s, n, full):
        LV0[pl.ds(s - OFF, n)] = full

    def emit_u(s, n, u):
        l, r = pl.ds(s - OFF, n), pl.ds(s, n)
        v = V0[r]
        u = W[l] * v + u
        U[2, r] = u
        padded[l] = u
        acc[0] = acc[0] + jnp.sum(G[2, r] * v, axis=0, keepdims=True)
        acc[1] = acc[1] + jnp.sum(v * u, axis=0, keepdims=True)

    with jax.named_scope("operator one"):
        once(emit_first)
        twice(emit_u)

    with jax.named_scope("transform one"):
        transform_start(1)
    with jax.named_scope("edges two send"):
        dot_send(0, 0, pack(*acc))
    with jax.named_scope("rim two send"):
        rim_send(1, U)
    with jax.named_scope("halo two send"):
        halo_send(2, U)
    with jax.named_scope("cross one"):
        own_cross()
    with jax.named_scope("sums zero"):
        dot_send(0, 1, dot_take(0, 0))
    with jax.named_scope("rim two wait"):
        rim_take(1, U)
    with jax.named_scope("border two send"):
        border_send(1, U)
    with jax.named_scope("hand on two"):
        halo_hand(2, U)
    with jax.named_scope("spread one"):
        own_spread()
    with jax.named_scope("halo two wait"):
        halo_wait(2, U)
        border_take(1, U)
    with jax.named_scope("filter one local"):
        filter_local(U, V)
    with jax.named_scope("finish one"):
        transform_finish(1, (0,))
    with jax.named_scope("filter one own"):
        filter_own(1, V)
    with jax.named_scope("step zero"):
        step0 = ratio(dot_take(0, 1))
    with jax.named_scope("finish one days"):
        transform_finish(1, (1, -1, 2, -2))
    with jax.named_scope("filter one days"):
        filter_days(1)
    acc[0] = acc[1] = jnp.zeros((1, rows), F32)

    def emit_sums(s, n, full):
        l, r = pl.ds(s - OFF, n), pl.ds(s, n)
        search = V0[r] - step0 * V[r]
        gradient = G[2, r] - step0 * U[2, r]
        bent = LV0[l] - step0 * full
        acc[0] = acc[0] + jnp.sum(gradient * search, axis=0, keepdims=True)
        acc[1] = acc[1] + jnp.sum(W[l] * (search * search) + B[r] * (bent * bent), axis=0, keepdims=True)
        out_s[0, l] = search
        out_g[0, l] = gradient

    with jax.named_scope("operator two once"):
        once(emit_sums)
    with jax.named_scope("sums one a"):
        dot_send(1, 0, pack(*acc))

    def emit_last(s, n, u1):
        l, r = pl.ds(s - OFF, n), pl.ds(s, n)
        out_c[0, l] = U[2, r] - step0 * (W[l] * V[r] + u1)
        out_a[0, l] = E[2, r] - step0 * V0[r]

    with jax.named_scope("operator two twice"):
        twice(emit_last)
    with jax.named_scope("sums one b"):
        dot_send(1, 1, dot_take(1, 0))
    halo_done(0, E)
    halo_done(2, U)
    for i, dt in enumerate((1, -1)):
        when_t(dt, lambda i=i: edge_copy(i).wait_send())
    seam_near().wait_send()
    seam_far().wait_send()
    first_done()
    for p in range(2):
        transform_done(p)
        rim_all(p).wait_send()
        border_done(p)
    dot_done(0)
    with jax.named_scope("sums one c"):
        out_step[...] = jnp.broadcast_to(ratio(dot_take(1, 1)), out_step.shape)
    with jax.named_scope("drain"):
        dot_done(1)


def on_device(NT, NL, first, obs, track, land, bw):
    _, N, rows = first.shape
    forward, inverse, row, seams = tables(NL, N, rows)
    plane = pltpu.VMEM((N + 32, rows), F32)
    planes = pltpu.VMEM((5, N + 32, rows), F32)
    flat = pltpu.VMEM((N, rows), F32)
    whole = pltpu.VMEM((N, rows), jnp.int32)
    dma = pltpu.SemaphoreType.DMA
    hbm = pl.BlockSpec(memory_space=pltpu.HBM)
    surface, search, gradient, curved, step = pl.pallas_call(
        functools.partial(kernel, NT, N),
        out_shape=[pltpu.VMEM(first.shape, F32)] * 4 + [pltpu.VMEM((1, rows), F32)],
        in_specs=[hbm] * 9,
        out_specs=[pl.BlockSpec(memory_space=pltpu.VMEM)] * 5,
        scratch_shapes=[
            pltpu.VMEM(row.shape, F32), planes, planes, planes,
            plane, flat, flat, whole, whole,
            pltpu.VMEM(forward.shape[1:], F32), pltpu.VMEM(inverse.shape[1:], F32),
            plane, plane, plane, plane, plane, flat,
            pltpu.VMEM((forward.shape[2], rows), F32),
            pltpu.VMEM(seams.shape[1:], F32), pltpu.VMEM((128, rows), F32),
            pltpu.VMEM((16, rows), F32), pltpu.VMEM((8, 8, rows), F32),
            pltpu.VMEM((forward.shape[2], 3 * rows), F32),
            pltpu.VMEM((4, 48, rows), F32), pltpu.VMEM((4, 48, rows), F32),
            pltpu.VMEM((48, rows), F32), pltpu.VMEM((5, 48, rows), F32),
            pltpu.VMEM((2, 4, 16, rows), F32), pltpu.VMEM((2, 2, 16, rows), F32),
            pltpu.VMEM((2, 16, rows), F32),
            pltpu.VMEM((2, MW, rows), F32),
            pltpu.VMEM((2, 2, 16, rows), F32),
            pltpu.VMEM((2, 16, rows), F32),
            pltpu.VMEM((2, 5, MW, rows), F32),
            pltpu.VMEM((2, 32, 1, rows), F32),
            pltpu.VMEM((2, 16, 1, rows), F32),
            pltpu.VMEM((2, rows), F32),
            pltpu.VMEM((2, 2, rows), F32),
            pltpu.VMEM((2, 2, 2, rows), F32),
            pltpu.VMEM((2, 2, 2, rows), F32),
            pltpu.VMEM((2, 8, rows), F32),
            pltpu.VMEM((2, 4, 8, rows), F32),
            pltpu.SemaphoreType.REGULAR((3,)), dma((2,)), dma((2, 5)), dma((4,)), dma((4,)), dma((4,)), dma((2, 4)), dma((2, 4)), dma((9,)), dma((3, 4)), dma((3, 4)),
            dma((2,)), dma((2,)), dma((2,)), dma((2,)),
            dma((2,)), dma((2,)), dma((2,)), dma((2,)), dma((2, 5)), dma((2, 5)),
            dma((2, 2)), dma((2, 2)),
        ],
        compiler_params=pltpu.CompilerParams(
            collective_id=0, has_side_effects=True, vmem_limit_bytes=56 * 1024 * 1024
        ),
    )(first, obs, track, land, bw, forward, inverse, row, seams)
    return surface - step[None] * search, gradient - step[None] * curved


def solution(mesh):
    in_specs = (
        P("tm", "lon", None),
        P("tm", "lon", None),
        P("tm", "lon", None),
        P("lon", None),
        P("lon", None),
    )
    out_specs = (P("tm", "lon", None), P("tm", "lon", None))
    return jax.shard_map(
        functools.partial(on_device, mesh.shape["tm"], mesh.shape["lon"]),
        mesh=mesh, in_specs=in_specs, out_specs=out_specs, check_vma=False,
    )
```

```python
import functools

import jax
import jax.numpy as jnp
import numpy as np
from jax import lax
from jax.experimental import pallas as pl
from jax.experimental.pallas import tpu as pltpu
from jax.sharding import PartitionSpec as P

CAP = 64
MW = 64
MESH = pl.DeviceIdType.MESH
OFF = 16
EXT = 8
F32 = jnp.float32


def tables(segments, length, rows):
    circle = segments * length
    harmonic = np.arange(MW)
    w = np.where(harmonic == 0, 1.0 / circle, 2.0 / circle)
    padded = -(-length // 128) * 128
    forward = np.zeros((segments, 2 * MW, padded), np.float32)
    inverse = np.zeros((segments, length + 16, 2 * MW), np.float32)
    for s in range(segments):
        a = 2 * np.pi * ((np.arange(length) + s * length)[:, None] * harmonic % circle) / circle
        forward[s, :MW, :length] = np.cos(a).T
        forward[s, MW:, :length] = np.sin(a).T
        a = 2 * np.pi * ((np.arange(length + 16) - 8 + s * length)[:, None] * harmonic % circle) / circle
        inverse[s] = np.concatenate([w * np.cos(a), w * np.sin(a)], axis=1)
    phi = (90.0 - (rows - np.arange(rows) - 0.5) * 0.125) * (np.pi / 180.0)
    bend = 1.0 / (np.cos(phi) + 0.5) ** 2
    shrink = np.zeros(rows)
    shrink[rows - CAP:] = 0.9 * (np.arange(CAP) + 1.0) / CAP
    row = np.zeros((8, rows), np.float32)
    row[0] = bend
    row[1] = -2.0 * (bend + 1.0)
    row[2] = shrink
    row[3] = 1.0 - shrink
    seams = np.zeros((4, 32, 128), np.float32)
    for i, offset in enumerate((0, 1, -1, -2)):
        place = (np.arange(segments) + 1) * length + offset
        a = 2 * np.pi * (place[None, :] * harmonic[:, None] % circle) / circle
        for q in range(4):
            seams[q, :16, 8 * i:8 * i + 8] = np.cos(a[16 * q:16 * q + 16])
            seams[q, 16:, 8 * i:8 * i + 8] = np.sin(a[16 * q:16 * q + 16])
    return forward, inverse, row, seams


def kernel(
    NT, N, first_ref, obs_ref, track_ref, land_ref, bw_ref, fwd_ref, inv_ref, row_hbm, seams_hbm,
    out_a, out_s, out_g, out_c, out_step,
    row_ref, E, G, U, B, W, obs, track, land, fwd, inv, V, TV, T2V, Y, V0, LV0, padded, seams, seam_rows, seam_amp, ED, three, amp3, rs3, sum3, day3, own_buf, own_sum, own_z_buf, amp, quarter,
    z_buf, AT, dots_a, dots_b, ts, tr, ls, lr, bs, br,
    hello, ow, osend, fs, fr, sems, bsem, brem, lsem, hs, hr, es, er, rs_, rr, xs, xr, zs, zr, ats, atr, ds_, dr,
):
    tm = lax.axis_index("tm")
    lon = lax.axis_index("lon")
    x, zh = lon // 2, lon % 2
    zl, k = tm // 8, tm % 8
    rows = 128

    def inside(t):
        return (t >= 0) & (t < NT)

    def when_t(dt, fn):
        if dt == 0:
            fn()
        else:
            pl.when(inside(tm + dt))(fn)

    def lon_at(d):
        return lax.rem(lon + d + 8, 8)

    own = pl.ds(OFF, N)
    loads = [
        pltpu.make_async_copy(first_ref.at[0], E.at[2, own], lsem.at[0]),
        pltpu.make_async_copy(bw_ref, B.at[own], lsem.at[1]),
        pltpu.make_async_copy(obs_ref.at[0], obs, lsem.at[2]),
        pltpu.make_async_copy(track_ref.at[0], track, lsem.at[3]),
        pltpu.make_async_copy(land_ref, land, lsem.at[4]),
        pltpu.make_async_copy(fwd_ref.at[lon], fwd, lsem.at[5]),
        pltpu.make_async_copy(inv_ref.at[lon], inv, lsem.at[6]),
        pltpu.make_async_copy(row_hbm, row_ref, lsem.at[7]),
        pltpu.make_async_copy(seams_hbm.at[x], seams, lsem.at[8]),
    ]
    loads[0].start()
    loads[7].start()

    barrier = pltpu.get_barrier_semaphore()

    def greet(t, l, sem=barrier):
        pl.semaphore_signal(sem, inc=1, device_id={"tm": t, "lon": l}, device_id_type=MESH)

    z = zh * 8 + zl

    def on_z(place, xx):
        place = lax.rem(place + 16, 16)
        return lax.rem(place, 8) * 8 + k, xx * 2 + place // 8

    for dz in (2, -2, 1, -1):
        greet(*on_z(z + dz, x))
    for d in range(1, 8):
        greet(zl * 8 + lax.rem(k + d, 8), lon)
    for d in range(1, 4):
        greet(tm, lon_at(2 * d))
    count = jnp.int32(4 + 7 + 3)
    for dt in (-2, -1, 1, 2):
        when_t(dt, lambda dt=dt: greet(tm + dt, lon))
        count = count + jnp.where(inside(tm + dt), 1, 0)
    for c in loads[1:7] + loads[8:]:
        c.start()

    for dt in (-2, -1, 1, 2):

        @pl.when(jnp.logical_not(inside(tm + dt)))
        def _(dt=dt):
            for X in (E, G, U):
                X[2 + dt] = jnp.zeros(X.shape[1:], F32)
            for p in range(2):
                AT[p, 2 + dt] = jnp.zeros(AT.shape[2:], F32)
            if abs(dt) == 1:
                tr[(dt + 1) // 2] = jnp.zeros(tr.shape[1:], F32)
            day3[2 + dt] = jnp.zeros(day3.shape[1:], F32)

    seam_rows[...] = jnp.zeros(seam_rows.shape, F32)
    bs[...] = jnp.zeros(bs.shape, F32)
    three[pl.ds(N, three.shape[0] - N)] = jnp.zeros((three.shape[0] - N, 3 * rows), F32)
    padded[pl.ds(N, padded.shape[0] - N)] = jnp.zeros((padded.shape[0] - N, rows), F32)

    lane = lax.broadcasted_iota(jnp.int32, (8, rows), 1)
    first_lane, last_lane = lane[:1] == 0, lane[:1] == rows - 1
    loads[7].wait()
    bend = row_ref[0:1]
    centre = row_ref[1:2]
    shrink = row_ref[2:3]
    keep = row_ref[3:4]

    def flat(ref, start, n):
        v = ref[pl.ds(start, n)]
        up, down = ref[pl.ds(start + 1, n)], ref[pl.ds(start - 1, n)]
        lo = jnp.where(first_lane, 0.0, pltpu.roll(v, 1, axis=1))
        hi = jnp.where(last_lane, 0.0, pltpu.roll(v, rows - 1, axis=1))
        return bend * (up + down) + (lo + hi) + centre * v

    own_chunks = [(OFF + c, 72) for c in range(0, N, 72)]
    ext_chunks = [(EXT, 8)] + own_chunks + [(OFF + N, 8)]
    centre_t2 = jnp.where((tm == 0) | (tm == NT - 1), 5.0, 6.0).astype(F32)

    def second(a, b, c):
        return a + b - 2.0 * c

    def second2(a, b, c, d, e):
        return a + e - 4.0 * (b + d) + centre_t2 * c

    half = lax.broadcasted_iota(jnp.int32, (MW, rows), 1) < MW

    beside = ((OFF - 1, OFF - 2), (OFF + N, OFF + N + 1))
    for c in loads[:6]:
        c.wait()
    W[...] = track[...].astype(F32) * (1.0 - land[...].astype(F32))
    for near, _ in beside:
        for ref in (E.at[2], TV, Y):
            ref[near:near + 1] = jnp.zeros((1, rows), F32)
    for s, n in own_chunks:
        r = pl.ds(s, n)
        TV[r] = B[r] * E[2, r]
        Y[r] = B[r] * flat(E.at[2], s, n)
    for s, n in own_chunks:
        l, r = pl.ds(s - OFF, n), pl.ds(s, n)
        three[l, 0:rows] = W[l] * (E[2, r] - obs[l]) + flat(Y, s, n)
        three[l, rows:2 * rows] = Y[r] + flat(TV, s, n)
        three[l, 2 * rows:3 * rows] = TV[r]
    parts = lax.dot(fwd[...], three[...], precision=lax.Precision.HIGH, preferred_element_type=F32)
    for f in range(3):
        part = parts[:, f * rows:(f + 1) * rows]
        part = jnp.where(half, pltpu.roll(part[:MW], MW, axis=1), part[MW:])
        for q in range(4):
            amp3[q, 16 * f:16 * f + 16] = part[16 * q:16 * q + 16]

    with jax.named_scope("entry barrier"):
        pl.semaphore_wait(barrier, count)
    for dz in (2, -2):
        greet(*on_z(z + dz, x), sem=hello.at[0])

    def remote(src, dst, send, recv, t, l):
        return pltpu.make_async_remote_copy(
            src_ref=src, dst_ref=dst, send_sem=send, recv_sem=recv,
            device_id={"tm": t, "lon": l}, device_id_type=MESH,
        )

    side = 1 - 2 * lax.rem(tm, 2)
    send_days = (-side, 2 * side, side)
    recv_days = (-side, -2 * side, side, 2 * side)

    def plane_copy(p, X, i):
        dt = send_days[i]
        return remote(X.at[2, own], X.at[2 - dt, own], hs.at[i], hr.at[p, i], tm + dt, lon)

    def hand_copy(p, X):
        return remote(X.at[2 - side, own], X.at[2 - 2 * side, own], hs.at[3], hr.at[p, 3], tm + side, lon)

    def plane_recv(p, X, i):
        return remote(X.at[2, own], X.at[2 + recv_days[i], own], hs.at[i], hr.at[p, i], tm, lon)

    def halo_send(p, X):
        for i in range(3):
            pl.when(inside(tm + send_days[i]))(lambda i=i: plane_copy(p, X, i).start())

    def halo_hand(p, X):
        @pl.when(inside(tm - side))
        def _():
            plane_recv(p, X, 0).wait_recv()
            hand_copy(p, X).start()

    def halo_wait(p, X):
        for i in (1, 2, 3):
            pl.when(inside(tm + recv_days[i]))(lambda i=i: plane_recv(p, X, i).wait_recv())
        pl.when(inside(tm - side))(lambda: hand_copy(p, X).wait_send())

    def halo_done(p, X):
        for i in range(3):
            pl.when(inside(tm + send_days[i]))(lambda i=i: plane_copy(p, X, i).wait_send())

    first_row, last_row = OFF, OFF + N - 1

    def edge_copy(i):
        return remote(ts, tr.at[i], es.at[i], er.at[i], tm + (1, -1)[i], lon)

    def edge_send():
        ts[0:1] = E[2, first_row:first_row + 1]
        ts[1:2] = E[2, last_row:last_row + 1]
        for i, dt in enumerate((1, -1)):
            when_t(dt, lambda i=i: edge_copy(i).start())

    def seam_copy(l):
        return remote(ED.at[lon], ED.at[lon], sems.at[0], sems.at[1], tm, l)

    def seam_near():
        return remote(ED.at[pl.ds(0, 3)], ED.at[pl.ds(0, 3)], sems.at[0], sems.at[1], tm, lon)

    def seam_on(d):
        slot = ED.at[lon_at(2 * d)]
        return remote(slot, slot, sems.at[2], sems.at[3], tm, lon + 1 - 2 * zh)

    def seam_far():
        return remote(ED.at[pl.ds(0, 4)], ED.at[pl.ds(0, 4)], sems.at[2], sems.at[3], tm, lon)

    def seam_fill():
        for i, dt in enumerate((1, -1)):
            when_t(-dt, lambda i=i: edge_copy(i).wait_recv())
        bent = tr[0] + tr[1] - 2.0 * ts[...]
        for at, row, inner, side_row in ((0, first_row, first_row + 1, 0), (4, last_row, last_row - 1, 1)):
            ED[lon, at:at + 1] = E[2, row:row + 1]
            ED[lon, at + 1:at + 2] = E[2, inner:inner + 1]
            ED[lon, at + 2:at + 3] = bent[side_row:side_row + 1]
            ED[lon, at + 3:at + 4] = B[row:row + 1]

    def rim_copy(p, j):
        return remote(ls.at[p, j], lr.at[p, j], rs_.at[p], rr.at[p], tm, lon_at((1, -1)[j]))

    def rim_all(p):
        return remote(lr.at[p], lr.at[p], rs_.at[p], rr.at[p], tm, lon)

    def rim_send(p, X):
        ls[p, 0, 0:1] = X[2, last_row:last_row + 1]
        ls[p, 0, 1:2] = X[2, last_row - 1:last_row]
        ls[p, 1, 0:1] = X[2, first_row:first_row + 1]
        ls[p, 1, 1:2] = X[2, first_row + 1:first_row + 2]
        for j in range(2):
            rim_copy(p, j).start()

    before = lon_at(-1)

    def rim_take(p, X):
        rim_all(p).wait_recv()
        for j, (near, far) in enumerate(beside):
            for i, row in enumerate((near, far)):
                line = lr[p, j, i:i + 1]
                if p == 0:
                    line = line + seam_rows[pl.ds((16, 0)[j] + 8 * i + (before, lon)[j], 1)]
                X[2, row:row + 1] = line

    border_rows = (first_row, first_row + 1, last_row - 1, last_row, first_row - 1, last_row + 1)
    border_days = (2, -2, 1, -1)

    def border_copy(p, i):
        return remote(bs.at[p], br.at[p, i], bsem.at[i], brem.at[p, i], tm + border_days[i], lon)

    def border_send(p, X):
        for i, row in enumerate(border_rows):
            bs[p, i:i + 1] = X[2, row:row + 1]
        for i, dt in enumerate(border_days):
            when_t(dt, lambda i=i: border_copy(p, i).start())

    def border_take(p, X):
        for i, dt in enumerate(border_days):

            def take(i=i, dt=dt):
                border_copy(p, i).wait_recv()
                for j, row in enumerate(border_rows[:6 if abs(dt) == 1 else 4]):
                    X[2 - dt, row:row + 1] = br[p, i, j:j + 1]

            when_t(-dt, take)

    def border_done(p):
        for i, dt in enumerate(border_days):
            when_t(dt, lambda i=i: border_copy(p, i).wait_send())

    def first_copy(d):
        q = lax.rem(x + d, 4)
        return remote(amp3.at[q], rs3.at[d], xs.at[0], xr.at[0], tm, q * 2 + zh)

    def first_all():
        return remote(rs3.at[pl.ds(1, 3)], rs3.at[pl.ds(1, 3)], xs.at[0], xr.at[0], tm, lon)

    first_days = (2, -2, 1, -1)

    def first_day_copy(i):
        dt = first_days[i]
        some = pl.ds(16, 32) if abs(dt) == 1 else pl.ds(32, 16)
        return remote(sum3.at[some], day3.at[2 - dt, some], fs.at[i], fr.at[i], tm + dt, lon)

    def first_sum():
        first_all().wait_recv()
        sum3[...] = amp3[x] + rs3[1] + rs3[2] + rs3[3]
        for i, dt in enumerate(first_days):
            when_t(dt, lambda i=i: first_day_copy(i).start())

    def first_cross():
        for i, dt in enumerate(first_days):
            when_t(-dt, lambda i=i: first_day_copy(i).wait_recv())
        one, two = pl.ds(16, 16), pl.ds(32, 16)
        quarter[0, 0] = (
            sum3[0:16]
            + second(day3[1, one], day3[3, one], sum3[one])
            + second2(day3[0, two], day3[1, two], sum3[two], day3[3, two], day3[4, two])
        )
        z_copy(0).start()

    def first_done():
        first_all().wait_send()
        for i, dt in enumerate(first_days):
            when_t(dt, lambda i=i: first_day_copy(i).wait_send())
        z_copy(0).wait_send()

    def z_copy(p):
        return remote(quarter.at[p, 0], z_buf.at[p], zs.at[p], zr.at[p], tm, lon + 1 - 2 * zh)

    with jax.named_scope("first amplitudes"):
        for d in (2, 1, 3):
            first_copy(d).start()
    with jax.named_scope("guess edges"):
        edge_send()
        halo_send(0, E)
    with jax.named_scope("far hello"):
        pl.semaphore_wait(hello.at[0], 2)
        for dz in (4, -4):
            greet(*on_z(z + dz, x), sem=hello.at[1])
    with jax.named_scope("guess seams"):
        seam_fill()
        for d in (2, 1, 3):
            seam_copy(lon_at(2 * d)).start()
    with jax.named_scope("first sum"):
        first_sum()
    with jax.named_scope("guess far seam"):
        pl.semaphore_wait(hello.at[1], 2)
        for d in (2, 1, 3):
            greet(tm, lon_at(2 * d), sem=hello.at[2])
        seam_on(0).start()
    with jax.named_scope("guess hand on"):
        halo_hand(0, E)
    with jax.named_scope("guess far seams"):
        seam_near().wait_recv()
        for d in (2, 1, 3):
            seam_on(d).start()
    with jax.named_scope("first cross"):
        first_cross()

    def flatten(field):
        for s, n in ext_chunks:
            Y[pl.ds(s, n)] = flat(field, s, n)

    def once(emit=None):
        for s, n in ext_chunks:
            full = TV[pl.ds(s, n)] + Y[pl.ds(s, n)]
            Y[pl.ds(s, n)] = B[pl.ds(s, n)] * full
            if emit is not None and OFF <= s < OFF + N:
                emit(s, n, full)

    def twice(emit):
        for s, n in own_chunks:
            emit(s, n, B[pl.ds(s, n)] * (T2V[pl.ds(s, n)] + flat(TV, s, n)) + flat(Y, s, n))

    with jax.named_scope("guess halo wait"):
        halo_wait(0, E)
    for s, n in ext_chunks:
        r = pl.ds(s, n)
        TV[r] = second(E[1, r], E[3, r], E[2, r])
    for near, _ in beside:
        TV[near:near + 1] = jnp.zeros((1, rows), F32)
    for s, n in own_chunks:
        r = pl.ds(s, n)
        T2V[r] = second2(E[0, r], E[1, r], E[2, r], E[3, r], E[4, r])

    def emit_g(s, n, u):
        l = pl.ds(s - OFF, n)
        g = W[l] * (E[2, pl.ds(s, n)] - obs[l]) + u
        G[2, pl.ds(s, n)] = g

    with jax.named_scope("first operator"):
        for near, _ in beside:
            E[2, near:near + 1] = jnp.zeros((1, rows), F32)
        flatten(E.at[2])
        once()
        for near, _ in beside:
            Y[near:near + 1] = jnp.zeros((1, rows), F32)
        twice(emit_g)
    for c in loads[6:7] + loads[8:]:
        c.wait()

    days = (2, -2, 1, -1, 0)

    def at_copy(p, i, d):
        dt = days[i]
        xx = lax.rem(x + d, 4)
        return remote(
            quarter.at[p, 1], AT.at[p, 2 - dt, pl.ds(16 * x, 16)], ats.at[i], atr.at[p, i], tm + dt, xx * 2 + zh
        )

    def at_all(p, i):
        some = AT.at[p, 2 - days[i], pl.ds(0, MW if days[i] else MW - 16)]
        return remote(some, some, ats.at[i], atr.at[p, i], tm, lon)

    half16 = lax.broadcasted_iota(jnp.int32, (16, rows), 1) < MW

    def seam_take():
        seam_far().wait_recv()
        er1, er2, ter, ber = (pltpu.roll(ED[:, i, :], 7, axis=0) for i in range(4))
        el1, el2, tel, bel = (ED[:, i, :] for i in range(4, 8))

        def across(v):
            lo = jnp.where(first_lane, 0.0, pltpu.roll(v, 1, axis=1))
            hi = jnp.where(last_lane, 0.0, pltpu.roll(v, rows - 1, axis=1))
            return lo + hi - 2.0 * v

        yl = bel * (tel + across(el1) + bend * (el2 + er1 - 2.0 * el1))
        yr = ber * (ter + across(er1) + bend * (er2 + el1 - 2.0 * er1))
        dr_, dl_ = ber * bend * el1, bel * bend * er1
        seam_rows[0:8] = bend * (yl + ber * tel - 2.0 * dr_) + across(dr_)
        seam_rows[8:16] = bend * dr_
        seam_rows[16:24] = bend * (yr + bel * ter - 2.0 * dl_) + across(dl_)
        seam_rows[24:32] = bend * dl_
        for row, place in (
            (first_row, before), (first_row + 1, 8 + before), (last_row, 16 + lon), (last_row - 1, 24 + lon)
        ):
            G[2, row:row + 1] += seam_rows[pl.ds(place, 1)]
        B[first_row - 1:first_row] = ED[before, 7:8]
        B[last_row + 1:last_row + 2] = ED[lon_at(1), 3:4]
        part = lax.dot(seams[...], seam_rows[...], precision=lax.Precision.HIGH, preferred_element_type=F32)
        seam_amp[...] = jnp.where(half16, pltpu.roll(part[:16], MW, axis=1), part[16:])

    def transform_start(p):
        part = lax.dot(fwd[...], padded[...], precision=lax.Precision.HIGH, preferred_element_type=F32)
        amp[p] = jnp.where(half, pltpu.roll(part[:MW], MW, axis=1), part[MW:])
        own_start()

    def transform_spread(p):
        z_copy(p).wait_recv()
        total = quarter[p, 0] + z_buf[p]
        if p == 0:
            total = total + seam_amp[...]
        quarter[p, 1] = total
        for i, dt in enumerate(days):

            def shift(i=i, dt=dt):
                for d in (2, 1, 3, 0) if dt else (2, 1, 3):
                    at_copy(p, i, d).start()

            when_t(dt, shift)
        AT[p, 2, pl.ds(16 * x, 16)] = total

    core = lax.rem(tm, 2)
    odd, even = core == 1, core == 0
    top = tm + 1 - core

    def own_send(d):
        q = lax.rem(x + d, 4)
        return remote(amp.at[1, pl.ds(16 * q, 16)], own_buf.at[core, d], xs.at[1], ow.at[core], top, q * 2 + zh)

    def own_part(day, some):
        return remote(own_buf.at[day, some], own_buf.at[day, some], xs.at[1], ow.at[day], tm, lon)

    def own_z():
        return remote(own_sum.at[0], own_z_buf, zs.at[1], zr.at[1], tm, lon + 1 - 2 * zh)

    def own_start():
        for d in (2, 1, 3):
            own_send(d).start()
        pl.when(even)(lambda: own_send(0).start())

    def own_cross():
        @pl.when(odd)
        def _():
            own_buf[1, 0] = amp[1, pl.ds(16 * x, 16)]
            own_part(0, pl.ds(0, 4)).wait_recv()
            own_part(1, pl.ds(1, 3)).wait_recv()
            for day in range(2):
                own_sum[0, day] = own_buf[day, 0] + own_buf[day, 1] + own_buf[day, 2] + own_buf[day, 3]
            own_z().start()

    def own_copy(day, i, d):
        xx = lax.rem(x + d, 4)
        return remote(
            own_sum.at[1, day], AT.at[1, 2 - days[i], pl.ds(16 * x, 16)], osend.at[day, i], atr.at[1, i],
            tm - 1 + day + days[i], xx * 2 + zh,
        )

    def mine(day, dt):
        return day - 1 + dt == 0

    def own_spread():
        @pl.when(odd)
        def _():
            own_z().wait_recv()
            own_sum[1] = own_sum[0] + own_z_buf[...]
            for i, dt in enumerate(days):
                for day in range(2):

                    @pl.when(inside(tm - 1 + day + dt))
                    def _(i=i, dt=dt, day=day):
                        for d in (2, 1, 3) if mine(day, dt) else (2, 1, 3, 0):
                            own_copy(day, i, d).start()

            for day in range(2):
                AT[1, 1 + day, pl.ds(16 * x, 16)] = own_sum[1, day]

    def own_all(i, count, sem):
        some = AT.at[1, 2 - days[i], pl.ds(0, 16 * count)]
        return remote(some, some, sem, atr.at[1, i], tm, lon)

    def own_finish(some):
        for i, dt in enumerate(days):
            if dt not in some:
                continue
            here = inside(tm - dt)
            if dt in (0, 1):
                pl.when(here & odd)(lambda i=i: own_all(i, 3, osend.at[0, 0]).wait_recv())
                pl.when(here & even)(lambda i=i: own_all(i, 4, osend.at[0, 0]).wait_recv())
            else:
                pl.when(here)(lambda i=i: own_all(i, 4, osend.at[0, 0]).wait_recv())

    def own_done():
        pl.when(even)(lambda: own_part(0, pl.ds(0, 4)).wait_send())

        @pl.when(odd)
        def _():
            own_part(0, pl.ds(0, 3)).wait_send()
            own_z().wait_send()
            for i, dt in enumerate(days):
                for day in range(2):

                    @pl.when(inside(tm - 1 + day + dt))
                    def _(i=i, dt=dt, day=day):
                        own_all(i, 3 if mine(day, dt) else 4, osend.at[day, i]).wait_send()

    def transform_finish(p, some):
        if p == 1:
            own_finish(some)
            return
        for i, dt in enumerate(days):
            if dt in some:
                when_t(-dt, lambda i=i: at_all(p, i).wait_recv())

    def transform_done(p):
        if p == 1:
            own_done()
            return
        for i, dt in enumerate(days):
            when_t(dt, lambda i=i: at_all(p, i).wait_send())

    def stack(a):
        return jnp.concatenate([pltpu.roll(a, MW, axis=1), a], axis=0) * shrink

    def synthesis(s, n, amplitudes):
        return lax.dot(
            inv[pl.ds(s - EXT, n)], amplitudes, precision=lax.Precision.HIGH, preferred_element_type=F32
        )

    def filter_local(X, field):
        for s, n in ext_chunks:
            r = pl.ds(s, n)
            field[r] = keep * X[2, r]
            TV[r] = keep * second(X[1, r], X[3, r], X[2, r])
            T2V[r] = keep * second2(X[0, r], X[1, r], X[2, r], X[3, r], X[4, r])

    def filter_own(p, field):
        amplitudes = stack(AT[p, 2])
        for s, n in ext_chunks:
            field[pl.ds(s, n)] += synthesis(s, n, amplitudes)
        flatten(field)

    def filter_days(p):
        a = [AT[p, i] for i in range(5)]
        amplitudes = jnp.concatenate([stack(second(a[1], a[3], a[2])), stack(second2(*a))], axis=1)
        for s, n in ext_chunks:
            smooth = synthesis(s, n, amplitudes)
            TV[pl.ds(s, n)] += smooth[:, :rows]
            T2V[pl.ds(s, n)] += smooth[:, rows:]

    sizes = (32, 16)

    def stage_place(stage):
        return (x * 8 + k, z)[stage]

    def stage_device(stage, place):
        if stage == 0:
            return zl * 8 + lax.rem(place, 8), (place // 8) * 2 + zh
        return on_z(place, x)

    def dot_slots(stage):
        return (dots_a, dots_b)[stage]

    def dot_copy(p, stage, d):
        size, mine, slots = sizes[stage], stage_place(stage), dot_slots(stage)
        if stage == 0:
            other = lax.rem(x + d // 8, 4) * 8 + lax.rem(k + d % 8, 8)
        else:
            other = lax.rem(mine + d, size)
        t, l = stage_device(stage, other)
        slot = slots.at[p, mine]
        return remote(slot, slot, ds_.at[p, stage], dr.at[p, stage], t, l)

    def dot_all(p, stage):
        some = dot_slots(stage).at[p, pl.ds(0, sizes[stage] - 1)]
        return remote(some, some, ds_.at[p, stage], dr.at[p, stage], tm, lon)

    steps = (
        [8 * dx + dk for dx in (2, 1, 3, 0) for dk in (4, 3, 5, 2, 6, 1, 7, 0)][:-1],
        [8, 7, 9, 6, 10, 5, 11, 4, 12, 3, 13, 2, 14, 1, 15],
    )

    def dot_send(p, stage, line):
        dot_slots(stage)[p, stage_place(stage)] = line
        for d in steps[stage]:
            dot_copy(p, stage, d).start()

    def dot_take(p, stage):
        dot_all(p, stage).wait_recv()
        total = dot_slots(stage)[p, 0]
        for i in range(1, sizes[stage]):
            total = total + dot_slots(stage)[p, i]
        return total

    def dot_done(p):
        for stage in range(2):
            dot_all(p, stage).wait_send()

    low = lane[:1] < MW

    def pack(slope, curve):
        return jnp.where(low, slope + pltpu.roll(slope, MW, axis=1), curve + pltpu.roll(curve, MW, axis=1))

    def ratio(line):
        slope = jnp.sum(jnp.where(low, line, 0.0), axis=1, keepdims=True)
        return slope / jnp.sum(jnp.where(low, 0.0, line), axis=1, keepdims=True)

    with jax.named_scope("rim one send"):
        pl.semaphore_wait(hello.at[2], 3)
        rim_send(0, G)
    with jax.named_scope("halo one send"):
        halo_done(0, E)
        halo_send(1, G)
    with jax.named_scope("seams"):
        halo_done(1, G)
        seam_take()
    with jax.named_scope("spread zero"):
        transform_spread(0)
    with jax.named_scope("rim one wait"):
        rim_take(0, G)
    with jax.named_scope("border one send"):
        border_send(0, G)
    with jax.named_scope("hand on one"):
        halo_hand(1, G)
    with jax.named_scope("halo one wait"):
        halo_wait(1, G)
        border_take(0, G)
    with jax.named_scope("filter zero local"):
        filter_local(G, V0)
    with jax.named_scope("finish zero"):
        transform_finish(0, (0,))
    with jax.named_scope("filter zero own"):
        filter_own(0, V0)
    with jax.named_scope("finish zero days"):
        transform_finish(0, (1, -1, 2, -2))
    with jax.named_scope("filter zero days"):
        filter_days(0)
    acc = [jnp.zeros((1, rows), F32), jnp.zeros((1, rows), F32)]

    def emit_first(s, n, full):
        LV0[pl.ds(s - OFF, n)] = full

    def emit_u(s, n, u):
        l, r = pl.ds(s - OFF, n), pl.ds(s, n)
        v = V0[r]
        u = W[l] * v + u
        U[2, r] = u
        padded[l] = u
        acc[0] = acc[0] + jnp.sum(G[2, r] * v, axis=0, keepdims=True)
        acc[1] = acc[1] + jnp.sum(v * u, axis=0, keepdims=True)

    with jax.named_scope("operator one"):
        once(emit_first)
        twice(emit_u)

    with jax.named_scope("transform one"):
        transform_start(1)
    with jax.named_scope("edges two send"):
        dot_send(0, 0, pack(*acc))
    with jax.named_scope("rim two send"):
        rim_send(1, U)
    with jax.named_scope("halo two send"):
        halo_send(2, U)
    with jax.named_scope("cross one"):
        own_cross()
    with jax.named_scope("sums zero"):
        dot_send(0, 1, dot_take(0, 0))
    with jax.named_scope("rim two wait"):
        rim_take(1, U)
    with jax.named_scope("border two send"):
        border_done(0)
        border_send(1, U)
    with jax.named_scope("hand on two"):
        halo_hand(2, U)
    with jax.named_scope("spread one"):
        own_spread()
    with jax.named_scope("halo two wait"):
        halo_wait(2, U)
        border_take(1, U)
    with jax.named_scope("filter one local"):
        filter_local(U, V)
    with jax.named_scope("finish one"):
        transform_finish(1, (0,))
    with jax.named_scope("filter one own"):
        filter_own(1, V)
    with jax.named_scope("step zero"):
        step0 = ratio(dot_take(0, 1))
    with jax.named_scope("finish one days"):
        transform_finish(1, (1, -1, 2, -2))
    with jax.named_scope("filter one days"):
        filter_days(1)
    acc[0] = acc[1] = jnp.zeros((1, rows), F32)

    def emit_sums(s, n, full):
        l, r = pl.ds(s - OFF, n), pl.ds(s, n)
        search = V0[r] - step0 * V[r]
        gradient = G[2, r] - step0 * U[2, r]
        bent = LV0[l] - step0 * full
        acc[0] = acc[0] + jnp.sum(gradient * search, axis=0, keepdims=True)
        acc[1] = acc[1] + jnp.sum(W[l] * (search * search) + B[r] * (bent * bent), axis=0, keepdims=True)
        out_s[0, l] = search
        out_g[0, l] = gradient

    with jax.named_scope("operator two once"):
        once(emit_sums)
    with jax.named_scope("sums one a"):
        dot_send(1, 0, pack(*acc))

    def emit_last(s, n, u1):
        l, r = pl.ds(s - OFF, n), pl.ds(s, n)
        out_c[0, l] = U[2, r] - step0 * (W[l] * V[r] + u1)
        out_a[0, l] = E[2, r] - step0 * V0[r]

    with jax.named_scope("operator two twice"):
        twice(emit_last)
    with jax.named_scope("sums one b"):
        dot_send(1, 1, dot_take(1, 0))
    halo_done(2, U)
    for i, dt in enumerate((1, -1)):
        when_t(dt, lambda i=i: edge_copy(i).wait_send())
    seam_near().wait_send()
    seam_far().wait_send()
    first_done()
    for p in range(2):
        transform_done(p)
        rim_all(p).wait_send()
    border_done(1)
    dot_done(0)
    with jax.named_scope("sums one c"):
        out_step[...] = jnp.broadcast_to(ratio(dot_take(1, 1)), out_step.shape)
    with jax.named_scope("drain"):
        dot_done(1)


def on_device(NT, NL, first, obs, track, land, bw):
    _, N, rows = first.shape
    forward, inverse, row, seams = tables(NL, N, rows)
    plane = pltpu.VMEM((N + 32, rows), F32)
    planes = pltpu.VMEM((5, N + 32, rows), F32)
    flat = pltpu.VMEM((N, rows), F32)
    whole = pltpu.VMEM((N, rows), jnp.int32)
    dma = pltpu.SemaphoreType.DMA
    hbm = pl.BlockSpec(memory_space=pltpu.HBM)
    surface, search, gradient, curved, step = pl.pallas_call(
        functools.partial(kernel, NT, N),
        out_shape=[pltpu.VMEM(first.shape, F32)] * 4 + [pltpu.VMEM((1, rows), F32)],
        in_specs=[hbm] * 9,
        out_specs=[pl.BlockSpec(memory_space=pltpu.VMEM)] * 5,
        scratch_shapes=[
            pltpu.VMEM(row.shape, F32), planes, planes, planes,
            plane, flat, flat, whole, whole,
            pltpu.VMEM(forward.shape[1:], F32), pltpu.VMEM(inverse.shape[1:], F32),
            plane, plane, plane, plane, plane, flat,
            pltpu.VMEM((forward.shape[2], rows), F32),
            pltpu.VMEM(seams.shape[1:], F32), pltpu.VMEM((128, rows), F32),
            pltpu.VMEM((16, rows), F32), pltpu.VMEM((8, 8, rows), F32),
            pltpu.VMEM((forward.shape[2], 3 * rows), F32),
            pltpu.VMEM((4, 48, rows), F32), pltpu.VMEM((4, 48, rows), F32),
            pltpu.VMEM((48, rows), F32), pltpu.VMEM((5, 48, rows), F32),
            pltpu.VMEM((2, 4, 16, rows), F32), pltpu.VMEM((2, 2, 16, rows), F32),
            pltpu.VMEM((2, 16, rows), F32),
            pltpu.VMEM((2, MW, rows), F32),
            pltpu.VMEM((2, 2, 16, rows), F32),
            pltpu.VMEM((2, 16, rows), F32),
            pltpu.VMEM((2, 5, MW, rows), F32),
            pltpu.VMEM((2, 32, 1, rows), F32),
            pltpu.VMEM((2, 16, 1, rows), F32),
            pltpu.VMEM((2, rows), F32),
            pltpu.VMEM((2, 2, rows), F32),
            pltpu.VMEM((2, 2, 2, rows), F32),
            pltpu.VMEM((2, 2, 2, rows), F32),
            pltpu.VMEM((2, 8, rows), F32),
            pltpu.VMEM((2, 4, 8, rows), F32),
            pltpu.SemaphoreType.REGULAR((3,)), dma((2,)), dma((2, 5)), dma((4,)), dma((4,)), dma((4,)), dma((4,)), dma((2, 4)), dma((9,)), dma((4,)), dma((3, 4)),
            dma((2,)), dma((2,)), dma((2,)), dma((2,)),
            dma((2,)), dma((2,)), dma((2,)), dma((2,)), dma((5,)), dma((2, 5)),
            dma((2, 2)), dma((2, 2)),
        ],
        compiler_params=pltpu.CompilerParams(
            collective_id=0, has_side_effects=True, vmem_limit_bytes=56 * 1024 * 1024
        ),
    )(first, obs, track, land, bw, forward, inverse, row, seams)
    return surface - step[None] * search, gradient - step[None] * curved


def solution(mesh):
    in_specs = (
        P("tm", "lon", None),
        P("tm", "lon", None),
        P("tm", "lon", None),
        P("lon", None),
        P("lon", None),
    )
    out_specs = (P("tm", "lon", None), P("tm", "lon", None))
    return jax.shard_map(
        functools.partial(on_device, mesh.shape["tm"], mesh.shape["lon"]),
        mesh=mesh, in_specs=in_specs, out_specs=out_specs, check_vma=False,
    )
```
